32 devices in a mesh: seq: 4 (over x, core), batch: 8 (over z, y).
Axes of the slice: x: 2, y: 2, z: 4, core: 2. Of those that a mesh axis runs over, the one named last changes fastest.
Arguments:
- hidden_in: bfloat16 [32768, 768], P(('seq', 'batch')), may hold values from -6 to 6
- seq_lengths: int32 [32, 2], P(('seq', 'batch')), may hold values from 0 to 1023, as said below
- head_swap: int32 [12], replicated, may hold values from 0 to 1, as said below
- place: int32 [32768], P(('seq', 'batch')), may hold values from -1 to 28671, as said below
- w_qkv: bfloat16 [768, 2304], replicated, may hold values from -0.21875 to 0.21875
- qv_bias: float32 [1536], replicated, may hold values from -3 to 3
- w_out: bfloat16 [768, 768], replicated, may hold values from -0.875 to 0.875
- out_bias: float32 [768], replicated, may hold values from -2 to 2
- norm1_gain: float32 [768], replicated, may hold values from 0.25 to 1.75
- norm1_bias: float32 [768], replicated, may hold values from -2 to 2
- w_in: bfloat16 [768, 3072], replicated, may hold values from -0.21875 to 0.21875
- in_bias: float32 [3072], replicated, may hold values from -3 to 3
- w_down: bfloat16 [3072, 768], replicated, may hold values from -0.109375 to 0.109375
- down_bias: float32 [768], replicated, may hold values from -2 to 2
- norm2_gain: float32 [768], replicated, may hold values from 0.25 to 1.75
- norm2_bias: float32 [768], replicated, may hold values from -2 to 2
- cotangent: bfloat16 [28672, 768], P(('seq', 'batch')), may hold values from -6 to 6
Outputs:
- mixed: bfloat16 [28672, 768], P(('seq', 'batch'))
- input_grad: bfloat16 [32768, 768], P(('seq', 'batch'))
- grad_w_qkv: float32 [768, 2304], P('seq')
- grad_qv_bias: float32 [1536], P('seq')
- grad_w_out: float32 [768, 768], P('seq')
- grad_out_bias: float32 [768], P('seq')
- grad_norm1_gain: float32 [768], P('seq')
- grad_norm1_bias: float32 [768], P('seq')
- grad_w_in: float32 [768, 3072], P('seq')
- grad_in_bias: float32 [3072], P('seq')
- grad_w_down: float32 [3072, 768], P('seq')
- grad_down_bias: float32 [768], P('seq')
- grad_norm2_gain: float32 [768], P('seq')
- grad_norm2_bias: float32 [768], P('seq')
The draws below stay inside these ranges and needn't reach their ends.
Inputs may be any that keep to these rules, and one draw needn't show every extreme that they name: seq_lengths[g,1] = 0 marks a long group, with seq_lengths[g,0] from 769 to 1023; otherwise both entries lie from 385 to 511. The lengths of all groups sum to 28672. `head_swap`: at least one head has 0 and at least one has 1. place is -1 exactly on padding rows and maps the live rows one to one onto 0 to 28671; rows k * 896 to (k + 1) * 896 - 1 form device k's share, and the live rows of one row group map to at most 32 rows of one share, exactly 32 for some group and share.
All inputs are finite; a program needn't handle non-finite values.
Results may differ from the reference program's by a relative error of at most 0.02.
Values may be sent and summed in bfloat16 or wider, within the bound.
No kernel may reach another device: no remote copies, remote signals or barrier semaphores. Data moves between devices by JAX's collectives and lax.ppermute only.
A program may use at most 192 MiB of HBM per device.

```python
import jax
import jax.numpy as jnp
from jax import lax

D = 768
H = 12
FF = 3072
ROWS = 1024
FROWS = 896
TOKENS = 32768
OUT_ROWS = 28672
DEVICES = 32


def layout_draw(key):
    key_kind, key_short, key_long, key_order, key_turn = jax.random.split(key, 5)
    pair_count = DEVICES // 2
    eighth = ROWS // 8
    half_rows = ROWS // 2
    is_long = jax.random.randint(key_kind, (pair_count,), 0, 2)
    short_len = jax.random.randint(key_short, (pair_count, 2), 3 * eighth + 1, 4 * eighth)
    long_len = jax.random.randint(key_long, (pair_count,), 6 * eighth + 1, 8 * eighth)
    short_len = short_len.at[0].set(4 * eighth - 1)
    long_len = long_len.at[0].set(8 * eighth - 1)
    zero_fill = jnp.zeros_like(long_len)
    long_flag = is_long[:, None] == 1
    first_side = jnp.where(long_flag, jnp.stack([long_len, zero_fill], axis=1), short_len)
    second_side = jnp.where(long_flag, jnp.stack([14 * eighth - long_len, zero_fill], axis=1), 7 * eighth - short_len)
    all_lengths = jnp.concatenate([first_side, second_side], axis=0)
    order_perm = jax.random.permutation(key_order, DEVICES)
    lengths = all_lengths[order_perm]
    positions = jnp.arange(ROWS, dtype=jnp.int32)
    single = lengths[:, 1] == 0
    short_limit = jnp.where(positions[None, :] < half_rows, lengths[:, 0:1], lengths[:, 1:2])
    live = jnp.where(single[:, None], positions[None, :] < lengths[:, 0:1], (positions % half_rows)[None, :] < short_limit)
    live_flat = live.reshape(-1).astype(jnp.int32)
    real_index = jnp.cumsum(live_flat) - 1
    rotation = jax.random.randint(key_turn, (), 0, DEVICES)
    target = (real_index + rotation) % DEVICES * FROWS + real_index // DEVICES
    place = jnp.where(live_flat == 1, target, -1)
    return (lengths.astype(jnp.int32), place.astype(jnp.int32))


def draw_seq_lengths(key, part):
    lengths, place = layout_draw(key)
    return lengths


def draw_place(key, part):
    lengths, place = layout_draw(key)
    return place


def draw_head_swap(key, part):
    key = jax.random.fold_in(key, 11)
    key_count, key_order = jax.random.split(key)
    swap_count = jax.random.randint(key_count, (), 1, H)
    order_perm = jax.random.permutation(key_order, H)
    return (order_perm < swap_count).astype(jnp.int32)


def level_of(rng, shape, cuts, smallest, high):
    def one(axis_at, shards_of):
        draws = jax.random.uniform(jax.random.fold_in(jax.random.fold_in(rng, 6), axis_at), (shards_of,), jnp.float32, smallest / len(cuts), high / len(cuts))
        return jnp.repeat(jnp.exp(draws), shape[axis_at] // shards_of).reshape((-1,) + (1,) * (len(shape) - axis_at - 1))

    factor_of = one(*cuts[0])
    for cut in cuts[1:]:
        factor_of = factor_of * one(*cut)
    return factor_of


def gaussian(own_key, dims, spread, reach, pieces=(), held_as=jnp.bfloat16):
    values = jax.random.normal(own_key, dims, jnp.float32) * spread
    if len(pieces) > 0:
        values = level_of(own_key, dims, pieces, -0.22, 0.18) * values
    return jnp.clip(values, min=-reach, max=reach).astype(held_as)


def setup_inputs(seed: int = 0) -> dict:
    seeds = jax.random.split(jax.random.key(seed), 18)
    return {
        "hidden_in": gaussian(seeds[0], (TOKENS, D), 1.0, 6.0, ((0, 32),)),
        "seq_lengths": draw_seq_lengths(jax.random.fold_in(seeds[17], 71), 0),
        "head_swap": draw_head_swap(jax.random.fold_in(seeds[17], 71), 0),
        "place": draw_place(jax.random.fold_in(seeds[17], 71), 0),
        "w_qkv": gaussian(seeds[4], (D, 3 * D), D ** -0.5, 0.21875),
        "qv_bias": gaussian(seeds[5], (2 * D,), 0.5, 3.0, (), jnp.float32),
        "w_out": gaussian(seeds[6], (D, D), (D // 16) ** -0.5, 0.875),
        "out_bias": gaussian(seeds[7], (D,), 0.3, 2.0, (), jnp.float32),
        "norm1_gain": jnp.clip(1.0 + 0.15 * jax.random.normal(seeds[8], (D,), jnp.float32), 0.25, 1.75),
        "norm1_bias": gaussian(seeds[9], (D,), 0.3, 2.0, (), jnp.float32),
        "w_in": gaussian(seeds[10], (D, FF), D ** -0.5, 0.21875),
        "in_bias": gaussian(seeds[11], (FF,), 0.5, 3.0, (), jnp.float32),
        "w_down": gaussian(seeds[12], (FF, D), FF ** -0.5, 0.109375),
        "down_bias": gaussian(seeds[13], (D,), 0.3, 2.0, (), jnp.float32),
        "norm2_gain": jnp.clip(1.0 + 0.15 * jax.random.normal(seeds[14], (D,), jnp.float32), 0.25, 1.75),
        "norm2_bias": gaussian(seeds[15], (D,), 0.3, 2.0, (), jnp.float32),
        "cotangent": gaussian(seeds[16], (OUT_ROWS, D), 1.0, 6.0, ((0, 32),)),
    }


@jax.custom_vjp
def low(v):
    return lax.optimization_barrier(v.astype(jnp.bfloat16)).astype(jnp.float32)

@jax.custom_vjp
def low_back(v):
    return v

def low_keep(v):
    return (low(v), None)

def low_pass(kept, grad):
    return (grad,)

def back_keep(v):
    return (v, None)

def back_low(kept, grad):
    return (low(grad),)
low.defvjp(low_keep, low_pass)
low_back.defvjp(back_keep, back_low)
EPS = 1e-05
BIG = 1e+30
HIGH = lax.Precision.HIGHEST

def hdot(left_op, right_op):
    return jnp.dot(left_op, right_op, precision=HIGH, preferred_element_type=jnp.float32)

def layer_norm(inputs, gain_vec, bias_vec):
    center = inputs - lax.optimization_barrier(jnp.mean(inputs, axis=-1, keepdims=True))
    variance = lax.optimization_barrier(jnp.mean(center * center, axis=-1, keepdims=True))
    return center * lax.rsqrt(variance + EPS) * gain_vec + bias_vec

def block_masks(lengths, swaps, row_count):
    half_rows = row_count // 2
    quarter_rows = row_count // 4
    is_long = lengths[1] == 0
    positions = jnp.arange(half_rows, dtype=jnp.int32)
    first_ok = positions < lengths[0]
    second_ok = jnp.where(is_long, positions + half_rows < lengths[0], positions < lengths[1])
    key_ok = jnp.stack([first_ok, second_ok])
    swapped = swaps == 1
    cross_pair = jnp.logical_and(is_long, swapped)
    key_pick = jnp.where(cross_pair[:, None, None], key_ok[::-1][None], key_ok[None])
    band_index = positions // quarter_rows
    same_band = band_index[:, None] == band_index[None, :]
    band_ok = jnp.logical_or(is_long, same_band[None] != swapped[:, None, None])
    return (cross_pair, jnp.logical_and(band_ok[:, None], key_pick[:, :, None, :]))

def attend_one(projected, lengths, swaps):
    row_count = projected.shape[0]
    model_width = projected.shape[1] // 3
    head_count = swaps.shape[0]
    head_size = model_width // head_count
    half_rows = row_count // 2
    cross_pair, allowed = block_masks(lengths, swaps, row_count)

    def heads_of(columns):
        return columns.reshape(2, half_rows, head_count, head_size).transpose(2, 0, 1, 3)

    def pick_half(blocked):
        return jnp.where(cross_pair[:, None, None, None], blocked[:, ::-1], blocked)
    queries = heads_of(projected[:, :model_width])
    keys_sel = pick_half(heads_of(projected[:, model_width:2 * model_width]))
    values_sel = pick_half(heads_of(projected[:, 2 * model_width:]))
    raw_scores = jnp.einsum('hbid,hbjd->hbij', queries, keys_sel, precision=HIGH) * head_size ** (-0.5)
    scores = low_back(raw_scores)
    masked = jnp.where(allowed, scores, -BIG)
    top_score = lax.optimization_barrier(jnp.max(masked, axis=-1, keepdims=True))
    exp_scores = jnp.exp(masked - top_score)
    soft = exp_scores / lax.optimization_barrier(jnp.sum(exp_scores, axis=-1, keepdims=True))
    mixed_heads = jnp.einsum('hbij,hbjd->hbid', low(soft), values_sel, precision=HIGH)
    return mixed_heads.transpose(1, 2, 0, 3).reshape(row_count, model_width)

def reference(hidden_in, seq_lengths, head_swap, place, w_qkv, qv_bias, w_out, out_bias, norm1_gain, norm1_bias, w_in, in_bias, w_down, down_bias, norm2_gain, norm2_bias, cotangent):
    group_count = seq_lengths.shape[0]
    row_count = hidden_in.shape[0] // group_count
    model_width = hidden_in.shape[1]
    out_rows = cotangent.shape[0]
    target = jnp.where(place >= 0, place, out_rows).astype(jnp.int32)
    source = jnp.zeros((out_rows,), jnp.int32).at[target].set(jnp.arange(place.shape[0], dtype=jnp.int32), mode='drop')

    def one_group(group_args):
        return attend_one(group_args[0], group_args[1], head_swap)

    def forward(inputs, wq_all, qv_vec, wo_mat, ob_vec, gain_one, shift_one, wi_mat, ib_vec, wd_mat, db_vec, gain_two, shift_two):
        zero_bias = jnp.zeros((model_width,), jnp.float32)
        bias_three = jnp.concatenate([qv_vec[:model_width], zero_bias, qv_vec[model_width:]])
        projected = low(low_back(hdot(inputs, wq_all) + bias_three))
        context = lax.map(jax.checkpoint(one_group), (projected.reshape(group_count, row_count, 3 * model_width), seq_lengths))
        context = low(low_back(context.reshape(group_count * row_count, model_width)))
        attn = low_back(hdot(context, wo_mat) + ob_vec)
        first_out = low(low_back(layer_norm(inputs + attn, gain_one, shift_one)))
        moved = jnp.take(first_out, source, axis=0)
        pre_act = low_back(hdot(moved, wi_mat) + ib_vec)
        hidden = low(jax.nn.gelu(pre_act, approximate=False))
        branch = low_back(hdot(hidden, wd_mat) + db_vec)
        return layer_norm(moved + branch, gain_two, shift_two)
    primals = (hidden_in.astype(jnp.float32), w_qkv.astype(jnp.float32), qv_bias, w_out.astype(jnp.float32), out_bias, norm1_gain, norm1_bias, w_in.astype(jnp.float32), in_bias, w_down.astype(jnp.float32), down_bias, norm2_gain, norm2_bias)
    mixed, pullback = jax.vjp(forward, *primals)
    grads = pullback(cotangent.astype(jnp.float32))
    return (mixed.astype(jnp.bfloat16), grads[0].astype(jnp.bfloat16), grads[1], grads[2], grads[3], grads[4], grads[5], grads[6], grads[7], grads[8], grads[9], grads[10], grads[11], grads[12])
```

```python
import functools

import jax
import jax.numpy as jnp
from jax import lax
from jax.experimental import pallas as pl
from jax.experimental.pallas import tpu as pltpu
from jax.sharding import PartitionSpec as P

EPS = 1e-05
BIG = 1e30
BF = jnp.bfloat16
F32 = jnp.float32
I32 = jnp.int32
MIB = 1 << 20

NN = (((1,), (0,)), ((), ()))
NT = (((1,), (1,)), ((), ()))
TN = (((0,), (0,)), ((), ()))


def mm(left_op, right_op, dims):
    return lax.dot_general(left_op, right_op, dims, preferred_element_type=F32)


def sds(shape, dtype):
    return jax.ShapeDtypeStruct(shape, dtype)


def whole_block(shape):
    zeros = (0,) * len(shape)
    return pl.BlockSpec(shape, lambda *_: zeros)


def smem():
    return pl.BlockSpec(memory_space=pltpu.SMEM)


class Chain:
    def __init__(self):
        self.last = None

    def link(self, outs):
        flat = jax.tree.leaves(outs)
        self.last = min(flat, key=lambda a: a.size * a.dtype.itemsize)


def call(chain, body, name, *, grid, in_specs, out_specs, out_shape, scratch=(), prefetch=0,
         aliases=None, vmem=56):
    count = prefetch + len(in_specs)
    before = [] if chain.last is None else [chain.last]

    def ordered(*refs):
        body(*refs[:count], *refs[count + len(before) :])

    kernel = pl.pallas_call(
        ordered,
        name=name,
        grid_spec=pltpu.PrefetchScalarGridSpec(
            num_scalar_prefetch=prefetch,
            grid=grid,
            in_specs=list(in_specs) + [pl.BlockSpec(memory_space=pl.ANY)] * len(before),
            out_specs=out_specs,
            scratch_shapes=list(scratch),
        ),
        out_shape=out_shape,
        input_output_aliases=aliases or {},
        compiler_params=pltpu.CompilerParams(
            vmem_limit_bytes=vmem * MIB, dimension_semantics=("arbitrary",) * len(grid)
        ),
        cost_estimate=pl.CostEstimate(flops=1, bytes_accessed=1, transcendentals=0),
    )

    def run(*args):
        outs = kernel(*args, *before)
        chain.link(outs)
        return outs

    return run


def slot_of(rel):
    return jnp.where(rel == 0, 3, jnp.where(rel == 3, 0, rel))


def floor_div(values, divisor):
    return jnp.floor((values.astype(F32) + 0.5) * (1.0 / divisor)).astype(I32)


def route_kernel(ffn_rows, capacity, place_ref, slot_ref, target_ref):
    devices = target_ref.shape[0]
    rows = place_ref.shape[1]
    place = place_ref[...]
    live = place >= 0
    dev = jnp.where(live, floor_div(place, ffn_rows), -1)
    local = place - dev * ffn_rows
    hit = lax.broadcasted_iota(I32, (devices, rows), 0) == dev
    onehot = hit.astype(F32)
    upper = (
        lax.broadcasted_iota(I32, (rows, rows), 0) <= lax.broadcasted_iota(I32, (rows, rows), 1)
    ).astype(F32).astype(BF)
    running = mm(onehot.astype(BF), upper, NN)
    rank = (jnp.sum(running * onehot, axis=0, keepdims=True) - 1.0).astype(I32)
    slot_ref[...] = jnp.where(live, dev * capacity + rank, devices * capacity)
    ranked = (lax.broadcasted_iota(I32, (capacity, rows), 0) == rank).astype(F32).astype(BF)
    high = (local >> 5).astype(F32)
    low = (local & 31).astype(F32)
    filled = mm(onehot.astype(BF), ranked, NT)
    high_at = mm((onehot * high).astype(BF), ranked, NT)
    low_at = mm((onehot * low).astype(BF), ranked, NT)
    target = (high_at * 32.0 + low_at).astype(I32)
    target_ref[...] = jnp.where(filled > 0.5, target, ffn_rows)


def expand_targets(target, capacity):
    devices = target.shape[0]
    slots = devices * capacity
    lane = lax.broadcasted_iota(I32, (capacity, slots), 1)
    lane_dev = floor_div(lane, capacity)
    spread = ((lane - lane_dev * capacity) == lax.broadcasted_iota(I32, (capacity, slots), 0)).astype(
        F32
    ).astype(BF)
    high = mm((target >> 5).astype(F32).astype(BF), spread, NN)
    low = mm((target & 31).astype(F32).astype(BF), spread, NN)
    wide = high * 32.0 + low
    own_dev = floor_div(lax.broadcasted_iota(I32, (devices, slots), 1), capacity)
    own = own_dev == lax.broadcasted_iota(I32, (devices, slots), 0)
    return jnp.sum(jnp.where(own, wide, 0.0), axis=0, keepdims=True).astype(I32)


def onehot_rows(row_index, row_count):
    lanes = row_index.shape[1]
    return (lax.broadcasted_iota(I32, (row_count, lanes), 0) == row_index).astype(F32).astype(BF)


def onehot_cols(row_index, col_count):
    rows = row_index.shape[1]
    column = jnp.broadcast_to(row_index.astype(F32), (128, rows)).T[:, :1].astype(I32)
    return (lax.broadcasted_iota(I32, (rows, col_count), 1) == column).astype(F32).astype(BF)


def gather_kernel(capacity, target_ref, cot_ref, out_ref, row_ref):
    row = expand_targets(target_ref[...], capacity)
    row_ref[...] = row
    chosen = onehot_cols(row, cot_ref.shape[0])
    out_ref[...] = mm(chosen, cot_ref[...], NN).astype(BF)


def place_kernel(row_ref, in_ref, out_ref):
    chosen = onehot_rows(row_ref[...], out_ref.shape[0])
    out_ref[...] = mm(chosen, in_ref[...], NN).astype(BF)


def norm_rows(values):
    center = values - jnp.mean(values, axis=-1, keepdims=True)
    inverse = lax.rsqrt(jnp.mean(center * center, axis=-1, keepdims=True) + EPS)
    return center * inverse, inverse


def attend_heads(
    head_base, heads, len_ref, swap_ref, x_ref, wq_ref, wk_ref, wv_ref, bq, bv,
    q_ref, k_ref, v_ref, ctx_ref, soft_ref, linv_ref,
):
    rows = x_ref.shape[0]
    half = rows // 2
    quarter = rows // 4
    cols = q_ref.shape[1]
    x = x_ref[...]
    q_ref[...] = (mm(x, wq_ref[...], NN) + bq).astype(BF)
    k_ref[...] = mm(x, wk_ref[...], NN).astype(BF)
    v_ref[...] = (mm(x, wv_ref[...], NN) + bv).astype(BF)
    head_size = cols // heads
    scale = head_size ** (-0.5)
    len0, len1 = len_ref[0, 0], len_ref[0, 1]
    is_long = len1 == 0
    lane = lax.broadcasted_iota(I32, (1, 128), 1)
    row = lax.broadcasted_iota(I32, (half, 1), 0)
    row_quarter = (row >= quarter).astype(I32)
    per_pair = 128 // head_size
    for pair in range(heads // per_pair):
        cut = slice(pair * 128, pair * 128 + 128)
        for b in range(2):
            q_rows = slice(b * half, (b + 1) * half)
            q_blk = q_ref[q_rows, cut] * jnp.asarray(scale, BF)
            out_blk = linv_blk = None
            for sub in range(per_pair):
                h = pair * per_pair + sub
                swapped = swap_ref[head_base + h] == 1
                cross = jnp.logical_and(is_long, swapped)
                kb = jnp.where(cross, 1 - b, b)
                limit = jnp.where(is_long, len0 - kb * half, jnp.where(kb == 0, len0, len1))
                mine = jnp.logical_and(lane >= sub * head_size, lane < (sub + 1) * head_size)
                spare = ((sub + 1) % per_pair) * head_size
                key_rows = pl.ds(pl.multiple_of(kb * half, half), half)
                k_one = jnp.where(mine, k_ref[key_rows, cut].astype(F32), 0.0)
                q_one = jnp.where(mine, q_blk.astype(F32), 0.0)
                for part in range(2):
                    other = jnp.where(swapped, 1 - part, part)
                    band_ok = jnp.logical_or(is_long, row_quarter == other)
                    bias = jnp.where(jnp.logical_and(band_ok, row < limit), 0.0, -BIG)
                    at = lane == spare + part
                    k_one = jnp.where(at, bias, k_one)
                    q_one = jnp.where(at, jnp.where(row_quarter == part, 1.0, 0.0), q_one)
                scores = mm(q_one.astype(BF), k_one.astype(BF), NT)
                top = jnp.max(scores, axis=1, keepdims=True)
                weights = jnp.exp(scores - top)
                linv = 1.0 / jnp.sum(weights, axis=1, keepdims=True)
                soft = weights.astype(BF)
                soft_ref[h, b] = soft
                mixed = mm(soft, v_ref[key_rows, cut], NN) * linv
                out_blk = mixed if out_blk is None else jnp.where(mine, mixed, out_blk)
                linv_blk = (
                    jnp.broadcast_to(linv, mixed.shape)
                    if linv_blk is None
                    else jnp.where(mine, linv, linv_blk)
                )
            ctx_ref[q_rows, cut] = out_blk.astype(BF)
            linv_ref[q_rows, cut] = linv_blk


def attend_first_kernel(
    heads, ids_ref, len_ref, swap_ref, x_ref, wq_ref, wk_ref, wv_ref, b_ref,
    q_ref, k_ref, v_ref, ctx_ref, soft_ref, linv_ref, xt_ref,
):
    cols = q_ref.shape[1]
    width = x_ref.shape[1]
    bq = b_ref[pl.ds(0, cols)].reshape(1, -1)
    bv = b_ref[pl.ds(width, cols)].reshape(1, -1)
    attend_heads(
        0, heads, len_ref, swap_ref, x_ref, wq_ref, wk_ref, wv_ref, bq, bv,
        q_ref, k_ref, v_ref, ctx_ref, soft_ref, linv_ref,
    )
    write_turned(x_ref[...], ids_ref[0], xt_ref)


def attend_rest_kernel(
    heads, ids_ref, len_ref, swap_ref, x_ref, wq_ref, wk_ref, wv_ref, b_ref, ctx0_ref, wo0_ref,
    wo_ref, ob_ref, gain_ref, shift_ref,
    q_ref, k_ref, v_ref, ctx_ref, soft_ref, linv_ref, first_ref, normed_ref, inv_ref, ctxt_ref,
    acc_ref, ctx_all,
):
    step = pl.program_id(0)
    cols = q_ref.shape[1]
    width = x_ref.shape[1]
    group = step + 1
    bq = b_ref[pl.ds(pl.multiple_of(group * cols, cols), cols)].reshape(1, -1)
    bv = b_ref[pl.ds(pl.multiple_of(width + group * cols, cols), cols)].reshape(1, -1)
    attend_heads(
        group * heads, heads, len_ref, swap_ref, x_ref, wq_ref, wk_ref, wv_ref, bq, bv,
        q_ref, k_ref, v_ref, ctx_ref, soft_ref, linv_ref,
    )
    ctx = ctx_ref[...]
    part_sum = mm(ctx, wo_ref[...], NN)
    ctx_all[:, pl.ds(pl.multiple_of(group * cols, cols), cols)] = ctx

    @pl.when(step == 0)
    def _():
        ctx_all[:, :cols] = ctx0_ref[...]
        acc_ref[...] = part_sum + mm(ctx0_ref[...], wo0_ref[...], NN)

    @pl.when(step > 0)
    def _():
        acc_ref[...] += part_sum

    @pl.when(step == pl.num_programs(0) - 1)
    def _():
        attn = acc_ref[...] + ob_ref[...].reshape(1, -1)
        normed, inverse = norm_rows(x_ref[...].astype(F32) + attn)
        normed_ref[...] = normed
        inv_ref[...] = inverse
        first = normed * gain_ref[...].reshape(1, -1) + shift_ref[...].reshape(1, -1)
        first_ref[...] = first.astype(BF)
        write_turned(ctx_all[...], ids_ref[0], ctxt_ref)


def write_turned(values, seq_id, out_ref):
    turned = values.T
    quarter = turned.shape[0] // 4
    for q in range(4):
        at = slot_of(jnp.bitwise_xor(seq_id, q))
        out_ref[pl.ds(pl.multiple_of(at * quarter, quarter), quarter), :] = turned[
            q * quarter : (q + 1) * quarter
        ]


def ffn_kernel(
    ids_ref, x_ref, wi_ref, bi_ref, wd_ref, bd_ref, gain_ref, shift_ref, slot_ref,
    hid_ref, slope_ref, normed_ref, inv_ref, out_ref, xt_ref, acc_ref,
):
    step = pl.program_id(0)
    steps = pl.num_programs(0)
    x = x_ref[...]
    blk = wi_ref.shape[1]
    pre = mm(x, wi_ref[...], NN) + bi_ref[pl.ds(pl.multiple_of(step * blk, blk), blk)].reshape(1, -1)
    phi = 0.5 * (1.0 + lax.erf(pre * 0.7071067811865476))
    hid = (pre * phi).astype(BF)
    hid_ref[...] = hid
    slope_ref[...] = (phi + pre * jnp.exp(-0.5 * pre * pre) * 0.3989422804014327).astype(BF)
    part_sum = mm(hid, wd_ref[...], NN)

    @pl.when(step == 0)
    def _():
        acc_ref[...] = part_sum
        write_turned(x, ids_ref[0], xt_ref)

    @pl.when(step > 0)
    def _():
        acc_ref[...] += part_sum

    @pl.when(step == steps - 1)
    def _():
        branch = acc_ref[...] + bd_ref[...].reshape(1, -1)
        normed, inverse = norm_rows(x_ref[...].astype(F32) + branch)
        normed_ref[...] = normed
        inv_ref[...] = inverse
        mixed = (normed * gain_ref[...].reshape(1, -1) + shift_ref[...].reshape(1, -1)).astype(BF)
        chosen = onehot_rows(slot_ref[...], out_ref.shape[0])
        out_ref[...] = mm(chosen, mixed, NN).astype(BF)


def norm_back(upstream, normed, inverse, gain):
    scaled = upstream * gain
    inner = (
        scaled
        - jnp.mean(scaled, axis=-1, keepdims=True)
        - normed * jnp.mean(scaled * normed, axis=-1, keepdims=True)
    )
    return inner * inverse


def put_rows(ref, *rows):
    for at, row in enumerate(rows):
        ref[at : at + 1, :] = row


def down_back_kernel(
    ids_ref, slot_ref, in_ref, normed_ref, inv_ref, gain_ref, wd_ref, slope_ref, hid_ref,
    pre_ref, branch_ref, vec_ref, act_ref, bias_ref, gw_ref,
):
    @pl.when(pl.program_id(0) == 0)
    def _():
        chosen = onehot_cols(slot_ref[...], in_ref.shape[0])
        cot = mm(chosen, in_ref[...], NN)
        normed = normed_ref[...]
        g_pre = norm_back(cot, normed, inv_ref[...], gain_ref[...].reshape(1, -1))
        pre_ref[...] = g_pre
        branch = g_pre.astype(BF)
        branch_ref[...] = branch
        put_rows(
            vec_ref,
            jnp.sum(cot * normed, axis=0, keepdims=True),
            jnp.sum(cot, axis=0, keepdims=True),
            jnp.sum(branch.astype(F32), axis=0, keepdims=True),
        )

    branch = branch_ref[...]
    g_act = (mm(branch, wd_ref[...], NT) * slope_ref[...].astype(F32)).astype(BF)
    act_ref[...] = g_act
    bias_ref[...] = jnp.sum(g_act.astype(F32), axis=0, keepdims=True)
    gw_ref[0] = mm(hid_ref[...], branch, TN).astype(BF)


def act_back_kernel(ids_ref, branch_ref, wd_ref, slope_ref, old_act, act_ref, bias_ref):
    g_act = (mm(branch_ref[...], wd_ref[...], NT) * slope_ref[...].astype(F32)).astype(BF)
    act_ref[...] = g_act
    bias_ref[...] = jnp.sum(g_act.astype(F32), axis=0, keepdims=True)


def down_grad_kernel(ids_ref, hid_ref, branch_ref, mate_ref, send_ref, keep_ref):
    own = mm(hid_ref[...], branch_ref[...], TN).astype(BF).astype(F32)
    total = (own + mate_ref[0].astype(F32)).astype(BF)

    @pl.when(pl.program_id(0) == 0)
    def _():
        send_ref[...] = total

    @pl.when(pl.program_id(0) == 1)
    def _():
        keep_ref[...] = total


def in_grad_kernel(xt_ref, act_ref, gw_ref):
    gw_ref[...] = mm(xt_ref[...], act_ref[...], NN).astype(BF)


def in_grad_add_kernel(xt_ref, act_ref, mate_ref, send_ref, keep_ref):
    own = mm(xt_ref[...], act_ref[...], NN).astype(BF).astype(F32)
    total = (own + mate_ref[...].astype(F32)).astype(BF)
    rows = send_ref.shape[0]
    send_ref[...] = total[:rows]
    keep_ref[...] = total[rows:]


def first_back_kernel(
    pre2_ref, act_ref, wi_ref, normed_ref, inv_ref, gain_ref, wo_ref, ctxt_ref, linv0_ref, linv_ref,
    pre1_ref, gctx_ref, vec_ref, gw_far, gw_near, acc_ref,
):
    step = pl.program_id(0)
    part_sum = mm(act_ref[...], wi_ref[...], NT)

    @pl.when(step == 0)
    def _():
        acc_ref[...] = part_sum

    @pl.when(step > 0)
    def _():
        acc_ref[...] += part_sum

    @pl.when(step == pl.num_programs(0) - 1)
    def _():
        g_first = (pre2_ref[...] + acc_ref[...]).astype(BF).astype(F32)
        normed = normed_ref[...]
        g_pre = norm_back(g_first, normed, inv_ref[...], gain_ref[...].reshape(1, -1))
        pre1_ref[...] = g_pre
        g_attn = g_pre.astype(BF)
        put_rows(
            vec_ref,
            jnp.sum(g_first * normed, axis=0, keepdims=True),
            jnp.sum(g_first, axis=0, keepdims=True),
            jnp.sum(g_attn.astype(F32), axis=0, keepdims=True),
        )
        g_ctx = mm(g_attn, wo_ref[...], NT)
        cols = linv0_ref.shape[1]
        gctx_ref[:, :cols] = (g_ctx[:, :cols] * linv0_ref[...]).astype(BF)
        gctx_ref[:, cols:] = (g_ctx[:, cols:] * linv_ref[...]).astype(BF)
        cut = ctxt_ref.shape[0] // 2
        gw_far[...] = mm(ctxt_ref[:cut], g_attn, NN).astype(BF)
        gw_near[...] = mm(ctxt_ref[cut:], g_attn, NN).astype(BF)


def attend_back_kernel(
    head_base, heads, len_ref, swap_ref, q_ref, k_ref, v_ref, soft_ref, gctx_ref, ctx_ref, xt_ref,
    proj_ref, vec_ref, gw_far, gw_near, gq_s, gk_s, gv_s,
):
    step = pl.program_id(0)
    rows = q_ref.shape[0]
    half = rows // 2
    head_size = 128 // heads
    scale = head_size ** (-0.5)
    is_long = len_ref[0, 1] == 0
    lane = lax.broadcasted_iota(I32, (1, 128), 1)
    for sub in range(heads):
        swapped = swap_ref[head_base + step * heads + sub] == 1
        cross = jnp.logical_and(is_long, swapped)
        mine = jnp.logical_and(lane >= sub * head_size, lane < (sub + 1) * head_size)
        for b in range(2):
            q_rows = slice(b * half, (b + 1) * half)
            kb = jnp.where(cross, 1 - b, b)
            key_rows = pl.ds(pl.multiple_of(kb * half, half), half)
            soft = soft_ref[sub, b]
            up = gctx_ref[q_rows, :]
            up_one = jnp.where(mine, up, jnp.zeros_like(up))
            inner = jnp.sum(
                up_one.astype(F32) * ctx_ref[q_rows, :].astype(F32), axis=1, keepdims=True
            )
            g_soft = mm(up_one, v_ref[key_rows, :], NT)
            g_scores = (soft.astype(F32) * (g_soft - inner)).astype(BF)
            g_q = mm(g_scores, k_ref[key_rows, :], NN) * scale
            g_k = mm(g_scores, q_ref[q_rows, :], TN) * scale
            g_v = mm(soft, up, TN)
            if sub == 0:
                gq_s[q_rows, :] = g_q
                gk_s[key_rows, :] = g_k
                gv_s[key_rows, :] = g_v
            else:
                gq_s[q_rows, :] = jnp.where(mine, g_q, gq_s[q_rows, :])
                gk_s[key_rows, :] = jnp.where(mine, g_k, gk_s[key_rows, :])
                gv_s[key_rows, :] = jnp.where(mine, g_v, gv_s[key_rows, :])
    cols = proj_ref.shape[1] // 3
    for at, ref in enumerate((gq_s, gk_s, gv_s)):
        low = ref[...].astype(BF)
        out_cols = pl.ds(pl.multiple_of(at * cols + step * 128, 128), 128)
        proj_ref[:, out_cols] = low
        vec_ref[:, out_cols] = jnp.sum(low.astype(F32), axis=0, keepdims=True)

    @pl.when(step == pl.num_programs(0) - 1)
    def _():
        proj = proj_ref[...]
        cut = xt_ref.shape[0] // 2
        gw_far[...] = mm(xt_ref[:cut], proj, NN).astype(BF)
        gw_near[...] = mm(xt_ref[cut:], proj, NN).astype(BF)


def input_grad_kernel(groups, *refs):
    proj_refs, (wq_ref, wk_ref, wv_ref, pre_ref, out_ref, acc_ref) = refs[:groups], refs[groups:]
    step = pl.program_id(0)
    cols = wq_ref.shape[1]

    @pl.when(step == 0)
    def _():
        acc_ref[...] = pre_ref[...]

    for at, proj_ref in enumerate(proj_refs):

        @pl.when(step == at)
        def _():
            acc_ref[...] += (
                mm(proj_ref[:, :cols], wq_ref[...], NT)
                + mm(proj_ref[:, cols : 2 * cols], wk_ref[...], NT)
                + mm(proj_ref[:, 2 * cols :], wv_ref[...], NT)
            )

    @pl.when(step == groups - 1)
    def _():
        out_ref[...] = acc_ref[...].astype(BF)


def vector_kernel(
    groups, ids_ref, vec2_ref, bias_a, bias_b, vec1_ref, *refs
):
    proj_refs, (far_ref, near_ref) = refs[:groups], refs[groups:]
    seq_id = ids_ref[0]
    far_ref[...] = jnp.zeros_like(far_ref)
    near_ref[...] = jnp.zeros_like(near_ref)
    width = vec1_ref.shape[1]
    cols = width // groups
    wide = jnp.concatenate(
        [ref[:, :cols] for ref in proj_refs] + [ref[:, 2 * cols :] for ref in proj_refs], axis=1
    )
    for q in range(4):
        rel = jnp.bitwise_xor(seq_id, q)
        odd = (rel & 1) == 1
        hid_q = slice(q * (bias_a.shape[1] // 4), (q + 1) * (bias_a.shape[1] // 4))
        rows = [jnp.where(odd, bias_a[:, hid_q], bias_b[:, hid_q])]
        qv = width // 2
        rows.append(wide[:, q * qv : (q + 1) * qv])
        part = slice(q * (width // 4), (q + 1) * (width // 4))
        for ref in (vec2_ref, vec1_ref):
            for at in range(3):
                rows.append(ref[at : at + 1, part])

        def store(out_ref, at):
            base = at * (out_ref.shape[0] // 2)
            for r, row in enumerate(rows):
                out_ref[base + r : base + r + 1, : row.shape[1]] = row.astype(BF)

        for at, want in enumerate((3, 1)):
            pl.when(rel == want)(functools.partial(store, far_ref, at))
        for at, want in enumerate((2, 0)):
            pl.when(rel == want)(functools.partial(store, near_ref, at))


def first_add_kernel(sizes, *refs):
    count = len(sizes)
    owns, mates = refs[:count], refs[count : 2 * count]
    send_ref, keep_ref = refs[2 * count :]
    base = 0
    for own, mate, rows in zip(owns, mates, sizes):
        if mate is None:
            total = own[...]
        else:
            total = (own[...].astype(F32) + mate[...].astype(F32)).astype(BF)
        send_ref[base : base + rows, :] = total[:rows]
        keep_ref[base : base + rows, :] = total[rows:]
        base += rows


def split_cols_kernel(ids_ref, keep_ref, got_ref, mine_ref, other_ref):
    total = (keep_ref[...].astype(F32) + got_ref[...].astype(F32)).astype(BF)
    half = mine_ref.shape[1]
    second = (ids_ref[1] & 1) == 1
    left, right = total[:, :half], total[:, half:]
    mine_ref[...] = jnp.where(second, right, left)
    other_ref[...] = jnp.where(second, left, right)


def split_rows_kernel(ids_ref, keep_ref, got_ref, mine_ref, other_ref):
    half = mine_ref.shape[0]
    bit = (ids_ref[1] >> 1) & 1

    def part(at):
        rows = pl.ds(pl.multiple_of(at * half, half), half)
        return (keep_ref[rows, :].astype(F32) + got_ref[rows, :].astype(F32)).astype(BF)

    mine_ref[...] = part(bit)
    other_ref[...] = part(1 - bit)


def add_kernel(left_ref, right_ref, out_ref):
    out_ref[...] = (left_ref[...].astype(F32) + right_ref[...].astype(F32)).astype(BF)


def join_kernel(ids_ref, own_ref, near_ref, far_own_ref, far_near_ref, out_ref):
    half_rows, half_cols = own_ref.shape
    second = (ids_ref[1] & 1) == 1
    bit = (ids_ref[1] >> 1) & 1
    for rel, (mine, other) in enumerate(((own_ref, far_own_ref), (near_ref, far_near_ref))):
        at = jnp.bitwise_xor(bit, rel)
        rows = pl.ds(pl.multiple_of(at * half_rows, half_rows), half_rows)
        a, b = mine[...].astype(F32), other[...].astype(F32)
        out_ref[rows, :half_cols] = jnp.where(second, b, a)
        out_ref[rows, half_cols:] = jnp.where(second, a, b)


def join_into(ids_ref, refs, out_ref):
    own_ref, near_ref, far_own_ref, far_near_ref = refs
    half_rows, half_cols = own_ref.shape
    second = (ids_ref[1] & 1) == 1
    bit = (ids_ref[1] >> 1) & 1
    for rel, (mine, other) in enumerate(((own_ref, far_own_ref), (near_ref, far_near_ref))):
        at = jnp.bitwise_xor(bit, rel)
        rows = pl.ds(pl.multiple_of(at * half_rows, half_rows), half_rows)
        a, b = mine[...].astype(F32), other[...].astype(F32)
        out_ref[rows, :half_cols] = jnp.where(second, b, a)
        out_ref[rows, half_cols:] = jnp.where(second, a, b)


def join_kernel(ids_ref, own_ref, near_ref, far_own_ref, far_near_ref, out_ref):
    join_into(ids_ref, (own_ref, near_ref, far_own_ref, far_near_ref), out_ref)


def attend_join_kernel(groups, ids_ref, *refs):
    a_refs, b_refs = refs[:4], refs[4:8]
    gwq_ref, gwo_ref, qv_ref, hid_ref = refs[8:12]
    vec_refs, (a_all, b_all) = refs[12:18], refs[18:]
    join_into(ids_ref, a_refs, a_all)
    join_into(ids_ref, b_refs, b_all)
    part, width = gwo_ref.shape
    cols = width // groups
    gwo_ref[...] = a_all[:part, :]
    places = [(a_all, part)] + [(b_all, part * at) for at in range(groups - 1)]
    for g, (ref, base) in enumerate(places):
        for at in range(3):
            gwq_ref[:, at * width + g * cols : at * width + (g + 1) * cols] = ref[
                base : base + part, at * cols : (at + 1) * cols
            ]
    base = part * (groups - 1)
    hid_ref[...] = b_all[base, :]
    qv_ref[...] = b_all[base + 1, : qv_ref.shape[0]]
    for at, ref in enumerate(vec_refs):
        ref[...] = b_all[base + 2 + at, : ref.shape[0]]


def exchange(values, axis, mask):
    count = lax.axis_size(axis)
    return lax.ppermute(values, axis, [(i, i ^ mask) for i in range(count)])


def simple(chain, body, name, args, out_shape, prefetch=0, vmem=56, scratch=()):
    tensors = args[prefetch:]
    return call(
        chain,
        body,
        name,
        grid=(1,),
        in_specs=[whole_block(a.shape) for a in tensors],
        out_specs=[whole_block(o.shape) for o in out_shape],
        out_shape=out_shape,
        prefetch=prefetch,
        vmem=vmem,
        scratch=scratch,
    )(*args)


class Share:
    def __init__(self, chain, ids, name, send, keep):
        self.chain, self.ids, self.name = chain, ids, name
        self.keep, self.got = keep, exchange(send, "seq", 2)
        self.shape = keep.shape

    def halve(self, kernel, shape, label, mask):
        self.keep, other = simple(
            self.chain, kernel, self.name + label, (self.ids, self.keep, self.got),
            [sds(shape, BF)] * 2, 1,
        )
        self.got = exchange(other, "batch", mask)

    def step_y(self):
        rows, cols = self.shape
        self.halve(split_cols_kernel, (rows, cols // 2), "_y", 1)

    def step_z(self):
        rows, cols = self.shape
        self.halve(split_rows_kernel, (rows // 2, cols // 2), "_z", 2)

    def add(self, label):
        (self.keep,) = simple(
            self.chain, add_kernel, self.name + label, (self.keep, self.got),
            [sds(self.keep.shape, BF)],
        )

    def step_far(self):
        mask = 4
        while mask <= lax.axis_size("batch") // 2:
            self.add("_a")
            self.got = exchange(self.keep, "batch", mask)
            mask *= 2

    def step_back(self):
        self.add("_f")
        near = exchange(self.keep, "batch", 2)
        far_own = exchange(self.keep, "batch", 1)
        self.pieces = (self.keep, near, far_own, exchange(near, "batch", 1))

    def join(self):
        (whole,) = simple(
            self.chain, join_kernel, self.name + "_j", (self.ids, *self.pieces),
            [sds(self.shape, F32)], 1,
        )
        return whole


def body(
    hidden_in, seq_lengths, head_swap, place, w_qkv, qv_bias, w_out, out_bias, norm1_gain,
    norm1_bias, w_in, in_bias, w_down, down_bias, norm2_gain, norm2_bias, cotangent,
):
    rows, width = hidden_in.shape
    ff = w_in.shape[1]
    ffn_rows = cotangent.shape[0]
    devices = lax.axis_size(("seq", "batch"))
    capacity = (rows + devices - 1) // devices
    slots = devices * capacity
    head_count = head_swap.shape[0]
    head_size = width // head_count
    half = rows // 2
    cols = 256
    groups = width // cols
    heads = cols // head_size
    pair = 128 // head_size
    ids = jnp.stack([lax.axis_index("seq"), lax.axis_index("batch")]).astype(I32)
    chain = Chain()

    slot_row, out_target = simple(
        chain,
        functools.partial(route_kernel, ffn_rows, capacity),
        "route",
        (place.reshape(1, -1),),
        [sds((1, rows), I32), sds((devices, capacity), I32)],
    )
    in_target = lax.all_to_all(out_target, ("seq", "batch"), split_axis=0, concat_axis=0, tiled=True)

    low, wide = sds((rows, width), BF), sds((rows, width), F32)
    vec_spec = whole_block((width,))
    some = lambda count, dtype: sds((rows, count * cols), dtype)
    col = lambda base: pl.BlockSpec((width, cols), lambda g, *_: (0, base + g))
    out_col = pl.BlockSpec((rows, cols), lambda g, *_: (0, g))
    soft_spec = pl.BlockSpec((heads, 2, half, half), lambda g, *_: (g, 0, 0, 0))
    head_outs = [out_col] * 4 + [soft_spec, out_col]
    head_shapes = lambda count: [some(count, BF)] * 4 + [
        sds((count * heads, 2, half, half), BF), some(count, F32)
    ]
    head_args = (ids, seq_lengths, head_swap, hidden_in, w_qkv, w_qkv, w_qkv, qv_bias)
    head_specs = lambda first: [
        smem(), smem(), whole_block((rows, width)), col(first), col(groups + first),
        col(2 * groups + first), whole_block((2 * width,)),
    ]
    *first_heads, x_turned = call(
        chain,
        functools.partial(attend_first_kernel, heads),
        "attend_first",
        grid=(1,),
        in_specs=head_specs(0),
        out_specs=head_outs + [whole_block((width, rows))],
        out_shape=head_shapes(1) + [sds((width, rows), BF)],
        prefetch=1,
    )(*head_args)
    context0, linv0 = first_heads[3], first_heads[5]
    cot_out, in_row = simple(
        chain,
        functools.partial(gather_kernel, capacity),
        "cot_gather",
        (in_target, cotangent),
        [sds((slots, width), BF), sds((1, slots), I32)],
    )
    cot_in = lax.all_to_all(cot_out, ("seq", "batch"), split_axis=0, concat_axis=0, tiled=True)
    *rest_heads, first_low, normed1, inv1, ctx_turned = call(
        chain,
        functools.partial(attend_rest_kernel, heads),
        "attend_rest",
        grid=(groups - 1,),
        in_specs=head_specs(1)
        + [
            whole_block((rows, cols)), pl.BlockSpec((cols, width), lambda g, *_: (0, 0)),
            pl.BlockSpec((cols, width), lambda g, *_: (1 + g, 0)), vec_spec, vec_spec, vec_spec,
        ],
        out_specs=head_outs
        + [
            whole_block((rows, width)), whole_block((rows, width)), whole_block((rows, 1)),
            whole_block((width, rows)),
        ],
        out_shape=head_shapes(groups - 1) + [low, wide, sds((rows, 1), F32), sds((width, rows), BF)],
        scratch=[pltpu.VMEM((rows, width), F32), pltpu.VMEM((rows, width), BF)],
        prefetch=1,
    )(*head_args, context0, w_out, w_out, out_bias, norm1_gain, norm1_bias)
    linv_rest = rest_heads[5]

    blk = ff // 4
    hid, slope, normed2, inv2, mixed_out, first_turned = call(
        chain,
        ffn_kernel,
        "ffn",
        grid=(4,),
        in_specs=[
            whole_block((rows, width)),
            pl.BlockSpec((width, blk), lambda j, *_: (0, j)),
            whole_block((ff,)),
            pl.BlockSpec((blk, width), lambda j, *_: (j, 0)),
            vec_spec, vec_spec, vec_spec, whole_block((1, rows)),
        ],
        out_specs=[
            pl.BlockSpec((rows, blk), lambda j, *_: (0, j)),
            pl.BlockSpec((rows, blk), lambda j, *_: (0, j)),
            whole_block((rows, width)), whole_block((rows, 1)), whole_block((slots, width)),
            whole_block((width, rows)),
        ],
        out_shape=[
            sds((rows, ff), BF), sds((rows, ff), BF), wide, sds((rows, 1), F32),
            sds((slots, width), BF), sds((width, rows), BF),
        ],
        scratch=[pltpu.VMEM((rows, width), F32)],
        prefetch=1,
    )(ids, first_low, w_in, in_bias, w_down, down_bias, norm2_gain, norm2_bias, slot_row)
    mixed_in = lax.all_to_all(mixed_out, ("seq", "batch"), split_axis=0, concat_axis=0, tiled=True)

    def quarter(first):
        def at(j, ids_ref):
            rel = jnp.where(j == 0, 3, 1) if first else jnp.where(j == 0, 2, 0)
            return jnp.bitwise_xor(ids_ref[0], rel)

        return at

    far, near = quarter(True), quarter(False)
    wd_spec = lambda at: pl.BlockSpec((blk, width), lambda j, i: (at(j, i), 0))
    act_spec = lambda at: pl.BlockSpec((rows, blk), lambda j, i: (0, at(j, i)))
    bias_spec = lambda at: pl.BlockSpec((1, blk), lambda j, i: (0, at(j, i)))
    gw_spec = pl.BlockSpec((1, blk, width), lambda j, *_: (j, 0, 0))
    g_pre2, g_branch, vec2, act_half, bias_a, gwd_far = call(
        chain,
        down_back_kernel,
        "down_back",
        grid=(2,),
        in_specs=[
            whole_block((1, rows)), whole_block((slots, width)), whole_block((rows, width)),
            whole_block((rows, 1)), vec_spec, wd_spec(far), act_spec(far), act_spec(far),
        ],
        out_specs=[
            whole_block((rows, width)), whole_block((rows, width)), whole_block((8, width)),
            act_spec(far), bias_spec(far), gw_spec,
        ],
        out_shape=[
            wide, low, sds((8, width), F32), sds((rows, ff), BF), sds((1, ff), F32),
            sds((2, blk, width), BF),
        ],
        prefetch=1,
    )(ids, slot_row, cot_in, normed2, inv2, norm2_gain, w_down, slope, hid)
    gwd_mate = exchange(gwd_far, "seq", 1)
    any_spec = pl.BlockSpec(memory_space=pl.ANY)
    g_act, bias_b = call(
        chain,
        act_back_kernel,
        "act_back",
        grid=(2,),
        in_specs=[whole_block((rows, width)), wd_spec(near), act_spec(near), any_spec],
        out_specs=[act_spec(near), bias_spec(near)],
        out_shape=[sds((rows, ff), BF), sds((1, ff), F32)],
        prefetch=1,
        aliases={4: 0},
    )(ids, g_branch, w_down, slope, act_half)
    share_spec = pl.BlockSpec((blk, width), lambda j, *_: (0, 0))
    send, keep = call(
        chain,
        down_grad_kernel,
        "down_grad",
        grid=(2,),
        in_specs=[act_spec(near), whole_block((rows, width)), gw_spec],
        out_specs=[share_spec, share_spec],
        out_shape=[sds((blk, width), BF)] * 2,
        prefetch=1,
    )(ids, hid, g_branch, gwd_mate)
    down_share = Share(chain, ids, "w_down", send, keep)

    part = width // 4
    xt_half = lambda at: pl.BlockSpec((2 * part, rows), lambda j: (at, 0))
    act_col = pl.BlockSpec((rows, blk), lambda j: (0, j))
    gwi_spec = pl.BlockSpec((2 * part, blk), lambda j: (0, j))
    gwi_far = call(
        chain,
        in_grad_kernel,
        "in_grad_far",
        grid=(4,),
        in_specs=[xt_half(0), act_col],
        out_specs=gwi_spec,
        out_shape=sds((2 * part, ff), BF),
    )(first_turned, g_act)
    gwi_mate = exchange(gwi_far, "seq", 1)

    g_pre1, g_ctx, vec1, gwo_far, gwo_near = call(
        chain,
        first_back_kernel,
        "first_back",
        grid=(4,),
        in_specs=[
            whole_block((rows, width)), act_col, pl.BlockSpec((width, blk), lambda j: (0, j)),
            whole_block((rows, width)), whole_block((rows, 1)), vec_spec,
            whole_block((width, width)), whole_block((width, rows)), whole_block(linv0.shape),
            whole_block(linv_rest.shape),
        ],
        out_specs=[
            whole_block((rows, width)), whole_block((rows, width)), whole_block((8, width)),
            whole_block((2 * part, width)), whole_block((2 * part, width)),
        ],
        out_shape=[
            wide, low, sds((8, width), F32), sds((2 * part, width), BF), sds((2 * part, width), BF),
        ],
        scratch=[pltpu.VMEM((rows, width), F32)],
    )(g_pre2, g_act, w_in, normed1, inv1, norm1_gain, w_out, ctx_turned, linv0, linv_rest)

    one_share = pl.BlockSpec((part, blk), lambda j: (0, j))
    send, keep = call(
        chain,
        in_grad_add_kernel,
        "in_grad_near",
        grid=(4,),
        in_specs=[xt_half(1), act_col, gwi_spec],
        out_specs=[one_share, one_share],
        out_shape=[sds((part, ff), BF)] * 2,
    )(first_turned, g_act, gwi_mate)
    in_share = Share(chain, ids, "w_in", send, keep)

    projs, vecs, fars, nears = [], [], [gwo_far], [gwo_near]
    steps = heads // pair

    def group_back(g):
        arrays, base = (first_heads, 0) if g == 0 else (rest_heads, g - 1)
        own_col = pl.BlockSpec((rows, 128), lambda p: (0, base * steps + p))
        all_col = pl.BlockSpec((rows, 128), lambda p: (0, g * steps + p))
        proj, vec, gw_far, gw_near = call(
            chain,
            functools.partial(attend_back_kernel, g * heads, pair),
            "attend_back",
            grid=(steps,),
            in_specs=[
                smem(), smem(), own_col, own_col, own_col,
                pl.BlockSpec((pair, 2, half, half), lambda p: (base * steps + p, 0, 0, 0)),
                all_col, own_col, whole_block((width, rows)),
            ],
            out_specs=[
                whole_block((rows, 3 * cols)), whole_block((1, 3 * cols)),
                whole_block((2 * part, 3 * cols)), whole_block((2 * part, 3 * cols)),
            ],
            out_shape=[
                sds((rows, 3 * cols), BF), sds((1, 3 * cols), F32),
                sds((2 * part, 3 * cols), BF), sds((2 * part, 3 * cols), BF),
            ],
            scratch=[pltpu.VMEM((rows, 128), F32)] * 3,
        )(
            seq_lengths, head_swap, *arrays[:3], arrays[4], g_ctx, arrays[3], x_turned
        )
        projs.append(proj)
        vecs.append(vec)
        fars.append(gw_far)
        nears.append(gw_near)

    def attention_share(first, last, name):
        own = nears[first:last]
        sizes = tuple(a.shape[0] // 2 for a in own)
        mates = [exchange(a, "seq", 1) for a in fars[first:last]]
        send, keep = simple(
            chain,
            functools.partial(first_add_kernel, sizes),
            name + "_x",
            (*own, *mates),
            [sds((sum(sizes), width), BF)] * 2,
        )
        return Share(chain, ids, name, send, keep)

    group_back(0)
    down_share.step_y()
    share_a = attention_share(0, 2, "attn_a")
    group_back(1)
    down_share.step_z()
    group_back(2)
    down_share.step_far()
    vec_far, vec_near = simple(
        chain,
        functools.partial(vector_kernel, groups),
        "vectors",
        (ids, vec2, bias_a, bias_b, vec1, *vecs),
        [sds((64, width), BF)] * 2,
        1,
    )
    fars.append(vec_far)
    nears.append(vec_near)
    in_share.step_y()
    share_b = attention_share(2, 5, "attn_b")
    down_share.step_back()
    in_share.step_z()
    share_a.step_y()
    (mixed,) = simple(
        chain, place_kernel, "mixed_place", (in_row, mixed_in), [sds((ffn_rows, width), BF)]
    )
    in_share.step_far()
    share_a.step_z()
    share_b.step_y()
    share_a.step_far()
    in_share.step_back()
    input_grad = call(
        chain,
        functools.partial(input_grad_kernel, groups),
        "input_grad",
        grid=(groups,),
        in_specs=[whole_block((rows, 3 * cols))] * groups
        + [
            pl.BlockSpec((width, cols), lambda g: (0, g)),
            pl.BlockSpec((width, cols), lambda g: (0, groups + g)),
            pl.BlockSpec((width, cols), lambda g: (0, 2 * groups + g)),
            whole_block((rows, width)),
        ],
        out_specs=whole_block((rows, width)),
        out_shape=low,
        scratch=[pltpu.VMEM((rows, width), F32)],
    )(*projs, w_qkv, w_qkv, w_qkv, g_pre1)
    share_b.step_z()
    share_a.step_back()
    share_b.step_far()
    g_w_down = down_share.join()
    g_w_in = in_share.join()
    share_b.step_back()
    one = lambda size: sds((size,), F32)
    g_w_qkv, g_w_out, g_qv, g_in_bias, g_n2g, g_n2b, g_down_bias, g_n1g, g_n1b, g_out_bias = simple(
        chain,
        functools.partial(attend_join_kernel, groups),
        "attn_join",
        (ids, *share_a.pieces, *share_b.pieces),
        [sds((part, 3 * width), F32), sds((part, width), F32), one(width // 2), one(width)]
        + [one(part)] * 6,
        1,
        scratch=[pltpu.VMEM(share_a.shape, F32), pltpu.VMEM(share_b.shape, F32)],
    )
    return (
        mixed, input_grad, g_w_qkv, g_qv, g_w_out, g_out_bias, g_n1g, g_n1b, g_w_in, g_in_bias,
        g_w_down, g_down_bias, g_n2g, g_n2b,
    )


def solution(mesh):
    rows_spec = P(("seq", "batch"), None)
    in_specs = (
        rows_spec, rows_spec, P(), P(("seq", "batch")), P(), P(), P(), P(), P(), P(), P(), P(),
        P(), P(), P(), P(), rows_spec,
    )
    out_specs = (
        rows_spec, rows_spec, P("seq", None), P("seq"), P("seq", None), P("seq"), P("seq"),
        P("seq"), P("seq", None), P("seq"), P("seq", None), P("seq"), P("seq"), P("seq"),
    )
    return jax.shard_map(body, mesh=mesh, in_specs=in_specs, out_specs=out_specs, check_vma=False)
```

```python
import functools

import jax
import jax.numpy as jnp
from jax import lax
from jax.experimental import pallas as pl
from jax.experimental.pallas import tpu as pltpu
from jax.sharding import PartitionSpec as P

EPS = 1e-05
BIG = 1e30
BF = jnp.bfloat16
F32 = jnp.float32
I32 = jnp.int32
MIB = 1 << 20
COST = 5e10
COST_SMALL = 1e10

NN = (((1,), (0,)), ((), ()))
NT = (((1,), (1,)), ((), ()))
TN = (((0,), (0,)), ((), ()))


def mm(left_op, right_op, dims):
    return lax.dot_general(left_op, right_op, dims, preferred_element_type=F32)


def sds(shape, dtype):
    return jax.ShapeDtypeStruct(shape, dtype)


def hbm(shape, dtype):
    return pltpu.HBM(shape, dtype)


def vmem(shape, dtype):
    return pltpu.VMEM(shape, dtype)


def whole_block(shape):
    zeros = (0,) * len(shape)
    return pl.BlockSpec(shape, lambda *_: zeros)


def smem():
    return pl.BlockSpec(memory_space=pltpu.SMEM)


class Chain:
    def __init__(self):
        self.last = None
        self.spaces = {}

    def link(self, outs, shapes):
        flat = jax.tree.leaves(outs)
        self.last = min(flat, key=lambda a: a.size * a.dtype.itemsize)
        for out, shape in zip(flat, shapes if isinstance(shapes, (list, tuple)) else [shapes]):
            if getattr(shape, "memory_space", None) in (pltpu.HBM, pltpu.VMEM):
                self.keep(shape.memory_space, out)

    def keep(self, space, *arrays):
        for array in arrays:
            self.spaces[id(array)] = (space, array)

    def place(self, array):
        if id(array) in self.spaces:
            return pltpu.with_memory_space_constraint(array, self.spaces[id(array)][0])
        return array


def call(chain, body, name, *, grid, in_specs, out_specs, out_shape, scratch=(), prefetch=0,
         aliases=None, vmem=56, cost=COST, free=()):
    count = prefetch + len(in_specs)
    before = [] if chain.last is None else [chain.last]

    def ordered(*refs):
        body(*refs[:count], *refs[count + len(before) :])

    kernel = pl.pallas_call(
        ordered,
        name=name,
        grid_spec=pltpu.PrefetchScalarGridSpec(
            num_scalar_prefetch=prefetch,
            grid=grid,
            in_specs=list(in_specs) + [pl.BlockSpec(memory_space=pl.ANY)] * len(before),
            out_specs=out_specs,
            scratch_shapes=list(scratch),
        ),
        out_shape=out_shape,
        input_output_aliases=aliases or {},
        compiler_params=pltpu.CompilerParams(
            vmem_limit_bytes=vmem * MIB, dimension_semantics=("arbitrary",) * len(grid)
        ),
        cost_estimate=pl.CostEstimate(flops=int(cost), bytes_accessed=1, transcendentals=0),
    )

    def run(*args):
        placed = [a if at in free else chain.place(a) for at, a in enumerate(args)]
        outs = kernel(*placed, *[chain.place(a) for a in before])
        chain.link(outs, out_shape)
        return outs

    return run


def slot_of(rel):
    return jnp.where(rel == 0, 3, jnp.where(rel == 3, 0, rel))


def floor_div(values, divisor):
    return jnp.floor((values.astype(F32) + 0.5) * (1.0 / divisor)).astype(I32)


def route_kernel(ffn_rows, capacity, place_ref, slot_ref, target_ref):
    devices = target_ref.shape[0]
    rows = place_ref.shape[1]
    place = place_ref[...]
    live = place >= 0
    dev = jnp.where(live, floor_div(place, ffn_rows), -1)
    local = place - dev * ffn_rows
    hit = lax.broadcasted_iota(I32, (devices, rows), 0) == dev
    onehot = hit.astype(F32)
    upper = (
        lax.broadcasted_iota(I32, (rows, rows), 0) <= lax.broadcasted_iota(I32, (rows, rows), 1)
    ).astype(F32).astype(BF)
    running = mm(onehot.astype(BF), upper, NN)
    rank = (jnp.sum(running * onehot, axis=0, keepdims=True) - 1.0).astype(I32)
    slot_ref[...] = jnp.where(live, dev * capacity + rank, devices * capacity)
    ranked = (lax.broadcasted_iota(I32, (capacity, rows), 0) == rank).astype(F32).astype(BF)
    high = (local >> 5).astype(F32)
    low = (local & 31).astype(F32)
    filled = mm(onehot.astype(BF), ranked, NT)
    high_at = mm((onehot * high).astype(BF), ranked, NT)
    low_at = mm((onehot * low).astype(BF), ranked, NT)
    target = (high_at * 32.0 + low_at).astype(I32)
    target_ref[...] = jnp.where(filled > 0.5, target, ffn_rows)


def expand_targets(target, capacity):
    devices = target.shape[0]
    slots = devices * capacity
    lane = lax.broadcasted_iota(I32, (capacity, slots), 1)
    lane_dev = floor_div(lane, capacity)
    spread = ((lane - lane_dev * capacity) == lax.broadcasted_iota(I32, (capacity, slots), 0)).astype(
        F32
    ).astype(BF)
    high = mm((target >> 5).astype(F32).astype(BF), spread, NN)
    low = mm((target & 31).astype(F32).astype(BF), spread, NN)
    wide = high * 32.0 + low
    own_dev = floor_div(lax.broadcasted_iota(I32, (devices, slots), 1), capacity)
    own = own_dev == lax.broadcasted_iota(I32, (devices, slots), 0)
    return jnp.sum(jnp.where(own, wide, 0.0), axis=0, keepdims=True).astype(I32)


def onehot_rows(row_index, row_count):
    lanes = row_index.shape[1]
    return (lax.broadcasted_iota(I32, (row_count, lanes), 0) == row_index).astype(F32).astype(BF)


def onehot_cols(row_index, col_count):
    rows = row_index.shape[1]
    column = jnp.broadcast_to(row_index.astype(F32), (128, rows)).T[:, :1].astype(I32)
    return (lax.broadcasted_iota(I32, (rows, col_count), 1) == column).astype(F32).astype(BF)


def gather_kernel(capacity, target_ref, cot_ref, out_ref, row_ref):
    row = expand_targets(target_ref[...], capacity)
    row_ref[...] = row
    chosen = onehot_cols(row, cot_ref.shape[0])
    out_ref[...] = mm(chosen, cot_ref[...], NN).astype(BF)


def place_kernel(row_ref, in_ref, out_ref):
    chosen = onehot_rows(row_ref[...], out_ref.shape[0])
    out_ref[...] = mm(chosen, in_ref[...], NN).astype(BF)


def norm_rows(values):
    center = values - jnp.mean(values, axis=-1, keepdims=True)
    inverse = lax.rsqrt(jnp.mean(center * center, axis=-1, keepdims=True) + EPS)
    return center * inverse, inverse


def project(x_ref, w_refs, bq, bv, outs):
    x = x_ref[...]
    wq_ref, wk_ref, wv_ref = w_refs
    q_ref, k_ref, v_ref = outs
    q_ref[...] = (mm(x, wq_ref[...], NN) + bq).astype(BF)
    k_ref[...] = mm(x, wk_ref[...], NN).astype(BF)
    v_ref[...] = (mm(x, wv_ref[...], NN) + bv).astype(BF)


def attend_pair(
    head_base, heads, len_ref, swap_ref, q_ref, k_ref, v_ref, cut, ctx_ref, soft_ref, linv_ref
):
    rows = q_ref.shape[0]
    half = rows // 2
    quarter = rows // 4
    head_size = 128 // heads
    scale = head_size ** (-0.5)
    len0, len1 = len_ref[0, 0], len_ref[0, 1]
    is_long = len1 == 0
    lane = lax.broadcasted_iota(I32, (1, 128), 1)
    row = lax.broadcasted_iota(I32, (half, 1), 0)
    row_quarter = (row >= quarter).astype(I32)
    for b in range(2):
        q_rows = slice(b * half, (b + 1) * half)
        q_blk = q_ref[q_rows, cut].astype(F32) * scale
        out_blk = linv_blk = None
        for sub in range(heads):
            swapped = swap_ref[head_base + sub] == 1
            cross = jnp.logical_and(is_long, swapped)
            kb = jnp.where(cross, 1 - b, b)
            limit = jnp.where(is_long, len0 - kb * half, jnp.where(kb == 0, len0, len1))
            mine = jnp.logical_and(lane >= sub * head_size, lane < (sub + 1) * head_size)
            spare = ((sub + 1) % heads) * head_size
            key_rows = pl.ds(pl.multiple_of(kb * half, half), half)
            k_one = jnp.where(mine, k_ref[key_rows, cut].astype(F32), 0.0)
            q_one = jnp.where(mine, q_blk, 0.0)
            for part in range(2):
                other = jnp.where(swapped, 1 - part, part)
                band_ok = jnp.logical_or(is_long, row_quarter == other)
                bias = jnp.where(jnp.logical_and(band_ok, row < limit), 0.0, -BIG)
                at = lane == spare + part
                k_one = jnp.where(at, bias, k_one)
                q_one = jnp.where(at, jnp.where(row_quarter == part, 1.0, 0.0), q_one)
            scores = mm(q_one.astype(BF), k_one.astype(BF), NT)
            top = jnp.max(scores, axis=1, keepdims=True)
            weights = jnp.exp(scores - top)
            linv = 1.0 / jnp.sum(weights, axis=1, keepdims=True)
            soft = weights.astype(BF)
            soft_ref[sub, b] = soft
            mixed = mm(soft, v_ref[key_rows, cut], NN) * linv
            out_blk = mixed if out_blk is None else jnp.where(mine, mixed, out_blk)
            linv_blk = (
                jnp.broadcast_to(linv, mixed.shape)
                if linv_blk is None
                else jnp.where(mine, linv, linv_blk)
            )
        ctx_ref[q_rows, :] = out_blk.astype(BF)
        linv_ref[q_rows, :] = linv_blk


def attend_kernel(
    first, pairs, heads, ids_ref, len_ref, swap_ref, x_ref, wq_ref, wk_ref, wv_ref, b_ref, *refs
):
    if first == 0:
        q_ref, k_ref, v_ref, ctx_ref, soft_ref, linv_ref, xt_ref = refs
    else:
        (
            ctx0_ref, wo0_ref, wo_ref, ob_ref, gain_ref, shift_ref,
            q_ref, k_ref, v_ref, ctx_ref, soft_ref, linv_ref, first_ref, normed_ref, inv_ref,
            ctxt_ref, acc_ref, ctx_all,
        ) = refs
    cols = q_ref.shape[1]
    width = x_ref.shape[1]
    group = first + pl.program_id(0)
    pair = pl.program_id(1)

    @pl.when(pair == 0)
    def _():
        bq = b_ref[pl.ds(pl.multiple_of(group * cols, cols), cols)].reshape(1, -1)
        bv = b_ref[pl.ds(pl.multiple_of(width + group * cols, cols), cols)].reshape(1, -1)
        project(x_ref, (wq_ref, wk_ref, wv_ref), bq, bv, (q_ref, k_ref, v_ref))

    cut = pl.ds(pl.multiple_of(pair * 128, 128), 128)
    attend_pair(
        group * (pairs * heads) + pair * heads, heads, len_ref, swap_ref, q_ref, k_ref, v_ref, cut,
        ctx_ref, soft_ref, linv_ref,
    )
    if first == 0:

        @pl.when(pair == pairs - 1)
        def _():
            write_turned(x_ref[...], ids_ref[0], xt_ref)

        return
    ctx_all[:, pl.ds(pl.multiple_of(group * cols + pair * 128, 128), 128)] = ctx_ref[...]

    @pl.when(pair == pairs - 1)
    def _():
        own = pl.ds(pl.multiple_of(group * cols, cols), cols)
        part_sum = mm(ctx_all[:, own], wo_ref[...], NN)

        @pl.when(group == first)
        def _():
            ctx_all[:, :cols] = ctx0_ref[...]
            acc_ref[...] = part_sum + mm(ctx0_ref[...], wo0_ref[...], NN)

        @pl.when(group > first)
        def _():
            acc_ref[...] += part_sum

        @pl.when(pl.program_id(0) == pl.num_programs(0) - 1)
        def _():
            attn = acc_ref[...] + ob_ref[...].reshape(1, -1)
            normed, inverse = norm_rows(x_ref[...].astype(F32) + attn)
            normed_ref[...] = normed.astype(BF)
            inv_ref[...] = inverse
            out = normed * gain_ref[...].reshape(1, -1) + shift_ref[...].reshape(1, -1)
            first_ref[...] = out.astype(BF)
            write_turned(ctx_all[...], ids_ref[0], ctxt_ref)


def write_turned(values, seq_id, out_ref):
    turned = values.T
    quarter = turned.shape[0] // 4
    for q in range(4):
        at = slot_of(jnp.bitwise_xor(seq_id, q))
        out_ref[pl.ds(pl.multiple_of(at * quarter, quarter), quarter), :] = turned[
            q * quarter : (q + 1) * quarter
        ]


def block_cols(index, size):
    return pl.ds(pl.multiple_of(index * size, size), size)


def ffn_kernel(
    ids_ref, x_ref, wi_ref, bi_ref, wd_ref, bd_ref, gain_ref, shift_ref,
    hid_ref, slope_ref, normed_ref, inv_ref, out_ref, xt_ref, acc_ref,
):
    step = pl.program_id(0)
    steps = pl.num_programs(0)
    x = x_ref[...]
    own = block_cols(step, wi_ref.shape[1])
    pre = mm(x, wi_ref[...], NN) + bi_ref[own].reshape(1, -1)
    phi = 0.5 * (1.0 + lax.erf(pre * 0.7071067811865476))
    hid = (pre * phi).astype(BF)
    hid_ref[...] = hid
    slope_ref[...] = (phi + pre * jnp.exp(-0.5 * pre * pre) * 0.3989422804014327).astype(BF)
    part_sum = mm(hid, wd_ref[...], NN)

    @pl.when(step == 0)
    def _():
        acc_ref[...] = part_sum
        write_turned(x, ids_ref[0], xt_ref)

    @pl.when(step > 0)
    def _():
        acc_ref[...] += part_sum

    @pl.when(step == steps - 1)
    def _():
        branch = acc_ref[...] + bd_ref[...].reshape(1, -1)
        normed, inverse = norm_rows(x_ref[...].astype(F32) + branch)
        normed_ref[...] = normed.astype(BF)
        inv_ref[...] = inverse
        out = normed * gain_ref[...].reshape(1, -1) + shift_ref[...].reshape(1, -1)
        out_ref[...] = out.astype(BF)


def norm_back(upstream, normed, inverse, gain):
    scaled = upstream * gain
    inner = (
        scaled
        - jnp.mean(scaled, axis=-1, keepdims=True)
        - normed * jnp.mean(scaled * normed, axis=-1, keepdims=True)
    )
    return inner * inverse


def put_rows(ref, *rows):
    for at, row in enumerate(rows):
        ref[at : at + 1, :] = row


def store_halves(ids_ref, total, mine_ref, other_ref):
    half = mine_ref.shape[1]
    second = (ids_ref[1] & 1) == 1
    left, right = total[:, :half], total[:, half:]
    mine_ref[...] = jnp.where(second, right, left)
    other_ref[...] = jnp.where(second, left, right)


def quarter_at(step, ids_ref, near):
    rel = jnp.where(step == 0, 2, 0) if near else jnp.where(step == 0, 3, 1)
    return jnp.bitwise_xor(ids_ref[0], rel)


def act_back(ids_ref, near, branch, wd_ref, slope_ref, act_ref, bias_ref):
    own = block_cols(quarter_at(pl.program_id(0), ids_ref, near), wd_ref.shape[0])
    g_act = (mm(branch, wd_ref[...], NT) * slope_ref[:, own].astype(F32)).astype(BF)
    act_ref[:, own] = g_act
    bias_ref[:, own] = jnp.sum(g_act.astype(F32), axis=0, keepdims=True)


def cot_back_kernel(
    slot_ref, in_ref, normed_ref, inv_ref, gain_ref, pre_ref, branch_ref, vec_ref
):
    chosen = onehot_cols(slot_ref[...], in_ref.shape[0])
    cot = mm(chosen, in_ref[...], NN)
    normed = normed_ref[...].astype(F32)
    g_pre = norm_back(cot, normed, inv_ref[...], gain_ref[...].reshape(1, -1))
    pre_ref[...] = g_pre
    branch = g_pre.astype(BF)
    branch_ref[...] = branch
    put_rows(
        vec_ref,
        jnp.sum(cot * normed, axis=0, keepdims=True),
        jnp.sum(cot, axis=0, keepdims=True),
        jnp.sum(branch.astype(F32), axis=0, keepdims=True),
    )


def down_back_kernel(ids_ref, branch_ref, wd_ref, slope_ref, hid_ref, act_ref, bias_ref, gw_ref):
    branch = branch_ref[...]
    act_back(ids_ref, False, branch, wd_ref, slope_ref, act_ref, bias_ref)
    own = block_cols(quarter_at(pl.program_id(0), ids_ref, False), wd_ref.shape[0])
    gw_ref[pl.program_id(0)] = mm(hid_ref[:, own], branch, TN).astype(BF)


def act_back_kernel(ids_ref, branch_ref, wd_ref, slope_ref, old_act, act_ref, bias_ref):
    act_back(ids_ref, True, branch_ref[...], wd_ref, slope_ref, act_ref, bias_ref)


def down_grad_kernel(ids_ref, hid_ref, branch_ref, mate_ref, send_ref, keep_ref):
    step = pl.program_id(0)
    own = block_cols(quarter_at(step, ids_ref, True), send_ref.shape[0])
    grad = mm(hid_ref[:, own], branch_ref[...], TN).astype(BF).astype(F32)
    total = (grad + mate_ref[step].astype(F32)).astype(BF)

    @pl.when(step == 0)
    def _():
        send_ref[...] = total

    @pl.when(step == 1)
    def _():
        keep_ref[...] = total


def in_grad_kernel(near, ids_ref, xt_ref, act_ref, *refs):
    half = xt_ref.shape[0] // 2
    turned = xt_ref[half:, :] if near else xt_ref[:half, :]
    grad = mm(turned, act_ref[...], NN).astype(BF)
    if not near:
        refs[0][...] = grad
        return
    mate_ref, mine_ref, other_ref = refs
    total = (grad.astype(F32) + mate_ref[...].astype(F32)).astype(BF)
    store_halves(ids_ref, total, mine_ref, other_ref)


def first_back_kernel(
    pre2_ref, act_ref, wi_ref, normed_ref, inv_ref, gain_ref, wo_ref, linv0_ref, linv_ref,
    pre1_ref, gattn_ref, gctx_ref, vec_ref, acc_ref,
):
    step = pl.program_id(0)
    part_sum = mm(act_ref[:, block_cols(step, wi_ref.shape[1])], wi_ref[...], NT)

    @pl.when(step == 0)
    def _():
        acc_ref[...] = part_sum

    @pl.when(step > 0)
    def _():
        acc_ref[...] += part_sum

    @pl.when(step == pl.num_programs(0) - 1)
    def _():
        g_first = (pre2_ref[...] + acc_ref[...]).astype(BF).astype(F32)
        normed = normed_ref[...].astype(F32)
        g_pre = norm_back(g_first, normed, inv_ref[...], gain_ref[...].reshape(1, -1))
        pre1_ref[...] = g_pre
        g_attn = g_pre.astype(BF)
        put_rows(
            vec_ref,
            jnp.sum(g_first * normed, axis=0, keepdims=True),
            jnp.sum(g_first, axis=0, keepdims=True),
            jnp.sum(g_attn.astype(F32), axis=0, keepdims=True),
        )
        g_ctx = mm(g_attn, wo_ref[...], NT)
        cols = linv0_ref.shape[1]
        gctx_ref[:, :cols] = (g_ctx[:, :cols] * linv0_ref[...]).astype(BF)
        gctx_ref[:, cols:] = (g_ctx[:, cols:] * linv_ref[...]).astype(BF)
        gattn_ref[...] = g_attn


def attend_back_kernel(
    head_base, heads, len_ref, swap_ref, q_ref, k_ref, v_ref, soft_ref, gctx_ref, ctx_ref,
    proj_ref, vec_ref, gq_s, gk_s, gv_s,
):
    step = pl.program_id(0)
    rows = q_ref.shape[0]
    half = rows // 2
    head_size = 128 // heads
    scale = head_size ** (-0.5)
    is_long = len_ref[0, 1] == 0
    lane = lax.broadcasted_iota(I32, (1, 128), 1)
    for sub in range(heads):
        swapped = swap_ref[head_base + step * heads + sub] == 1
        cross = jnp.logical_and(is_long, swapped)
        mine = jnp.logical_and(lane >= sub * head_size, lane < (sub + 1) * head_size)
        for b in range(2):
            q_rows = slice(b * half, (b + 1) * half)
            kb = jnp.where(cross, 1 - b, b)
            key_rows = pl.ds(pl.multiple_of(kb * half, half), half)
            soft = soft_ref[sub, b]
            up = gctx_ref[q_rows, :]
            up_one = jnp.where(mine, up, jnp.zeros_like(up))
            inner = jnp.sum(
                up_one.astype(F32) * ctx_ref[q_rows, :].astype(F32), axis=1, keepdims=True
            )
            g_soft = mm(up_one, v_ref[key_rows, :], NT)
            g_scores = (soft.astype(F32) * (g_soft - inner)).astype(BF)
            g_q = mm(g_scores, k_ref[key_rows, :], NN) * scale
            g_k = mm(g_scores, q_ref[q_rows, :], TN) * scale
            g_v = mm(soft, up, TN)
            if sub == 0:
                gq_s[q_rows, :] = g_q
                gk_s[key_rows, :] = g_k
                gv_s[key_rows, :] = g_v
            else:
                gq_s[q_rows, :] = jnp.where(mine, g_q, gq_s[q_rows, :])
                gk_s[key_rows, :] = jnp.where(mine, g_k, gk_s[key_rows, :])
                gv_s[key_rows, :] = jnp.where(mine, g_v, gv_s[key_rows, :])
    cols = proj_ref.shape[1] // 3
    for at, ref in enumerate((gq_s, gk_s, gv_s)):
        low = ref[...].astype(BF)
        out_cols = pl.ds(pl.multiple_of(at * cols + step * 128, 128), 128)
        proj_ref[:, out_cols] = low
        vec_ref[:, out_cols] = jnp.sum(low.astype(F32), axis=0, keepdims=True)


def input_grad_kernel(groups, *refs):
    proj_refs, (wq_ref, wk_ref, wv_ref, pre_ref, out_ref, acc_ref) = refs[:groups], refs[groups:]
    step = pl.program_id(0)
    cols = wq_ref.shape[1]

    @pl.when(step == 0)
    def _():
        acc_ref[...] = pre_ref[...]

    for at, proj_ref in enumerate(proj_refs):

        @pl.when(step == at)
        def _():
            acc_ref[...] += (
                mm(proj_ref[:, :cols], wq_ref[...], NT)
                + mm(proj_ref[:, cols : 2 * cols], wk_ref[...], NT)
                + mm(proj_ref[:, 2 * cols :], wv_ref[...], NT)
            )

    @pl.when(step == groups - 1)
    def _():
        out_ref[...] = acc_ref[...].astype(BF)


def vector_rows(ids_ref, rel_of, rows_ref, base_of, vec_refs):
    vec2_ref, bias_a, bias_b, vec1_ref, *qkv_refs = vec_refs
    width = vec1_ref.shape[1]
    cols = width // len(qkv_refs)
    wide = jnp.concatenate(
        [ref[:, :cols] for ref in qkv_refs] + [ref[:, 2 * cols :] for ref in qkv_refs], axis=1
    )
    for q in range(4):
        rel = jnp.bitwise_xor(ids_ref[0], q)
        odd = (rel & 1) == 1
        hid_q = slice(q * (bias_a.shape[1] // 4), (q + 1) * (bias_a.shape[1] // 4))
        rows = [jnp.where(odd, bias_a[:, hid_q], bias_b[:, hid_q])]
        qv = width // 2
        rows.append(wide[:, q * qv : (q + 1) * qv])
        own = slice(q * (width // 4), (q + 1) * (width // 4))
        for ref in (vec2_ref, vec1_ref):
            for at in range(3):
                rows.append(ref[at : at + 1, own])

        def store(base):
            for r, row in enumerate(rows):
                rows_ref[base + r : base + r + 1, : row.shape[1]] = row

        for want, base in zip(rel_of, base_of):
            pl.when(rel == want)(functools.partial(store, base))


def share_grad_kernel(near, y_first, count, extra, ids_ref, *refs):
    pairs = [(refs[2 * at], refs[2 * at + 1]) for at in range(count)]
    refs = refs[2 * count :]
    part = pairs[0][0].shape[0] // 4
    size = count * part + extra
    if extra:
        *refs, rows_ref = refs
    if near:
        *vec_refs, mate_ref, left_ref, right_ref = refs
    else:
        *vec_refs, out_ref = refs

    def put(base, value):
        rows = slice(base, base + value.shape[0])
        if near:
            value = value.astype(F32) + mate_ref[rows, :].astype(F32)
        value = value.astype(BF)
        if not near:
            out_ref[rows, :] = value
        elif y_first:
            store_halves(ids_ref, value, left_ref.at[rows], right_ref.at[rows])
        else:
            out = left_ref if base < size else right_ref
            base -= 0 if base < size else size
            out[base : base + value.shape[0], :] = value

    for at, (turned_ref, product_ref) in enumerate(pairs):
        cut = 2 * part
        turned = turned_ref[cut:, :] if near else turned_ref[:cut, :]
        grad = mm(turned, product_ref[...], NN).astype(BF)
        put(at * part, grad[:part])
        put(size + at * part, grad[part:])
    if extra:
        rows_ref[...] = jnp.zeros_like(rows_ref)
        vector_rows(ids_ref, (2, 0) if near else (3, 1), rows_ref, (0, extra), vec_refs)
        for half in range(2):
            vectors = rows_ref[half * extra : (half + 1) * extra, :].astype(BF)
            put(half * size + count * part, vectors)


def split_cols_kernel(ids_ref, keep_ref, got_ref, mine_ref, other_ref):
    total = (keep_ref[...].astype(F32) + got_ref[...].astype(F32)).astype(BF)
    store_halves(ids_ref, total, mine_ref, other_ref)


def split_shares_kernel(mine_ref, got_ref, send_ref, keep_ref):
    total = (mine_ref[...].astype(F32) + got_ref[...].astype(F32)).astype(BF)
    rows = send_ref.shape[0]
    send_ref[...] = total[:rows]
    keep_ref[...] = total[rows:]


def split_rows_kernel(ids_ref, keep_ref, got_ref, mine_ref, other_ref):
    half = mine_ref.shape[0]
    bit = (ids_ref[1] >> 1) & 1

    def part(at):
        rows = pl.ds(pl.multiple_of(at * half, half), half)
        return (keep_ref[rows, :].astype(F32) + got_ref[rows, :].astype(F32)).astype(BF)

    mine_ref[...] = part(bit)
    other_ref[...] = part(1 - bit)


def add_kernel(left_ref, right_ref, out_ref):
    out_ref[...] = (left_ref[...].astype(F32) + right_ref[...].astype(F32)).astype(BF)


def join_kernel(ids_ref, own_ref, near_ref, far_own_ref, far_near_ref, out_ref):
    half_rows, half_cols = own_ref.shape
    second = (ids_ref[1] & 1) == 1
    bit = (ids_ref[1] >> 1) & 1
    for rel, (mine, other) in enumerate(((own_ref, far_own_ref), (near_ref, far_near_ref))):
        at = jnp.bitwise_xor(bit, rel)
        rows = pl.ds(pl.multiple_of(at * half_rows, half_rows), half_rows)
        a, b = mine[...].astype(F32), other[...].astype(F32)
        out_ref[rows, :half_cols] = jnp.where(second, b, a)
        out_ref[rows, half_cols:] = jnp.where(second, a, b)


def stack_kernel(ids_ref, own_ref, near_ref, out_ref):
    half = own_ref.shape[0]
    bit = (ids_ref[1] >> 1) & 1
    for rel, ref in enumerate((own_ref, near_ref)):
        at = jnp.bitwise_xor(bit, rel)
        out_ref[pl.ds(pl.multiple_of(at * half, half), half), :] = ref[...]


def join_into(ids_ref, mine_ref, other_ref, out_ref):
    half = mine_ref.shape[1]
    second = (ids_ref[1] & 1) == 1
    a, b = mine_ref[...].astype(F32), other_ref[...].astype(F32)
    out_ref[:, :half] = jnp.where(second, b, a)
    out_ref[:, half:] = jnp.where(second, a, b)


def join_kernel(ids_ref, mine_ref, other_ref, out_ref):
    join_into(ids_ref, mine_ref, other_ref, out_ref)


def attend_join_kernel(groups, ids_ref, *refs):
    a_refs, b_refs = refs[:2], refs[2:4]
    gwq_ref, gwo_ref, qv_ref, hid_ref = refs[4:8]
    vec_refs, (a_all, b_all) = refs[8:14], refs[14:]
    join_into(ids_ref, *a_refs, a_all)
    join_into(ids_ref, *b_refs, b_all)
    part, width = gwo_ref.shape
    cols = width // groups
    gwo_ref[...] = a_all[:part, :]
    places = [(a_all, part)] + [(b_all, part * at) for at in range(groups - 1)]
    for g, (ref, base) in enumerate(places):
        for at in range(3):
            gwq_ref[:, at * width + g * cols : at * width + (g + 1) * cols] = ref[
                base : base + part, at * cols : (at + 1) * cols
            ]
    base = part * (groups - 1)
    hid_ref[...] = b_all[base, :]
    qv_ref[...] = b_all[base + 1, : qv_ref.shape[0]]
    for at, ref in enumerate(vec_refs):
        ref[...] = b_all[base + 2 + at, : ref.shape[0]]


def exchange(values, axis, mask):
    count = lax.axis_size(axis)
    return lax.ppermute(values, axis, [(i, i ^ mask) for i in range(count)])


def simple(chain, body, name, args, out_shape, prefetch=0, vmem=12, scratch=(), cost=COST_SMALL):
    tensors = args[prefetch:]
    return call(
        chain,
        body,
        name,
        grid=(1,),
        in_specs=[whole_block(a.shape) for a in tensors],
        out_specs=[whole_block(o.shape) for o in out_shape],
        out_shape=out_shape,
        prefetch=prefetch,
        vmem=vmem,
        cost=cost,
        scratch=scratch,
    )(*args)


class Share:
    def __init__(self, chain, ids, name, left, right, y_first=False):
        self.chain, self.ids, self.name = chain, ids, name
        if y_first:
            self.keep, self.got = left, exchange(right, "batch", 1)
            self.shape = (left.shape[0] // 2, left.shape[1] * 2)
        else:
            self.keep, self.got = right, exchange(left, "seq", 2)
            self.shape = right.shape

    def step_x(self):
        rows, cols = self.shape
        send, self.keep = simple(
            self.chain, split_shares_kernel, self.name + "_x", (self.keep, self.got),
            [vmem((rows, cols // 2), BF)] * 2,
        )
        self.got = exchange(send, "seq", 2)

    def halve(self, kernel, shape, label, mask):
        self.keep, other = simple(
            self.chain, kernel, self.name + label, (self.ids, self.keep, self.got),
            [vmem(shape, BF)] * 2, 1,
        )
        self.got = exchange(other, "batch", mask)

    def step_y(self):
        rows, cols = self.shape
        self.halve(split_cols_kernel, (rows, cols // 2), "_y", 1)

    def step_z(self):
        rows, cols = self.shape
        self.halve(split_rows_kernel, (rows // 2, cols // 2), "_z", 2)

    def add(self, label):
        (self.keep,) = simple(
            self.chain, add_kernel, self.name + label, (self.keep, self.got),
            [vmem(self.keep.shape, BF)],
        )

    def step_far(self):
        mask = 4
        while mask <= lax.axis_size("batch") // 2:
            self.add("_a")
            self.got = exchange(self.keep, "batch", mask)
            mask *= 2

    def step_back(self):
        self.add("_f")
        self.got = exchange(self.keep, "batch", 2)

    def step_wide(self):
        rows, cols = self.shape
        (self.keep,) = simple(
            self.chain, stack_kernel, self.name + "_g", (self.ids, self.keep, self.got),
            [vmem((rows, cols // 2), BF)], 1,
        )
        self.pieces = (self.keep, exchange(self.keep, "batch", 1))

    def join(self):
        (whole,) = simple(
            self.chain, join_kernel, self.name + "_j", (self.ids, *self.pieces),
            [hbm(self.shape, F32)], 1,
        )
        return whole


def body(
    hidden_in, seq_lengths, head_swap, place, w_qkv, qv_bias, w_out, out_bias, norm1_gain,
    norm1_bias, w_in, in_bias, w_down, down_bias, norm2_gain, norm2_bias, cotangent,
):
    rows, width = hidden_in.shape
    ff = w_in.shape[1]
    ffn_rows = cotangent.shape[0]
    devices = lax.axis_size(("seq", "batch"))
    capacity = (rows + devices - 1) // devices
    slots = devices * capacity
    head_count = head_swap.shape[0]
    head_size = width // head_count
    half = rows // 2
    cols = 256
    groups = width // cols
    heads = cols // head_size
    pair = 128 // head_size
    ids = jnp.stack([lax.axis_index("seq"), lax.axis_index("batch")]).astype(I32)
    chain = Chain()
    chain.keep(pltpu.HBM, hidden_in, w_qkv, w_out, w_in, w_down, cotangent)

    slot_row, out_target = simple(
        chain,
        functools.partial(route_kernel, ffn_rows, capacity),
        "route",
        (place.reshape(1, -1),),
        [sds((1, rows), I32), sds((devices, capacity), I32)],
    )
    in_target = lax.all_to_all(out_target, ("seq", "batch"), split_axis=0, concat_axis=0, tiled=True)

    bf_rows = (rows, width)
    turned_shape = (width, rows)
    vec_spec = whole_block((width,))
    steps = heads // pair
    some = lambda count, dtype: hbm((rows, count * cols), dtype)
    col = lambda base: pl.BlockSpec((width, cols), lambda g, p, *_: (0, base + g))
    out_col = pl.BlockSpec((rows, cols), lambda g, p, *_: (0, g))
    pair_out = pl.BlockSpec((rows, 128), lambda g, p, *_: (0, g * steps + p))
    soft_spec = pl.BlockSpec((pair, 2, half, half), lambda g, p, *_: (g * steps + p, 0, 0, 0))
    head_outs = [out_col] * 3 + [pair_out, soft_spec, pair_out]
    head_shapes = lambda count: [some(count, BF)] * 4 + [
        hbm((count * heads, 2, half, half), BF), some(count, F32)
    ]
    head_args = (ids, seq_lengths, head_swap, hidden_in, w_qkv, w_qkv, w_qkv, qv_bias)
    head_specs = lambda first: [
        smem(), smem(), whole_block(bf_rows), col(first), col(groups + first),
        col(2 * groups + first), whole_block((2 * width,)),
    ]
    *first_heads, x_turned = call(
        chain,
        functools.partial(attend_kernel, 0, steps, pair),
        "attend_first",
        vmem=32,
        grid=(1, steps),
        in_specs=head_specs(0),
        out_specs=head_outs + [whole_block(turned_shape)],
        out_shape=head_shapes(1) + [hbm(turned_shape, BF)],
        prefetch=1,
    )(*head_args)
    context0, linv0 = first_heads[3], first_heads[5]
    cot_out, in_row = simple(
        chain,
        functools.partial(gather_kernel, capacity),
        "cot_gather",
        (in_target, cotangent),
        [sds((slots, width), BF), sds((1, slots), I32)],
    )
    cot_in = lax.all_to_all(cot_out, ("seq", "batch"), split_axis=0, concat_axis=0, tiled=True)
    *rest_heads, first_low, normed1, inv1, ctx_turned = call(
        chain,
        functools.partial(attend_kernel, 1, steps, pair),
        "attend_rest",
        vmem=40,
        grid=(groups - 1, steps),
        in_specs=head_specs(1)
        + [
            whole_block((rows, cols)), pl.BlockSpec((cols, width), lambda g, p, *_: (0, 0)),
            pl.BlockSpec((cols, width), lambda g, p, *_: (1 + g, 0)), vec_spec, vec_spec, vec_spec,
        ],
        out_specs=head_outs
        + [
            whole_block(bf_rows), whole_block(bf_rows), whole_block((rows, 1)),
            whole_block(turned_shape),
        ],
        out_shape=head_shapes(groups - 1)
        + [hbm(bf_rows, BF), hbm(bf_rows, BF), hbm((rows, 1), F32), hbm(turned_shape, BF)],
        scratch=[pltpu.VMEM(bf_rows, F32), pltpu.VMEM(bf_rows, BF)],
        prefetch=1,
    )(*head_args, context0, w_out, w_out, out_bias, norm1_gain, norm1_bias)
    linv_rest = rest_heads[5]

    blk = ff // 4
    act_shape = (rows, ff)
    act_col = pl.BlockSpec((rows, blk), lambda j, *_: (0, j))
    hid, slope, normed2, inv2, mixed_home, first_turned = call(
        chain,
        ffn_kernel,
        "ffn",
        vmem=36,
        grid=(4,),
        in_specs=[
            whole_block(bf_rows),
            pl.BlockSpec((width, blk), lambda j, *_: (0, j)),
            whole_block((ff,)),
            pl.BlockSpec((blk, width), lambda j, *_: (j, 0)),
            vec_spec, vec_spec, vec_spec,
        ],
        out_specs=[
            act_col, act_col, whole_block(bf_rows), whole_block((rows, 1)), whole_block(bf_rows),
            whole_block(turned_shape),
        ],
        out_shape=[
            hbm(act_shape, BF), hbm(act_shape, BF), hbm(bf_rows, BF), hbm((rows, 1), F32),
            hbm(bf_rows, BF), hbm(turned_shape, BF),
        ],
        scratch=[pltpu.VMEM(bf_rows, F32)],
        prefetch=1,
    )(ids, first_low, w_in, in_bias, w_down, down_bias, norm2_gain, norm2_bias)

    (mixed_out,) = simple(
        chain, place_kernel, "mixed_slots", (slot_row, mixed_home), [sds((slots, width), BF)],
        cost=COST,
    )
    mixed_in = lax.all_to_all(mixed_out, ("seq", "batch"), split_axis=0, concat_axis=0, tiled=True)

    def wd_spec(near):
        return pl.BlockSpec((blk, width), lambda j, ids_ref: (quarter_at(j, ids_ref, near), 0))

    g_pre2, g_branch, vec2 = simple(
        chain,
        cot_back_kernel,
        "cot_back",
        (slot_row, cot_in, normed2, inv2, norm2_gain),
        [hbm(bf_rows, F32), vmem(bf_rows, BF), sds((8, width), F32)],
        vmem=24,
        cost=COST,
    )
    act_half, bias_a, gwd_far = call(
        chain,
        down_back_kernel,
        "down_back",
        vmem=16,
        grid=(2,),
        in_specs=[
            whole_block(bf_rows), wd_spec(False), whole_block(act_shape), whole_block(act_shape),
        ],
        out_specs=[whole_block(act_shape), whole_block((1, ff)), whole_block((2, blk, width))],
        out_shape=[vmem(act_shape, BF), sds((1, ff), F32), vmem((2, blk, width), BF)],
        prefetch=1,
        free=(3, 4),
    )(ids, g_branch, w_down, slope, hid)
    gwd_mate = exchange(gwd_far, "seq", 1)
    g_act, bias_b = call(
        chain,
        act_back_kernel,
        "act_back",
        vmem=10,
        grid=(2,),
        in_specs=[
            whole_block(bf_rows), wd_spec(True), whole_block(act_shape), whole_block(act_shape),
        ],
        out_specs=[whole_block(act_shape), whole_block((1, ff))],
        out_shape=[vmem(act_shape, BF), sds((1, ff), F32)],
        prefetch=1,
        aliases={4: 0},
        free=(3,),
    )(ids, g_branch, w_down, slope, act_half)
    part = width // 4
    gwi_shape = (2 * part, ff)
    gwi_far = call(
        chain,
        functools.partial(in_grad_kernel, False),
        "in_grad_far",
        vmem=8,
        grid=(1,),
        in_specs=[whole_block(turned_shape), whole_block(act_shape)],
        out_specs=whole_block(gwi_shape),
        out_shape=vmem(gwi_shape, BF),
        prefetch=1,
        free=(1,),
    )(ids, first_turned, g_act)
    gwi_mate = exchange(gwi_far, "seq", 1)
    share_shape = (blk, width)
    send, keep = call(
        chain,
        down_grad_kernel,
        "down_grad",
        vmem=10,
        grid=(2,),
        in_specs=[whole_block(act_shape), whole_block(bf_rows), whole_block((2, blk, width))],
        out_specs=[whole_block(share_shape)] * 2,
        out_shape=[vmem(share_shape, BF)] * 2,
        prefetch=1,
        free=(1,),
    )(ids, hid, g_branch, gwd_mate)
    down_share = Share(chain, ids, "w_down", send, keep)


    in_share_shape = (2 * part, ff // 2)
    send, keep = call(
        chain,
        functools.partial(in_grad_kernel, True),
        "in_grad_near",
        vmem=8,
        grid=(1,),
        in_specs=[whole_block(turned_shape), whole_block(act_shape), whole_block(gwi_shape)],
        out_specs=[whole_block(in_share_shape)] * 2,
        out_shape=[vmem(in_share_shape, BF)] * 2,
        prefetch=1,
        free=(1,),
    )(ids, first_turned, g_act, gwi_mate)
    in_share = Share(chain, ids, "w_in", send, keep, y_first=True)

    g_pre1, g_attn, g_ctx, vec1 = call(
        chain,
        first_back_kernel,
        "first_back",
        vmem=32,
        grid=(4,),
        in_specs=[
            whole_block(bf_rows), whole_block(act_shape),
            pl.BlockSpec((width, blk), lambda j: (0, j)),
            whole_block(bf_rows), whole_block((rows, 1)), vec_spec,
            whole_block((width, width)), whole_block(linv0.shape), whole_block(linv_rest.shape),
        ],
        out_specs=[
            whole_block(bf_rows), whole_block(bf_rows), whole_block(bf_rows),
            whole_block((8, width)),
        ],
        out_shape=[hbm(bf_rows, F32), vmem(bf_rows, BF), vmem(bf_rows, BF), sds((8, width), F32)],
        scratch=[pltpu.VMEM(bf_rows, F32)],
        free=(0, 3, 6, 7, 8),
    )(g_pre2, g_act, w_in, normed1, inv1, norm1_gain, w_out, linv0, linv_rest)

    projs, vecs = [], []
    low = hbm(bf_rows, BF)

    def group_back(g):
        own_col = pl.BlockSpec((rows, 128), lambda p: (0, g * steps + p))
        arrays, base = (first_heads, 0) if g == 0 else (rest_heads, g - 1)
        head_col = pl.BlockSpec((rows, 128), lambda p: (0, base * steps + p))
        proj, vec = call(
            chain,
            functools.partial(attend_back_kernel, g * heads, pair),
            "attend_back",
            vmem=20,
            grid=(steps,),
            in_specs=[
                smem(), smem(), head_col, head_col, head_col,
                pl.BlockSpec((pair, 2, half, half), lambda p: (base * steps + p, 0, 0, 0)),
                own_col, head_col,
            ],
            out_specs=[whole_block((rows, 3 * cols)), whole_block((1, 3 * cols))],
            out_shape=[vmem((rows, 3 * cols), BF), sds((1, 3 * cols), F32)],
            scratch=[pltpu.VMEM((rows, 128), F32)] * 3,
        )(seq_lengths, head_swap, *arrays[:3], arrays[4], g_ctx, arrays[3])
        projs.append(proj)
        vecs.append(vec)

    def attention_share(pairs, vec_ins, name, y_first):
        extra = 32 if vec_ins else 0
        size = len(pairs) * part + extra
        flat = [a for both in pairs for a in both]
        scratch = [pltpu.VMEM((2 * extra, width), F32)] if extra else []
        (far_grad,) = simple(
            chain,
            functools.partial(share_grad_kernel, False, y_first, len(pairs), extra),
            name + "_far",
            (ids, *flat, *vec_ins),
            [vmem((2 * size, width), BF)],
            1,
            scratch=scratch,
        )
        mate = exchange(far_grad, "seq", 1)

        def near_part():
            shape = (2 * size, width // 2) if y_first else (size, width)
            left, right = simple(
                chain,
                functools.partial(share_grad_kernel, True, y_first, len(pairs), extra),
                name + "_near",
                (ids, *flat, *vec_ins, mate),
                [vmem(shape, BF)] * 2,
                1,
                scratch=scratch,
            )
            return Share(chain, ids, name, left, right, y_first)

        return near_part

    group_back(0)
    down_share.step_y()
    start_a = attention_share([(ctx_turned, g_attn), (x_turned, projs[0])], [], "attn_a", False)
    group_back(1)
    share_a = start_a()
    in_share.step_x()
    down_share.step_z()
    group_back(2)
    vec_ins = [vec2, bias_a, bias_b, vec1, *vecs]
    start_b = attention_share(
        [(x_turned, projs[1]), (x_turned, projs[2])], vec_ins, "attn_b", True
    )
    share_a.step_y()
    down_share.step_far()
    share_b = start_b()
    in_share.step_z()
    input_grad = call(
        chain,
        functools.partial(input_grad_kernel, groups),
        "input_grad",
        vmem=24,
        grid=(groups,),
        in_specs=[whole_block((rows, 3 * cols))] * groups
        + [
            pl.BlockSpec((width, cols), lambda g: (0, g)),
            pl.BlockSpec((width, cols), lambda g: (0, groups + g)),
            pl.BlockSpec((width, cols), lambda g: (0, 2 * groups + g)),
            whole_block((rows, width)),
        ],
        out_specs=whole_block((rows, width)),
        out_shape=low,
        scratch=[pltpu.VMEM((rows, width), F32)],
    )(*projs, w_qkv, w_qkv, w_qkv, g_pre1)
    (mixed,) = simple(
        chain, place_kernel, "mixed_place", (in_row, mixed_in), [hbm((ffn_rows, width), BF)]
    )
    share_b.step_x()
    share_a.step_z()
    in_share.step_far()
    down_share.step_back()
    share_b.step_z()
    share_a.step_far()
    in_share.step_back()
    share_b.step_far()
    down_share.step_wide()
    share_a.step_back()
    in_share.step_wide()
    share_b.step_back()
    share_a.step_wide()
    g_w_down = down_share.join()
    share_b.step_wide()
    g_w_in = in_share.join()
    one = lambda size: sds((size,), F32)
    g_w_qkv, g_w_out, g_qv, g_in_bias, g_n2g, g_n2b, g_down_bias, g_n1g, g_n1b, g_out_bias = simple(
        chain,
        functools.partial(attend_join_kernel, groups),
        "attn_join",
        (ids, *share_a.pieces, *share_b.pieces),
        [hbm((part, 3 * width), F32), hbm((part, width), F32), one(width // 2), one(width)]
        + [one(part)] * 6,
        1,
        scratch=[pltpu.VMEM(share_a.shape, F32), pltpu.VMEM(share_b.shape, F32)],
    )
    return (
        mixed, input_grad, g_w_qkv, g_qv, g_w_out, g_out_bias, g_n1g, g_n1b, g_w_in, g_in_bias,
        g_w_down, g_down_bias, g_n2g, g_n2b,
    )


def solution(mesh):
    rows_spec = P(("seq", "batch"), None)
    in_specs = (
        rows_spec, rows_spec, P(), P(("seq", "batch")), P(), P(), P(), P(), P(), P(), P(), P(),
        P(), P(), P(), P(), rows_spec,
    )
    out_specs = (
        rows_spec, rows_spec, P("seq", None), P("seq"), P("seq", None), P("seq"), P("seq"),
        P("seq"), P("seq", None), P("seq"), P("seq", None), P("seq"), P("seq"), P("seq"),
    )
    return jax.shard_map(body, mesh=mesh, in_specs=in_specs, out_specs=out_specs, check_vma=False)
```

```python
import functools

import jax
import jax.numpy as jnp
from jax import lax
from jax.experimental import pallas as pl
from jax.experimental.pallas import tpu as pltpu
from jax.sharding import PartitionSpec as P

EPS = 1e-05
BIG = 1e30
BF = jnp.bfloat16
F32 = jnp.float32
I32 = jnp.int32
MIB = 1 << 20
COST = 5e10
COST_MID = 2e10
COST_SMALL = 1e10
COST_TINY = 1e9

NN = (((1,), (0,)), ((), ()))
NT = (((1,), (1,)), ((), ()))
TN = (((0,), (0,)), ((), ()))


def mm(left_op, right_op, dims):
    return lax.dot_general(left_op, right_op, dims, preferred_element_type=F32)


def sds(shape, dtype):
    return jax.ShapeDtypeStruct(shape, dtype)


def hbm(shape, dtype):
    return pltpu.HBM(shape, dtype)


def vmem(shape, dtype):
    return pltpu.VMEM(shape, dtype)


def whole_block(shape):
    zeros = (0,) * len(shape)
    return pl.BlockSpec(shape, lambda *_: zeros)


def smem():
    return pl.BlockSpec(memory_space=pltpu.SMEM)


class Chain:
    def __init__(self):
        self.last = None
        self.spaces = {}

    def link(self, outs, shapes):
        flat = jax.tree.leaves(outs)
        self.last = min(flat, key=lambda a: a.size * a.dtype.itemsize)
        for out, shape in zip(flat, shapes if isinstance(shapes, (list, tuple)) else [shapes]):
            if getattr(shape, "memory_space", None) in (pltpu.HBM, pltpu.VMEM):
                self.keep(shape.memory_space, out)

    def keep(self, space, *arrays):
        for array in arrays:
            self.spaces[id(array)] = (space, array)

    def place(self, array):
        if id(array) in self.spaces:
            return pltpu.with_memory_space_constraint(array, self.spaces[id(array)][0])
        return array


def call(chain, body, name, *, grid, in_specs, out_specs, out_shape, scratch=(), prefetch=0,
         aliases=None, vmem=56, cost=COST, free=()):
    count = prefetch + len(in_specs)
    before = [] if chain.last is None else [chain.last]

    def ordered(*refs):
        body(*refs[:count], *refs[count + len(before) :])

    kernel = pl.pallas_call(
        ordered,
        name=name,
        grid_spec=pltpu.PrefetchScalarGridSpec(
            num_scalar_prefetch=prefetch,
            grid=grid,
            in_specs=list(in_specs) + [pl.BlockSpec(memory_space=pl.ANY)] * len(before),
            out_specs=out_specs,
            scratch_shapes=list(scratch),
        ),
        out_shape=out_shape,
        input_output_aliases=aliases or {},
        compiler_params=pltpu.CompilerParams(
            vmem_limit_bytes=vmem * MIB, dimension_semantics=("arbitrary",) * len(grid)
        ),
        cost_estimate=pl.CostEstimate(flops=int(cost), bytes_accessed=1, transcendentals=0),
    )

    def run(*args):
        placed = [a if at in free else chain.place(a) for at, a in enumerate(args)]
        outs = kernel(*placed, *[chain.place(a) for a in before])
        chain.link(outs, out_shape)
        return outs

    return run


def floor_div(values, divisor):
    return jnp.floor((values.astype(F32) + 0.5) * (1.0 / divisor)).astype(I32)


def route_kernel(ffn_rows, capacity, place_ref, slot_ref, target_ref):
    devices = target_ref.shape[0]
    rows = place_ref.shape[1]
    place = place_ref[...]
    live = place >= 0
    dev = jnp.where(live, floor_div(place, ffn_rows), -1)
    local = place - dev * ffn_rows
    hit = lax.broadcasted_iota(I32, (devices, rows), 0) == dev
    onehot = hit.astype(F32)
    upper = (
        lax.broadcasted_iota(I32, (rows, rows), 0) <= lax.broadcasted_iota(I32, (rows, rows), 1)
    ).astype(F32).astype(BF)
    running = mm(onehot.astype(BF), upper, NN)
    rank = (jnp.sum(running * onehot, axis=0, keepdims=True) - 1.0).astype(I32)
    slot_ref[...] = jnp.where(live, dev * capacity + rank, devices * capacity)
    ranked = (lax.broadcasted_iota(I32, (capacity, rows), 0) == rank).astype(F32).astype(BF)
    high = (local >> 5).astype(F32)
    low = (local & 31).astype(F32)
    filled = mm(onehot.astype(BF), ranked, NT)
    high_at = mm((onehot * high).astype(BF), ranked, NT)
    low_at = mm((onehot * low).astype(BF), ranked, NT)
    target = (high_at * 32.0 + low_at).astype(I32)
    target_ref[...] = jnp.where(filled > 0.5, target, ffn_rows)


def expand_targets(target, capacity):
    devices = target.shape[0]
    slots = devices * capacity
    lane = lax.broadcasted_iota(I32, (capacity, slots), 1)
    lane_dev = floor_div(lane, capacity)
    spread = ((lane - lane_dev * capacity) == lax.broadcasted_iota(I32, (capacity, slots), 0)).astype(
        F32
    ).astype(BF)
    high = mm((target >> 5).astype(F32).astype(BF), spread, NN)
    low = mm((target & 31).astype(F32).astype(BF), spread, NN)
    wide = high * 32.0 + low
    own_dev = floor_div(lax.broadcasted_iota(I32, (devices, slots), 1), capacity)
    own = own_dev == lax.broadcasted_iota(I32, (devices, slots), 0)
    return jnp.sum(jnp.where(own, wide, 0.0), axis=0, keepdims=True).astype(I32)


def onehot_rows(row_index, row_count):
    lanes = row_index.shape[1]
    return (lax.broadcasted_iota(I32, (row_count, lanes), 0) == row_index).astype(F32).astype(BF)


def onehot_cols(row_index, col_count):
    rows = row_index.shape[1]
    column = jnp.broadcast_to(row_index.astype(F32), (128, rows)).T[:, :1].astype(I32)
    return (lax.broadcasted_iota(I32, (rows, col_count), 1) == column).astype(F32).astype(BF)


def gather_kernel(capacity, target_ref, cot_ref, out_ref, row_ref):
    row = expand_targets(target_ref[...], capacity)
    row_ref[...] = row
    chosen = onehot_cols(row, cot_ref.shape[0])
    out_ref[...] = mm(chosen, cot_ref[...], NN).astype(BF)


def place_kernel(row_ref, in_ref, out_ref):
    chosen = onehot_rows(row_ref[...], out_ref.shape[0])
    out_ref[...] = mm(chosen, in_ref[...], NN).astype(BF)


def norm_rows(values):
    center = values - jnp.mean(values, axis=-1, keepdims=True)
    inverse = lax.rsqrt(jnp.mean(center * center, axis=-1, keepdims=True) + EPS)
    return center * inverse, inverse


def project(x_ref, w_refs, bq, bv, outs):
    x = x_ref[...]
    wq_ref, wk_ref, wv_ref = w_refs
    q_ref, k_ref, v_ref = outs
    q_ref[...] = (mm(x, wq_ref[...], NN) + bq).astype(BF)
    k_ref[...] = mm(x, wk_ref[...], NN).astype(BF)
    v_ref[...] = (mm(x, wv_ref[...], NN) + bv).astype(BF)


def attend_pair(
    head_base, heads, len_ref, swap_ref, q_ref, k_ref, v_ref, cut, ctx_ref, soft_ref, linv_ref
):
    rows = q_ref.shape[0]
    half = rows // 2
    quarter = rows // 4
    head_size = 128 // heads
    scale = head_size ** (-0.5)
    len0, len1 = len_ref[0, 0], len_ref[0, 1]
    is_long = len1 == 0
    lane = lax.broadcasted_iota(I32, (1, 128), 1)
    row = lax.broadcasted_iota(I32, (half, 1), 0)
    row_quarter = (row >= quarter).astype(I32)
    for b in range(2):
        q_rows = slice(b * half, (b + 1) * half)
        q_blk = q_ref[q_rows, cut].astype(F32) * scale
        out_blk = linv_blk = None
        for sub in range(heads):
            swapped = swap_ref[head_base + sub] == 1
            cross = jnp.logical_and(is_long, swapped)
            kb = jnp.where(cross, 1 - b, b)
            limit = jnp.where(is_long, len0 - kb * half, jnp.where(kb == 0, len0, len1))
            mine = jnp.logical_and(lane >= sub * head_size, lane < (sub + 1) * head_size)
            spare = ((sub + 1) % heads) * head_size
            key_rows = pl.ds(pl.multiple_of(kb * half, half), half)
            k_one = jnp.where(mine, k_ref[key_rows, cut].astype(F32), 0.0)
            q_one = jnp.where(mine, q_blk, 0.0)
            for part in range(2):
                other = jnp.where(swapped, 1 - part, part)
                band_ok = jnp.logical_or(is_long, row_quarter == other)
                bias = jnp.where(jnp.logical_and(band_ok, row < limit), 0.0, -BIG)
                at = lane == spare + part
                k_one = jnp.where(at, bias, k_one)
                q_one = jnp.where(at, jnp.where(row_quarter == part, 1.0, 0.0), q_one)
            scores = mm(q_one.astype(BF), k_one.astype(BF), NT)
            top = jnp.max(scores, axis=1, keepdims=True)
            weights = jnp.exp(scores - top)
            linv = 1.0 / jnp.sum(weights, axis=1, keepdims=True)
            soft = weights.astype(BF)
            soft_ref[sub, b] = soft
            mixed = mm(soft, v_ref[key_rows, cut], NN) * linv
            out_blk = mixed if out_blk is None else jnp.where(mine, mixed, out_blk)
            linv_blk = (
                jnp.broadcast_to(linv, mixed.shape)
                if linv_blk is None
                else jnp.where(mine, linv, linv_blk)
            )
        ctx_ref[q_rows, :] = out_blk.astype(BF)
        linv_ref[q_rows, :] = linv_blk


def attend_kernel(
    first, pairs, heads, len_ref, swap_ref, x_ref, wq_ref, wk_ref, wv_ref, b_ref, *refs
):
    if first == 0:
        q_ref, k_ref, v_ref, ctx_ref, soft_ref, linv_ref = refs
    else:
        (
            ctx0_ref, wo0_ref, wo_ref, ob_ref, gain_ref, shift_ref,
            q_ref, k_ref, v_ref, soft_ref, linv_ref, first_ref, normed_ref, inv_ref, ctx_all,
            acc_ref,
        ) = refs
    cols = q_ref.shape[1]
    width = x_ref.shape[1]
    group = first + pl.program_id(0)
    pair = pl.program_id(1)

    @pl.when(pair == 0)
    def _():
        bq = b_ref[pl.ds(pl.multiple_of(group * cols, cols), cols)].reshape(1, -1)
        bv = b_ref[pl.ds(pl.multiple_of(width + group * cols, cols), cols)].reshape(1, -1)
        project(x_ref, (wq_ref, wk_ref, wv_ref), bq, bv, (q_ref, k_ref, v_ref))

    cut = pl.ds(pl.multiple_of(pair * 128, 128), 128)
    if first > 0:
        ctx_ref = ctx_all.at[:, pl.ds(pl.multiple_of(group * cols + pair * 128, 128), 128)]
    attend_pair(
        group * (pairs * heads) + pair * heads, heads, len_ref, swap_ref, q_ref, k_ref, v_ref, cut,
        ctx_ref, soft_ref, linv_ref,
    )
    if first == 0:
        return

    @pl.when(pair == pairs - 1)
    def _():
        own = pl.ds(pl.multiple_of(group * cols, cols), cols)
        part_sum = mm(ctx_all[:, own], wo_ref[...], NN)

        @pl.when(group == first)
        def _():
            ctx_all[:, :cols] = ctx0_ref[...]
            acc_ref[...] = part_sum + mm(ctx0_ref[...], wo0_ref[...], NN)

        @pl.when(group > first)
        def _():
            acc_ref[...] += part_sum

        @pl.when(pl.program_id(0) == pl.num_programs(0) - 1)
        def _():
            attn = acc_ref[...] + ob_ref[...].reshape(1, -1)
            normed, inverse = norm_rows(x_ref[...].astype(F32) + attn)
            normed_ref[...] = normed.astype(BF)
            inv_ref[...] = inverse
            out = normed * gain_ref[...].reshape(1, -1) + shift_ref[...].reshape(1, -1)
            first_ref[...] = out.astype(BF)


def block_cols(index, size):
    return pl.ds(pl.multiple_of(index * size, size), size)


def ffn_kernel(
    x_ref, wi_ref, bi_ref, wd_ref, bd_ref, gain_ref, shift_ref,
    hid_ref, slope_ref, normed_ref, inv_ref, out_ref, acc_ref,
):
    step = pl.program_id(0)
    steps = pl.num_programs(0)
    x = x_ref[...]
    own = block_cols(step, wi_ref.shape[1])
    pre = mm(x, wi_ref[...], NN) + bi_ref[own].reshape(1, -1)
    phi = 0.5 * (1.0 + lax.erf(pre * 0.7071067811865476))
    hid = (pre * phi).astype(BF)
    hid_ref[...] = hid
    slope_ref[...] = (phi + pre * jnp.exp(-0.5 * pre * pre) * 0.3989422804014327).astype(BF)
    part_sum = mm(hid, wd_ref[...], NN)

    @pl.when(step == 0)
    def _():
        acc_ref[...] = part_sum

    @pl.when(step > 0)
    def _():
        acc_ref[...] += part_sum

    @pl.when(step == steps - 1)
    def _():
        branch = acc_ref[...] + bd_ref[...].reshape(1, -1)
        normed, inverse = norm_rows(x_ref[...].astype(F32) + branch)
        normed_ref[...] = normed.astype(BF)
        inv_ref[...] = inverse
        out = normed * gain_ref[...].reshape(1, -1) + shift_ref[...].reshape(1, -1)
        out_ref[...] = out.astype(BF)


def norm_back(upstream, normed, inverse, gain):
    scaled = upstream * gain
    inner = (
        scaled
        - jnp.mean(scaled, axis=-1, keepdims=True)
        - normed * jnp.mean(scaled * normed, axis=-1, keepdims=True)
    )
    return inner * inverse


def put_rows(ref, *rows):
    for at, row in enumerate(rows):
        ref[at : at + 1, :] = row


def store_halves(ids_ref, total, mine_ref, other_ref):
    half = mine_ref.shape[1]
    second = (ids_ref[1] & 1) == 1
    left, right = total[:, :half], total[:, half:]
    mine_ref[...] = jnp.where(second, right, left)
    other_ref[...] = jnp.where(second, left, right)


def quarter_at(step, ids_ref):
    rel = jnp.where(step == 0, 3, jnp.where(step == 3, 0, step))
    return jnp.bitwise_xor(ids_ref[0], rel)


def store_quarters(ids_ref, grad, far_ref, near_ref, base, size, cols=slice(None)):
    part = grad.shape[0] // 4
    for q in range(4):
        rel = jnp.bitwise_xor(ids_ref[0], q)
        value = grad[q * part : (q + 1) * part]
        rows = pl.ds(pl.multiple_of(jnp.where(rel < 2, size, 0) + base, 16), part)

        @pl.when((rel & 1) == 1)
        def _():
            far_ref[rows, cols] = value

        @pl.when((rel & 1) == 0)
        def _():
            near_ref[rows, cols] = value


def cot_back_kernel(
    slot_ref, in_ref, normed_ref, inv_ref, gain_ref, pre_ref, branch_ref, vec_ref
):
    chosen = onehot_cols(slot_ref[...], in_ref.shape[0])
    cot = mm(chosen, in_ref[...], NN)
    normed = normed_ref[...].astype(F32)
    g_pre = norm_back(cot, normed, inv_ref[...], gain_ref[...].reshape(1, -1))
    pre_ref[...] = g_pre
    branch = g_pre.astype(BF)
    branch_ref[...] = branch
    put_rows(
        vec_ref,
        jnp.sum(cot * normed, axis=0, keepdims=True),
        jnp.sum(cot, axis=0, keepdims=True),
        jnp.sum(branch.astype(F32), axis=0, keepdims=True),
    )


def down_back_kernel(
    ids_ref, branch_ref, wd_ref, slope_ref, hid_ref, act_ref, bias_ref, far_ref, near_ref
):
    step = pl.program_id(0)
    branch = branch_ref[...]
    own = block_cols(quarter_at(step, ids_ref), wd_ref.shape[0])
    g_act = (mm(branch, wd_ref[...], NT) * slope_ref[...].astype(F32)).astype(BF)
    act_ref[:, own] = g_act
    bias_ref[:, own] = jnp.sum(g_act.astype(F32), axis=0, keepdims=True)
    grad = mm(hid_ref[...], branch, TN).astype(BF)

    @pl.when(step < 2)
    def _():
        far_ref[step] = grad

    @pl.when(step >= 2)
    def _():
        near_ref[step - 2] = grad


def down_add_kernel(near_ref, mate_ref, send_ref, keep_ref):
    for at, out_ref in enumerate((send_ref, keep_ref)):
        out_ref[...] = (near_ref[at].astype(F32) + mate_ref[at].astype(F32)).astype(BF)


def in_back_kernel(ids_ref, x_ref, act_ref, far_ref, near_ref):
    blk = x_ref.shape[1]
    own = block_cols(pl.program_id(0), blk)
    grad = mm(x_ref[...], act_ref[:, own], TN).astype(BF)
    store_quarters(ids_ref, grad, far_ref, near_ref, 0, blk // 4, own)


def in_add_kernel(ids_ref, near_ref, mate_ref, mine_ref, other_ref):
    total = (near_ref[...].astype(F32) + mate_ref[...].astype(F32)).astype(BF)
    store_halves(ids_ref, total, mine_ref, other_ref)


def first_back_kernel(
    pre2_ref, act_ref, wi_ref, normed_ref, inv_ref, gain_ref, wo_ref, linv0_ref, linv_ref,
    pre1_ref, gattn_ref, gctx_ref, vec_ref, acc_ref,
):
    step = pl.program_id(0)
    part_sum = mm(act_ref[:, block_cols(step, wi_ref.shape[1])], wi_ref[...], NT)

    @pl.when(step == 0)
    def _():
        acc_ref[...] = part_sum

    @pl.when(step > 0)
    def _():
        acc_ref[...] += part_sum

    @pl.when(step == pl.num_programs(0) - 1)
    def _():
        g_first = (pre2_ref[...] + acc_ref[...]).astype(BF).astype(F32)
        normed = normed_ref[...].astype(F32)
        g_pre = norm_back(g_first, normed, inv_ref[...], gain_ref[...].reshape(1, -1))
        pre1_ref[...] = g_pre
        g_attn = g_pre.astype(BF)
        put_rows(
            vec_ref,
            jnp.sum(g_first * normed, axis=0, keepdims=True),
            jnp.sum(g_first, axis=0, keepdims=True),
            jnp.sum(g_attn.astype(F32), axis=0, keepdims=True),
        )
        g_ctx = mm(g_attn, wo_ref[...], NT)
        cols = linv0_ref.shape[1]
        gctx_ref[:, :cols] = (g_ctx[:, :cols] * linv0_ref[...]).astype(BF)
        gctx_ref[:, cols:] = (g_ctx[:, cols:] * linv_ref[...]).astype(BF)
        gattn_ref[...] = g_attn


def attend_back_kernel(
    head_base, heads, len_ref, swap_ref, q_ref, k_ref, v_ref, soft_ref, gctx_ref, ctx_ref,
    proj_ref, vec_ref, gq_s, gk_s, gv_s,
):
    step = pl.program_id(0)
    rows = q_ref.shape[0]
    half = rows // 2
    head_size = 128 // heads
    scale = head_size ** (-0.5)
    is_long = len_ref[0, 1] == 0
    lane = lax.broadcasted_iota(I32, (1, 128), 1)
    for sub in range(heads):
        swapped = swap_ref[head_base + step * heads + sub] == 1
        cross = jnp.logical_and(is_long, swapped)
        mine = jnp.logical_and(lane >= sub * head_size, lane < (sub + 1) * head_size)
        for b in range(2):
            q_rows = slice(b * half, (b + 1) * half)
            kb = jnp.where(cross, 1 - b, b)
            key_rows = pl.ds(pl.multiple_of(kb * half, half), half)
            soft = soft_ref[sub, b]
            up = gctx_ref[q_rows, :]
            up_one = jnp.where(mine, up, jnp.zeros_like(up))
            inner = jnp.sum(
                up_one.astype(F32) * ctx_ref[q_rows, :].astype(F32), axis=1, keepdims=True
            )
            g_soft = mm(up_one, v_ref[key_rows, :], NT)
            g_scores = (soft.astype(F32) * (g_soft - inner)).astype(BF)
            g_q = mm(g_scores, k_ref[key_rows, :], NN) * scale
            g_k = mm(g_scores, q_ref[q_rows, :], TN) * scale
            g_v = mm(soft, up, TN)
            if sub == 0:
                gq_s[q_rows, :] = g_q
                gk_s[key_rows, :] = g_k
                gv_s[key_rows, :] = g_v
            else:
                gq_s[q_rows, :] = jnp.where(mine, g_q, gq_s[q_rows, :])
                gk_s[key_rows, :] = jnp.where(mine, g_k, gk_s[key_rows, :])
                gv_s[key_rows, :] = jnp.where(mine, g_v, gv_s[key_rows, :])
    cols = proj_ref.shape[1] // 3
    for at, ref in enumerate((gq_s, gk_s, gv_s)):
        low = ref[...].astype(BF)
        out_cols = pl.ds(pl.multiple_of(at * cols + step * 128, 128), 128)
        proj_ref[:, out_cols] = low
        vec_ref[:, out_cols] = jnp.sum(low.astype(F32), axis=0, keepdims=True)


def input_grad_kernel(groups, *refs):
    proj_refs, (wq_ref, wk_ref, wv_ref, pre_ref, out_ref, acc_ref) = refs[:groups], refs[groups:]
    step = pl.program_id(0)
    cols = wq_ref.shape[1]

    @pl.when(step == 0)
    def _():
        acc_ref[...] = pre_ref[...]

    for at, proj_ref in enumerate(proj_refs):

        @pl.when(step == at)
        def _():
            acc_ref[...] += (
                mm(proj_ref[:, :cols], wq_ref[...], NT)
                + mm(proj_ref[:, cols : 2 * cols], wk_ref[...], NT)
                + mm(proj_ref[:, 2 * cols :], wv_ref[...], NT)
            )

    @pl.when(step == groups - 1)
    def _():
        out_ref[...] = acc_ref[...].astype(BF)


def store_vectors(ids_ref, vec_refs, far_ref, near_ref, base, size):
    vec2_ref, bias_ref, vec1_ref, *qkv_refs = vec_refs
    width = vec1_ref.shape[1]
    cols = width // len(qkv_refs)
    part = width // 4
    wide = jnp.concatenate(
        [ref[:, :cols] for ref in qkv_refs] + [ref[:, 2 * cols :] for ref in qkv_refs], axis=1
    )
    extra = size - base
    for q in range(4):
        rel = jnp.bitwise_xor(ids_ref[0], q)
        rows = [bias_ref[:, q * width : (q + 1) * width]]
        rows.append(wide[:, q * (width // 2) : (q + 1) * (width // 2)])
        for ref in (vec2_ref, vec1_ref):
            rows += [ref[at : at + 1, q * part : (q + 1) * part] for at in range(3)]
        rows = [jnp.pad(row, ((0, 0), (0, width - row.shape[1]))) for row in rows]
        rows.append(jnp.zeros((extra - len(rows), width), F32))
        block = jnp.concatenate(rows, axis=0).astype(BF)
        at = pl.ds(pl.multiple_of(jnp.where(rel < 2, size, 0) + base, 16), extra)

        @pl.when((rel & 1) == 1)
        def _():
            far_ref[at, :] = block

        @pl.when((rel & 1) == 0)
        def _():
            near_ref[at, :] = block


def share_grad_kernel(count, extra, ids_ref, *refs):
    pairs = [(refs[2 * at], refs[2 * at + 1]) for at in range(count)]
    *vec_refs, far_ref, near_ref = refs[2 * count :]
    part = pairs[0][0].shape[1] // 4
    size = count * part + extra
    for at, (left_ref, right_ref) in enumerate(pairs):
        grad = mm(left_ref[...], right_ref[...], TN).astype(BF)
        store_quarters(ids_ref, grad, far_ref, near_ref, at * part, size)
    if extra:
        store_vectors(ids_ref, vec_refs, far_ref, near_ref, count * part, size)


def share_add_kernel(near_ref, mate_ref, send_ref, keep_ref):
    size = send_ref.shape[0]
    total = (near_ref[...].astype(F32) + mate_ref[...].astype(F32)).astype(BF)
    send_ref[...] = total[:size]
    keep_ref[...] = total[size:]


def split_cols_kernel(ids_ref, keep_ref, got_ref, mine_ref, other_ref):
    total = (keep_ref[...].astype(F32) + got_ref[...].astype(F32)).astype(BF)
    store_halves(ids_ref, total, mine_ref, other_ref)


def split_shares_kernel(mine_ref, got_ref, send_ref, keep_ref):
    total = (mine_ref[...].astype(F32) + got_ref[...].astype(F32)).astype(BF)
    rows = send_ref.shape[0]
    send_ref[...] = total[:rows]
    keep_ref[...] = total[rows:]


def split_rows_kernel(ids_ref, keep_ref, got_ref, mine_ref, other_ref):
    half = mine_ref.shape[0]
    bit = (ids_ref[1] >> 1) & 1

    def part(at):
        rows = pl.ds(pl.multiple_of(at * half, half), half)
        return (keep_ref[rows, :].astype(F32) + got_ref[rows, :].astype(F32)).astype(BF)

    mine_ref[...] = part(bit)
    other_ref[...] = part(1 - bit)


def add_kernel(left_ref, right_ref, out_ref):
    out_ref[...] = (left_ref[...].astype(F32) + right_ref[...].astype(F32)).astype(BF)


def join_kernel(ids_ref, own_ref, near_ref, far_own_ref, far_near_ref, out_ref):
    half_rows, half_cols = own_ref.shape
    second = (ids_ref[1] & 1) == 1
    bit = (ids_ref[1] >> 1) & 1
    for rel, (mine, other) in enumerate(((own_ref, far_own_ref), (near_ref, far_near_ref))):
        at = jnp.bitwise_xor(bit, rel)
        rows = pl.ds(pl.multiple_of(at * half_rows, half_rows), half_rows)
        a, b = mine[...].astype(F32), other[...].astype(F32)
        out_ref[rows, :half_cols] = jnp.where(second, b, a)
        out_ref[rows, half_cols:] = jnp.where(second, a, b)


def stack_kernel(ids_ref, own_ref, near_ref, out_ref):
    half = own_ref.shape[0]
    bit = (ids_ref[1] >> 1) & 1
    for rel, ref in enumerate((own_ref, near_ref)):
        at = jnp.bitwise_xor(bit, rel)
        out_ref[pl.ds(pl.multiple_of(at * half, half), half), :] = ref[...]


def join_into(ids_ref, mine_ref, other_ref, out_ref):
    half = mine_ref.shape[1]
    second = (ids_ref[1] & 1) == 1
    a, b = mine_ref[...].astype(F32), other_ref[...].astype(F32)
    out_ref[:, :half] = jnp.where(second, b, a)
    out_ref[:, half:] = jnp.where(second, a, b)


def join_kernel(ids_ref, mine_ref, other_ref, out_ref):
    join_into(ids_ref, mine_ref, other_ref, out_ref)


def attend_join_kernel(groups, ids_ref, *refs):
    a_refs, b_refs = refs[:2], refs[2:4]
    gwq_ref, gwo_ref, qv_ref, hid_ref = refs[4:8]
    vec_refs, (a_all, b_all) = refs[8:14], refs[14:]
    join_into(ids_ref, *a_refs, a_all)
    join_into(ids_ref, *b_refs, b_all)
    part, width = gwo_ref.shape
    cols = width // groups
    gwo_ref[...] = a_all[:part, :]
    places = [(a_all, part)] + [(b_all, part * at) for at in range(groups - 1)]
    for g, (ref, base) in enumerate(places):
        for at in range(3):
            gwq_ref[:, at * width + g * cols : at * width + (g + 1) * cols] = ref[
                base : base + part, at * cols : (at + 1) * cols
            ]
    base = part * (groups - 1)
    hid_ref[...] = b_all[base, :]
    qv_ref[...] = b_all[base + 1, : qv_ref.shape[0]]
    for at, ref in enumerate(vec_refs):
        ref[...] = b_all[base + 2 + at, : ref.shape[0]]


def exchange(values, axis, mask):
    count = lax.axis_size(axis)
    return lax.ppermute(values, axis, [(i, i ^ mask) for i in range(count)])


def simple(chain, body, name, args, out_shape, prefetch=0, vmem=12, scratch=(), cost=COST_SMALL, free=()):
    tensors = args[prefetch:]
    return call(
        chain,
        body,
        name,
        grid=(1,),
        in_specs=[whole_block(a.shape) for a in tensors],
        out_specs=[whole_block(o.shape) for o in out_shape],
        out_shape=out_shape,
        prefetch=prefetch,
        vmem=vmem,
        cost=cost,
        free=free,
        scratch=scratch,
    )(*args)


class Share:
    def __init__(self, chain, ids, name, left, right, y_first=False):
        self.chain, self.ids, self.name = chain, ids, name
        if y_first:
            self.keep, self.got = left, exchange(right, "batch", 1)
            self.shape = (left.shape[0] // 2, left.shape[1] * 2)
        else:
            self.keep, self.got = right, exchange(left, "seq", 2)
            self.shape = right.shape

    def step_x(self):
        rows, cols = self.shape
        send, self.keep = simple(
            self.chain, split_shares_kernel, self.name + "_x", (self.keep, self.got),
            [vmem((rows, cols // 2), BF)] * 2,
        )
        self.got = exchange(send, "seq", 2)

    def halve(self, kernel, shape, label, mask, cost=COST_SMALL):
        self.keep, other = simple(
            self.chain, kernel, self.name + label, (self.ids, self.keep, self.got),
            [vmem(shape, BF)] * 2, 1, cost=cost,
        )
        self.got = exchange(other, "batch", mask)

    def step_y(self):
        rows, cols = self.shape
        self.halve(split_cols_kernel, (rows, cols // 2), "_y", 1)

    def step_z(self, cost=COST_SMALL):
        rows, cols = self.shape
        self.halve(split_rows_kernel, (rows // 2, cols // 2), "_z", 2, cost)

    def add(self, label, cost=COST_SMALL):
        (self.keep,) = simple(
            self.chain, add_kernel, self.name + label, (self.keep, self.got),
            [vmem(self.keep.shape, BF)], cost=cost,
        )

    def step_far(self, cost=COST_SMALL):
        mask = 4
        while mask <= lax.axis_size("batch") // 2:
            self.add("_a", cost)
            self.got = exchange(self.keep, "batch", mask)
            mask *= 2

    def step_back(self):
        self.add("_f")
        self.got = exchange(self.keep, "batch", 2)

    def step_wide(self):
        rows, cols = self.shape
        (self.keep,) = simple(
            self.chain, stack_kernel, self.name + "_g", (self.ids, self.keep, self.got),
            [vmem((rows, cols // 2), BF)], 1,
        )
        self.pieces = (self.keep, exchange(self.keep, "batch", 1))

    def join(self):
        (whole,) = simple(
            self.chain, join_kernel, self.name + "_j", (self.ids, *self.pieces),
            [hbm(self.shape, F32)], 1,
        )
        return whole


def body(
    hidden_in, seq_lengths, head_swap, place, w_qkv, qv_bias, w_out, out_bias, norm1_gain,
    norm1_bias, w_in, in_bias, w_down, down_bias, norm2_gain, norm2_bias, cotangent,
):
    rows, width = hidden_in.shape
    ff = w_in.shape[1]
    ffn_rows = cotangent.shape[0]
    devices = lax.axis_size(("seq", "batch"))
    capacity = (rows + devices - 1) // devices
    slots = devices * capacity
    head_count = head_swap.shape[0]
    head_size = width // head_count
    half = rows // 2
    cols = 256
    groups = width // cols
    heads = cols // head_size
    pair = 128 // head_size
    ids = jnp.stack([lax.axis_index("seq"), lax.axis_index("batch")]).astype(I32)
    chain = Chain()
    chain.keep(pltpu.HBM, hidden_in, w_qkv, w_out, w_in, w_down, cotangent)

    slot_row, out_target = simple(
        chain,
        functools.partial(route_kernel, ffn_rows, capacity),
        "route",
        (place.reshape(1, -1),),
        [sds((1, rows), I32), sds((devices, capacity), I32)],
    )
    in_target = lax.all_to_all(out_target, ("seq", "batch"), split_axis=0, concat_axis=0, tiled=True)

    bf_rows = (rows, width)
    vec_spec = whole_block((width,))
    steps = heads // pair
    some = lambda count, dtype: hbm((rows, count * cols), dtype)
    col = lambda base: pl.BlockSpec((width, cols), lambda g, p, *_: (0, base + g))
    out_col = pl.BlockSpec((rows, cols), lambda g, p, *_: (0, g))
    pair_out = pl.BlockSpec((rows, 128), lambda g, p, *_: (0, g * steps + p))
    soft_spec = pl.BlockSpec((pair, 2, half, half), lambda g, p, *_: (g * steps + p, 0, 0, 0))
    head_outs = [out_col] * 3 + [pair_out, soft_spec, pair_out]
    head_shapes = lambda count: [some(count, BF)] * 4 + [
        hbm((count * heads, 2, half, half), BF), some(count, F32)
    ]
    head_args = (seq_lengths, head_swap, hidden_in, w_qkv, w_qkv, w_qkv, qv_bias)
    head_specs = lambda first: [
        smem(), smem(), whole_block(bf_rows), col(first), col(groups + first),
        col(2 * groups + first), whole_block((2 * width,)),
    ]
    first_heads = call(
        chain,
        functools.partial(attend_kernel, 0, steps, pair),
        "attend_first",
        vmem=32,
        grid=(1, steps),
        in_specs=head_specs(0),
        out_specs=head_outs,
        out_shape=head_shapes(1),
    )(*head_args)
    context0, linv0 = first_heads[3], first_heads[5]
    cot_out, in_row = simple(
        chain,
        functools.partial(gather_kernel, capacity),
        "cot_gather",
        (in_target, cotangent),
        [sds((slots, width), BF), sds((1, slots), I32)],
    )
    cot_in = lax.all_to_all(cot_out, ("seq", "batch"), split_axis=0, concat_axis=0, tiled=True)
    *rest_heads, first_low, normed1, inv1, context = call(
        chain,
        functools.partial(attend_kernel, 1, steps, pair),
        "attend_rest",
        vmem=40,
        grid=(groups - 1, steps),
        in_specs=head_specs(1)
        + [
            whole_block((rows, cols)), pl.BlockSpec((cols, width), lambda g, p, *_: (0, 0)),
            pl.BlockSpec((cols, width), lambda g, p, *_: (1 + g, 0)), vec_spec, vec_spec, vec_spec,
        ],
        out_specs=head_outs[:3] + head_outs[4:]
        + [whole_block(bf_rows), whole_block(bf_rows), whole_block((rows, 1)), whole_block(bf_rows)],
        out_shape=head_shapes(groups - 1)[:3] + head_shapes(groups - 1)[4:]
        + [hbm(bf_rows, BF), hbm(bf_rows, BF), hbm((rows, 1), F32), hbm(bf_rows, BF)],
        scratch=[pltpu.VMEM(bf_rows, F32)],
    )(*head_args, context0, w_out, w_out, out_bias, norm1_gain, norm1_bias)
    linv_rest = rest_heads[4]

    blk = ff // 4
    act_shape = (rows, ff)
    act_col = pl.BlockSpec((rows, blk), lambda j, *_: (0, j))
    hid, slope, normed2, inv2, mixed_home = call(
        chain,
        ffn_kernel,
        "ffn",
        vmem=36,
        grid=(4,),
        in_specs=[
            whole_block(bf_rows),
            pl.BlockSpec((width, blk), lambda j, *_: (0, j)),
            whole_block((ff,)),
            pl.BlockSpec((blk, width), lambda j, *_: (j, 0)),
            vec_spec, vec_spec, vec_spec,
        ],
        out_specs=[
            act_col, act_col, whole_block(bf_rows), whole_block((rows, 1)), whole_block(bf_rows),
        ],
        out_shape=[
            hbm(act_shape, BF), hbm(act_shape, BF), hbm(bf_rows, BF), hbm((rows, 1), F32),
            hbm(bf_rows, BF),
        ],
        scratch=[pltpu.VMEM(bf_rows, F32)],
    )(first_low, w_in, in_bias, w_down, down_bias, norm2_gain, norm2_bias)

    (mixed_out,) = simple(
        chain, place_kernel, "mixed_slots", (slot_row, mixed_home), [sds((slots, width), BF)],
        cost=COST,
    )
    mixed_in = lax.all_to_all(mixed_out, ("seq", "batch"), split_axis=0, concat_axis=0, tiled=True)

    g_pre2, g_branch, vec2 = simple(
        chain,
        cot_back_kernel,
        "cot_back",
        (slot_row, cot_in, normed2, inv2, norm2_gain),
        [hbm(bf_rows, F32), vmem(bf_rows, BF), sds((8, width), F32)],
        vmem=24,
        cost=COST,
    )
    part = width // 4
    quarter_rows = pl.BlockSpec((blk, width), lambda j, i: (quarter_at(j, i), 0))
    quarter_cols = pl.BlockSpec((rows, blk), lambda j, i: (0, quarter_at(j, i)))
    down_shape = (2, blk, width)
    g_act, bias_row, gwd_far, gwd_near = call(
        chain,
        down_back_kernel,
        "down_back",
        vmem=24,
        grid=(4,),
        in_specs=[whole_block(bf_rows), quarter_rows, quarter_cols, quarter_cols],
        out_specs=[
            whole_block(act_shape), whole_block((1, ff)), whole_block(down_shape),
            whole_block(down_shape),
        ],
        out_shape=[
            vmem(act_shape, BF), sds((1, ff), F32), vmem(down_shape, BF), vmem(down_shape, BF),
        ],
        prefetch=1,
        free=(3, 4),
    )(ids, g_branch, w_down, slope, hid)
    gwd_mate = exchange(gwd_far, "seq", 1)
    in_shape = (2 * part, ff)
    gwi_far, gwi_near = call(
        chain,
        in_back_kernel,
        "in_back",
        vmem=16,
        grid=(4,),
        in_specs=[whole_block(bf_rows), whole_block(act_shape)],
        out_specs=[whole_block(in_shape)] * 2,
        out_shape=[vmem(in_shape, BF)] * 2,
        prefetch=1,
        free=(1,),
    )(ids, first_low, g_act)
    gwi_mate = exchange(gwi_far, "seq", 1)
    send, keep = simple(
        chain, down_add_kernel, "w_down_c", (gwd_near, gwd_mate), [vmem((blk, width), BF)] * 2,
        cost=COST,
    )
    down_share = Share(chain, ids, "w_down", send, keep)

    mine, other = simple(
        chain, in_add_kernel, "w_in_c", (ids, gwi_near, gwi_mate),
        [vmem((2 * part, ff // 2), BF)] * 2, 1,
    )
    in_share = Share(chain, ids, "w_in", mine, other, y_first=True)

    g_pre1, g_attn, g_ctx, vec1 = call(
        chain,
        first_back_kernel,
        "first_back",
        vmem=32,
        grid=(4,),
        in_specs=[
            whole_block(bf_rows), whole_block(act_shape),
            pl.BlockSpec((width, blk), lambda j: (0, j)),
            whole_block(bf_rows), whole_block((rows, 1)), vec_spec,
            whole_block((width, width)), whole_block(linv0.shape), whole_block(linv_rest.shape),
        ],
        out_specs=[
            whole_block(bf_rows), whole_block(bf_rows), whole_block(bf_rows),
            whole_block((8, width)),
        ],
        out_shape=[hbm(bf_rows, F32), vmem(bf_rows, BF), vmem(bf_rows, BF), sds((8, width), F32)],
        scratch=[pltpu.VMEM(bf_rows, F32)],
        free=(0, 3, 6, 7, 8),
    )(g_pre2, g_act, w_in, normed1, inv1, norm1_gain, w_out, linv0, linv_rest)

    projs, vecs = [], []
    low = hbm(bf_rows, BF)

    def group_back(g):
        own_col = pl.BlockSpec((rows, 128), lambda p: (0, g * steps + p))
        arrays, base = (first_heads[:3] + first_heads[4:], 0) if g == 0 else (rest_heads, g - 1)
        head_col = pl.BlockSpec((rows, 128), lambda p: (0, base * steps + p))
        proj, vec = call(
            chain,
            functools.partial(attend_back_kernel, g * heads, pair),
            "attend_back",
            vmem=20,
            grid=(steps,),
            in_specs=[
                smem(), smem(), head_col, head_col, head_col,
                pl.BlockSpec((pair, 2, half, half), lambda p: (base * steps + p, 0, 0, 0)),
                own_col, own_col,
            ],
            out_specs=[whole_block((rows, 3 * cols)), whole_block((1, 3 * cols))],
            out_shape=[vmem((rows, 3 * cols), BF), sds((1, 3 * cols), F32)],
            scratch=[pltpu.VMEM((rows, 128), F32)] * 3,
        )(seq_lengths, head_swap, *arrays[:4], g_ctx, context)
        projs.append(proj)
        vecs.append(vec)

    def attention_share(pairs, vec_ins, name, y_first):
        extra = 32 if vec_ins else 0
        size = len(pairs) * part + extra
        flat = [a for both in pairs for a in both]
        far_grad, near_grad = simple(
            chain,
            functools.partial(share_grad_kernel, len(pairs), extra),
            name + "_w",
            (ids, *flat, *vec_ins),
            [vmem((2 * size, width), BF)] * 2,
            1,
            vmem=20,
            cost=COST,
            free=(1, 3),
        )
        mate = exchange(far_grad, "seq", 1)

        def near_part():
            if y_first:
                outs = simple(
                    chain, in_add_kernel, name + "_c", (ids, near_grad, mate),
                    [vmem((2 * size, width // 2), BF)] * 2, 1,
                )
            else:
                outs = simple(
                    chain, share_add_kernel, name + "_c", (near_grad, mate),
                    [vmem((size, width), BF)] * 2,
                )
            return Share(chain, ids, name, *outs, y_first)

        return near_part

    group_back(0)
    down_share.step_y()
    start_a = attention_share([(context, g_attn), (hidden_in, projs[0])], [], "attn_a", False)
    group_back(1)
    in_share.step_x()
    share_a = start_a()
    down_share.step_z()
    group_back(2)
    down_share.step_far()
    in_share.step_z()
    vec_ins = [vec2, bias_row, vec1, *vecs]
    start_b = attention_share(
        [(hidden_in, projs[1]), (hidden_in, projs[2])], vec_ins, "attn_b", True
    )
    in_share.step_far(COST_MID)
    share_b = start_b()
    input_grad = call(
        chain,
        functools.partial(input_grad_kernel, groups),
        "input_grad",
        vmem=24,
        grid=(groups,),
        in_specs=[whole_block((rows, 3 * cols))] * groups
        + [
            pl.BlockSpec((width, cols), lambda g: (0, g)),
            pl.BlockSpec((width, cols), lambda g: (0, groups + g)),
            pl.BlockSpec((width, cols), lambda g: (0, 2 * groups + g)),
            whole_block((rows, width)),
        ],
        out_specs=whole_block((rows, width)),
        out_shape=low,
        scratch=[pltpu.VMEM((rows, width), F32)],
    )(*projs, w_qkv, w_qkv, w_qkv, g_pre1)
    (mixed,) = simple(
        chain, place_kernel, "mixed_place", (in_row, mixed_in), [hbm((ffn_rows, width), BF)]
    )
    share_b.step_x()
    down_share.step_back()
    share_a.step_y()
    in_share.step_back()
    share_b.step_z()
    down_share.step_wide()
    share_a.step_z()
    share_b.step_far()
    in_share.step_wide()
    share_a.step_far()
    share_b.step_back()
    share_a.step_back()
    g_w_down = down_share.join()
    share_b.step_wide()
    share_a.step_wide()
    g_w_in = in_share.join()
    one = lambda size: sds((size,), F32)
    g_w_qkv, g_w_out, g_qv, g_in_bias, g_n2g, g_n2b, g_down_bias, g_n1g, g_n1b, g_out_bias = simple(
        chain,
        functools.partial(attend_join_kernel, groups),
        "attn_join",
        (ids, *share_a.pieces, *share_b.pieces),
        [hbm((part, 3 * width), F32), hbm((part, width), F32), one(width // 2), one(width)]
        + [one(part)] * 6,
        1,
        scratch=[pltpu.VMEM(share_a.shape, F32), pltpu.VMEM(share_b.shape, F32)],
    )
    return (
        mixed, input_grad, g_w_qkv, g_qv, g_w_out, g_out_bias, g_n1g, g_n1b, g_w_in, g_in_bias,
        g_w_down, g_down_bias, g_n2g, g_n2b,
    )


def solution(mesh):
    rows_spec = P(("seq", "batch"), None)
    in_specs = (
        rows_spec, rows_spec, P(), P(("seq", "batch")), P(), P(), P(), P(), P(), P(), P(), P(),
        P(), P(), P(), P(), rows_spec,
    )
    out_specs = (
        rows_spec, rows_spec, P("seq", None), P("seq"), P("seq", None), P("seq"), P("seq"),
        P("seq"), P("seq", None), P("seq"), P("seq", None), P("seq"), P("seq"), P("seq"),
    )
    return jax.shard_map(body, mesh=mesh, in_specs=in_specs, out_specs=out_specs, check_vma=False)
```

```python
import functools

import jax
import jax.numpy as jnp
from jax import lax
from jax.experimental import pallas as pl
from jax.experimental.pallas import tpu as pltpu
from jax.sharding import PartitionSpec as P

EPS = 1e-05
BIG = 1e30
BF = jnp.bfloat16
F32 = jnp.float32
I32 = jnp.int32
MIB = 1 << 20
COST = 5e10
COST_MID = 2e10
COST_SMALL = 1e10
COST_TINY = 1e9
COST_TINY = 1e9

NN = (((1,), (0,)), ((), ()))
NT = (((1,), (1,)), ((), ()))
TN = (((0,), (0,)), ((), ()))


def mm(left_op, right_op, dims):
    return lax.dot_general(left_op, right_op, dims, preferred_element_type=F32)


def sds(shape, dtype):
    return jax.ShapeDtypeStruct(shape, dtype)


def hbm(shape, dtype):
    return pltpu.HBM(shape, dtype)


def vmem(shape, dtype):
    return pltpu.VMEM(shape, dtype)


def whole_block(shape):
    zeros = (0,) * len(shape)
    return pl.BlockSpec(shape, lambda *_: zeros)


def smem():
    return pl.BlockSpec(memory_space=pltpu.SMEM)


class Chain:
    def __init__(self):
        self.last = None
        self.spaces = {}

    def link(self, outs, shapes):
        flat = jax.tree.leaves(outs)
        self.last = min(flat, key=lambda a: a.size * a.dtype.itemsize)
        for out, shape in zip(flat, shapes if isinstance(shapes, (list, tuple)) else [shapes]):
            if getattr(shape, "memory_space", None) in (pltpu.HBM, pltpu.VMEM):
                self.keep(shape.memory_space, out)

    def keep(self, space, *arrays):
        for array in arrays:
            self.spaces[id(array)] = (space, array)

    def place(self, array):
        if id(array) in self.spaces:
            return pltpu.with_memory_space_constraint(array, self.spaces[id(array)][0])
        return array


def call(chain, body, name, *, grid, in_specs, out_specs, out_shape, scratch=(), prefetch=0,
         aliases=None, vmem=56, cost=COST, free=()):
    count = prefetch + len(in_specs)
    before = [] if chain.last is None else [chain.last]

    def ordered(*refs):
        body(*refs[:count], *refs[count + len(before) :])

    kernel = pl.pallas_call(
        ordered,
        name=name,
        grid_spec=pltpu.PrefetchScalarGridSpec(
            num_scalar_prefetch=prefetch,
            grid=grid,
            in_specs=list(in_specs) + [pl.BlockSpec(memory_space=pl.ANY)] * len(before),
            out_specs=out_specs,
            scratch_shapes=list(scratch),
        ),
        out_shape=out_shape,
        input_output_aliases=aliases or {},
        compiler_params=pltpu.CompilerParams(
            vmem_limit_bytes=vmem * MIB, dimension_semantics=("arbitrary",) * len(grid)
        ),
        cost_estimate=pl.CostEstimate(flops=int(cost), bytes_accessed=1, transcendentals=0),
    )

    def run(*args):
        placed = [a if at in free else chain.place(a) for at, a in enumerate(args)]
        outs = kernel(*placed, *[chain.place(a) for a in before])
        chain.link(outs, out_shape)
        return outs

    return run


def floor_div(values, divisor):
    return jnp.floor((values.astype(F32) + 0.5) * (1.0 / divisor)).astype(I32)


def route_kernel(ffn_rows, capacity, place_ref, slot_ref, target_ref):
    devices = target_ref.shape[0]
    rows = place_ref.shape[1]
    place = place_ref[...]
    live = place >= 0
    dev = jnp.where(live, floor_div(place, ffn_rows), -1)
    local = place - dev * ffn_rows
    hit = lax.broadcasted_iota(I32, (devices, rows), 0) == dev
    onehot = hit.astype(F32)
    upper = (
        lax.broadcasted_iota(I32, (rows, rows), 0) <= lax.broadcasted_iota(I32, (rows, rows), 1)
    ).astype(F32).astype(BF)
    running = mm(onehot.astype(BF), upper, NN)
    rank = (jnp.sum(running * onehot, axis=0, keepdims=True) - 1.0).astype(I32)
    slot_ref[...] = jnp.where(live, dev * capacity + rank, devices * capacity)
    ranked = (lax.broadcasted_iota(I32, (capacity, rows), 0) == rank).astype(F32).astype(BF)
    high = (local >> 5).astype(F32)
    low = (local & 31).astype(F32)
    filled = mm(onehot.astype(BF), ranked, NT)
    high_at = mm((onehot * high).astype(BF), ranked, NT)
    low_at = mm((onehot * low).astype(BF), ranked, NT)
    target = (high_at * 32.0 + low_at).astype(I32)
    target_ref[...] = jnp.where(filled > 0.5, target, ffn_rows)


def expand_targets(target, capacity):
    devices = target.shape[0]
    slots = devices * capacity
    lane = lax.broadcasted_iota(I32, (capacity, slots), 1)
    lane_dev = floor_div(lane, capacity)
    spread = ((lane - lane_dev * capacity) == lax.broadcasted_iota(I32, (capacity, slots), 0)).astype(
        F32
    ).astype(BF)
    high = mm((target >> 5).astype(F32).astype(BF), spread, NN)
    low = mm((target & 31).astype(F32).astype(BF), spread, NN)
    wide = high * 32.0 + low
    own_dev = floor_div(lax.broadcasted_iota(I32, (devices, slots), 1), capacity)
    own = own_dev == lax.broadcasted_iota(I32, (devices, slots), 0)
    return jnp.sum(jnp.where(own, wide, 0.0), axis=0, keepdims=True).astype(I32)


def onehot_rows(row_index, row_count):
    lanes = row_index.shape[1]
    return (lax.broadcasted_iota(I32, (row_count, lanes), 0) == row_index).astype(F32).astype(BF)


def onehot_cols(row_index, col_count):
    rows = row_index.shape[1]
    column = jnp.broadcast_to(row_index.astype(F32), (128, rows)).T[:, :1].astype(I32)
    return (lax.broadcasted_iota(I32, (rows, col_count), 1) == column).astype(F32).astype(BF)


def gather_kernel(capacity, target_ref, cot_ref, out_ref, row_ref):
    row = expand_targets(target_ref[...], capacity)
    row_ref[...] = row
    chosen = onehot_cols(row, cot_ref.shape[0])
    out_ref[...] = mm(chosen, cot_ref[...], NN).astype(BF)


def place_kernel(row_ref, in_ref, out_ref):
    chosen = onehot_rows(row_ref[...], out_ref.shape[0])
    out_ref[...] = mm(chosen, in_ref[...], NN).astype(BF)


def norm_rows(values):
    center = values - jnp.mean(values, axis=-1, keepdims=True)
    inverse = lax.rsqrt(jnp.mean(center * center, axis=-1, keepdims=True) + EPS)
    return center * inverse, inverse


def project(x_ref, w_refs, bq, bv, outs):
    x = x_ref[...]
    wq_ref, wk_ref, wv_ref = w_refs
    q_ref, k_ref, v_ref = outs
    q_ref[...] = (mm(x, wq_ref[...], NN) + bq).astype(BF)
    k_ref[...] = mm(x, wk_ref[...], NN).astype(BF)
    v_ref[...] = (mm(x, wv_ref[...], NN) + bv).astype(BF)


def attend_pair(
    head_base, heads, len_ref, swap_ref, q_ref, k_ref, v_ref, cut, ctx_ref, soft_ref, linv_ref
):
    rows = q_ref.shape[0]
    half = rows // 2
    quarter = rows // 4
    head_size = 128 // heads
    scale = head_size ** (-0.5)
    len0, len1 = len_ref[0, 0], len_ref[0, 1]
    is_long = len1 == 0
    lane = lax.broadcasted_iota(I32, (1, 128), 1)
    row = lax.broadcasted_iota(I32, (half, 1), 0)
    row_quarter = (row >= quarter).astype(I32)
    for b in range(2):
        q_rows = slice(b * half, (b + 1) * half)
        q_blk = q_ref[q_rows, cut].astype(F32) * scale
        out_blk = linv_blk = None
        for sub in range(heads):
            swapped = swap_ref[head_base + sub] == 1
            cross = jnp.logical_and(is_long, swapped)
            kb = jnp.where(cross, 1 - b, b)
            limit = jnp.where(is_long, len0 - kb * half, jnp.where(kb == 0, len0, len1))
            mine = jnp.logical_and(lane >= sub * head_size, lane < (sub + 1) * head_size)
            spare = ((sub + 1) % heads) * head_size
            key_rows = pl.ds(pl.multiple_of(kb * half, half), half)
            k_one = jnp.where(mine, k_ref[key_rows, cut].astype(F32), 0.0)
            q_one = jnp.where(mine, q_blk, 0.0)
            for part in range(2):
                other = jnp.where(swapped, 1 - part, part)
                band_ok = jnp.logical_or(is_long, row_quarter == other)
                bias = jnp.where(jnp.logical_and(band_ok, row < limit), 0.0, -BIG)
                at = lane == spare + part
                k_one = jnp.where(at, bias, k_one)
                q_one = jnp.where(at, jnp.where(row_quarter == part, 1.0, 0.0), q_one)
            scores = mm(q_one.astype(BF), k_one.astype(BF), NT)
            top = jnp.max(scores, axis=1, keepdims=True)
            weights = jnp.exp(scores - top)
            linv = 1.0 / jnp.sum(weights, axis=1, keepdims=True)
            soft = weights.astype(BF)
            soft_ref[sub, b] = soft
            mixed = mm(soft, v_ref[key_rows, cut], NN) * linv
            out_blk = mixed if out_blk is None else jnp.where(mine, mixed, out_blk)
            linv_blk = (
                jnp.broadcast_to(linv, mixed.shape)
                if linv_blk is None
                else jnp.where(mine, linv, linv_blk)
            )
        ctx_ref[q_rows, :] = out_blk.astype(BF)
        linv_ref[q_rows, :] = linv_blk


def attend_kernel(
    first, pairs, heads, len_ref, swap_ref, x_ref, wq_ref, wk_ref, wv_ref, b_ref, *refs
):
    if first == 0:
        q_ref, k_ref, v_ref, ctx_ref, soft_ref, linv_ref = refs
    else:
        (
            ctx0_ref, wo0_ref, wo_ref, ob_ref, gain_ref, shift_ref,
            q_ref, k_ref, v_ref, soft_ref, linv_ref, first_ref, normed_ref, inv_ref, ctx_all,
            acc_ref,
        ) = refs
    cols = q_ref.shape[1]
    width = x_ref.shape[1]
    group = first + pl.program_id(0)
    pair = pl.program_id(1)

    @pl.when(pair == 0)
    def _():
        bq = b_ref[pl.ds(pl.multiple_of(group * cols, cols), cols)].reshape(1, -1)
        bv = b_ref[pl.ds(pl.multiple_of(width + group * cols, cols), cols)].reshape(1, -1)
        project(x_ref, (wq_ref, wk_ref, wv_ref), bq, bv, (q_ref, k_ref, v_ref))

    cut = pl.ds(pl.multiple_of(pair * 128, 128), 128)
    if first > 0:
        ctx_ref = ctx_all.at[:, pl.ds(pl.multiple_of(group * cols + pair * 128, 128), 128)]
    attend_pair(
        group * (pairs * heads) + pair * heads, heads, len_ref, swap_ref, q_ref, k_ref, v_ref, cut,
        ctx_ref, soft_ref, linv_ref,
    )
    if first == 0:
        return

    @pl.when(pair == pairs - 1)
    def _():
        own = pl.ds(pl.multiple_of(group * cols, cols), cols)
        part_sum = mm(ctx_all[:, own], wo_ref[...], NN)

        @pl.when(group == first)
        def _():
            ctx_all[:, :cols] = ctx0_ref[...]
            acc_ref[...] = part_sum + mm(ctx0_ref[...], wo0_ref[...], NN)

        @pl.when(group > first)
        def _():
            acc_ref[...] += part_sum

        @pl.when(pl.program_id(0) == pl.num_programs(0) - 1)
        def _():
            attn = acc_ref[...] + ob_ref[...].reshape(1, -1)
            normed, inverse = norm_rows(x_ref[...].astype(F32) + attn)
            normed_ref[...] = normed.astype(BF)
            inv_ref[...] = inverse
            out = normed * gain_ref[...].reshape(1, -1) + shift_ref[...].reshape(1, -1)
            first_ref[...] = out.astype(BF)


def block_cols(index, size):
    return pl.ds(pl.multiple_of(index * size, size), size)


def ffn_kernel(
    x_ref, wi_ref, bi_ref, wd_ref, bd_ref, gain_ref, shift_ref,
    hid_ref, slope_ref, normed_ref, inv_ref, out_ref, acc_ref,
):
    step = pl.program_id(0)
    steps = pl.num_programs(0)
    x = x_ref[...]
    own = block_cols(step, wi_ref.shape[1])
    pre = mm(x, wi_ref[...], NN) + bi_ref[own].reshape(1, -1)
    phi = 0.5 * (1.0 + lax.erf(pre * 0.7071067811865476))
    hid = (pre * phi).astype(BF)
    hid_ref[...] = hid
    slope_ref[...] = (phi + pre * jnp.exp(-0.5 * pre * pre) * 0.3989422804014327).astype(BF)
    part_sum = mm(hid, wd_ref[...], NN)

    @pl.when(step == 0)
    def _():
        acc_ref[...] = part_sum

    @pl.when(step > 0)
    def _():
        acc_ref[...] += part_sum

    @pl.when(step == steps - 1)
    def _():
        branch = acc_ref[...] + bd_ref[...].reshape(1, -1)
        normed, inverse = norm_rows(x_ref[...].astype(F32) + branch)
        normed_ref[...] = normed.astype(BF)
        inv_ref[...] = inverse
        out = normed * gain_ref[...].reshape(1, -1) + shift_ref[...].reshape(1, -1)
        out_ref[...] = out.astype(BF)


def norm_back(upstream, normed, inverse, gain):
    scaled = upstream * gain
    inner = (
        scaled
        - jnp.mean(scaled, axis=-1, keepdims=True)
        - normed * jnp.mean(scaled * normed, axis=-1, keepdims=True)
    )
    return inner * inverse


def put_rows(ref, *rows):
    for at, row in enumerate(rows):
        ref[at : at + 1, :] = row


def quarter_at(step, ids_ref):
    rel = jnp.where(step == 0, 3, jnp.where(step == 3, 0, step))
    return jnp.bitwise_xor(ids_ref[0], rel)


def store_quarters(ids_ref, grad, far_ref, near_ref, base, size, cols=slice(None)):
    part = grad.shape[0] // 4
    for q in range(4):
        rel = jnp.bitwise_xor(ids_ref[0], q)
        value = grad[q * part : (q + 1) * part]
        rows = pl.ds(pl.multiple_of(jnp.where(rel < 2, size, 0) + base, 16), part)

        @pl.when((rel & 1) == 1)
        def _():
            far_ref[rows, cols] = value

        @pl.when((rel & 1) == 0)
        def _():
            near_ref[rows, cols] = value


def cot_back_kernel(
    slot_ref, in_ref, normed_ref, inv_ref, gain_ref, pre_ref, branch_ref, vec_ref
):
    chosen = onehot_cols(slot_ref[...], in_ref.shape[0])
    cot = mm(chosen, in_ref[...], NN)
    normed = normed_ref[...].astype(F32)
    g_pre = norm_back(cot, normed, inv_ref[...], gain_ref[...].reshape(1, -1))
    pre_ref[...] = g_pre
    branch = g_pre.astype(BF)
    branch_ref[...] = branch
    put_rows(
        vec_ref,
        jnp.sum(cot * normed, axis=0, keepdims=True),
        jnp.sum(cot, axis=0, keepdims=True),
        jnp.sum(branch.astype(F32), axis=0, keepdims=True),
    )


def down_back_kernel(
    ids_ref, branch_ref, wd_ref, slope_ref, hid_ref, act_ref, bias_ref, far_ref, near_ref
):
    step = pl.program_id(0)
    branch = branch_ref[...]
    own = block_cols(quarter_at(step, ids_ref), wd_ref.shape[0])
    g_act = (mm(branch, wd_ref[...], NT) * slope_ref[...].astype(F32)).astype(BF)
    act_ref[:, own] = g_act
    bias_ref[:, own] = jnp.sum(g_act.astype(F32), axis=0, keepdims=True)
    grad = mm(hid_ref[...], branch, TN).astype(BF)

    @pl.when(step < 2)
    def _():
        far_ref[step] = grad

    @pl.when(step >= 2)
    def _():
        near_ref[step - 2] = grad


def in_back_kernel(ids_ref, x_ref, act_ref, far_ref, near_ref):
    blk = x_ref.shape[1]
    own = block_cols(pl.program_id(0), blk)
    grad = mm(x_ref[...], act_ref[:, own], TN).astype(BF)
    store_quarters(ids_ref, grad, far_ref, near_ref, 0, blk // 4, own)


def first_back_kernel(
    pre2_ref, act_ref, wi_ref, normed_ref, inv_ref, gain_ref, wo_ref, linv0_ref, linv_ref,
    pre1_ref, gattn_ref, gctx_ref, vec_ref, acc_ref,
):
    step = pl.program_id(0)
    part_sum = mm(act_ref[:, block_cols(step, wi_ref.shape[1])], wi_ref[...], NT)

    @pl.when(step == 0)
    def _():
        acc_ref[...] = part_sum

    @pl.when(step > 0)
    def _():
        acc_ref[...] += part_sum

    @pl.when(step == pl.num_programs(0) - 1)
    def _():
        g_first = (pre2_ref[...] + acc_ref[...]).astype(BF).astype(F32)
        normed = normed_ref[...].astype(F32)
        g_pre = norm_back(g_first, normed, inv_ref[...], gain_ref[...].reshape(1, -1))
        pre1_ref[...] = g_pre
        g_attn = g_pre.astype(BF)
        put_rows(
            vec_ref,
            jnp.sum(g_first * normed, axis=0, keepdims=True),
            jnp.sum(g_first, axis=0, keepdims=True),
            jnp.sum(g_attn.astype(F32), axis=0, keepdims=True),
        )
        g_ctx = mm(g_attn, wo_ref[...], NT)
        cols = linv0_ref.shape[1]
        gctx_ref[:, :cols] = (g_ctx[:, :cols] * linv0_ref[...]).astype(BF)
        gctx_ref[:, cols:] = (g_ctx[:, cols:] * linv_ref[...]).astype(BF)
        gattn_ref[...] = g_attn


def attend_back_kernel(
    head_base, heads, len_ref, swap_ref, q_ref, k_ref, v_ref, soft_ref, gctx_ref, ctx_ref,
    proj_ref, vec_ref, gq_s, gk_s, gv_s,
):
    step = pl.program_id(0)
    rows = q_ref.shape[0]
    half = rows // 2
    head_size = 128 // heads
    scale = head_size ** (-0.5)
    is_long = len_ref[0, 1] == 0
    lane = lax.broadcasted_iota(I32, (1, 128), 1)
    for sub in range(heads):
        swapped = swap_ref[head_base + step * heads + sub] == 1
        cross = jnp.logical_and(is_long, swapped)
        mine = jnp.logical_and(lane >= sub * head_size, lane < (sub + 1) * head_size)
        for b in range(2):
            q_rows = slice(b * half, (b + 1) * half)
            kb = jnp.where(cross, 1 - b, b)
            key_rows = pl.ds(pl.multiple_of(kb * half, half), half)
            soft = soft_ref[sub, b]
            up = gctx_ref[q_rows, :]
            up_one = jnp.where(mine, up, jnp.zeros_like(up))
            inner = jnp.sum(
                up_one.astype(F32) * ctx_ref[q_rows, :].astype(F32), axis=1, keepdims=True
            )
            g_soft = mm(up_one, v_ref[key_rows, :], NT)
            g_scores = (soft.astype(F32) * (g_soft - inner)).astype(BF)
            g_q = mm(g_scores, k_ref[key_rows, :], NN) * scale
            g_k = mm(g_scores, q_ref[q_rows, :], TN) * scale
            g_v = mm(soft, up, TN)
            if sub == 0:
                gq_s[q_rows, :] = g_q
                gk_s[key_rows, :] = g_k
                gv_s[key_rows, :] = g_v
            else:
                gq_s[q_rows, :] = jnp.where(mine, g_q, gq_s[q_rows, :])
                gk_s[key_rows, :] = jnp.where(mine, g_k, gk_s[key_rows, :])
                gv_s[key_rows, :] = jnp.where(mine, g_v, gv_s[key_rows, :])
    cols = proj_ref.shape[1] // 3
    for at, ref in enumerate((gq_s, gk_s, gv_s)):
        low = ref[...].astype(BF)
        out_cols = pl.ds(pl.multiple_of(at * cols + step * 128, 128), 128)
        proj_ref[:, out_cols] = low
        vec_ref[:, out_cols] = jnp.sum(low.astype(F32), axis=0, keepdims=True)


def input_grad_kernel(groups, *refs):
    proj_refs, (wq_ref, wk_ref, wv_ref, pre_ref, out_ref, acc_ref) = refs[:groups], refs[groups:]
    step = pl.program_id(0)
    cols = wq_ref.shape[1]

    @pl.when(step == 0)
    def _():
        acc_ref[...] = pre_ref[...]

    for at, proj_ref in enumerate(proj_refs):

        @pl.when(step == at)
        def _():
            acc_ref[...] += (
                mm(proj_ref[:, :cols], wq_ref[...], NT)
                + mm(proj_ref[:, cols : 2 * cols], wk_ref[...], NT)
                + mm(proj_ref[:, 2 * cols :], wv_ref[...], NT)
            )

    @pl.when(step == groups - 1)
    def _():
        out_ref[...] = acc_ref[...].astype(BF)


def store_vectors(ids_ref, vec_refs, far_ref, near_ref, base, size):
    vec2_ref, bias_ref, vec1_ref, *qkv_refs = vec_refs
    width = vec1_ref.shape[1]
    cols = width // len(qkv_refs)
    part = width // 4
    wide = jnp.concatenate(
        [ref[:, :cols] for ref in qkv_refs] + [ref[:, 2 * cols :] for ref in qkv_refs], axis=1
    )
    extra = size - base
    for q in range(4):
        rel = jnp.bitwise_xor(ids_ref[0], q)
        rows = [bias_ref[:, q * width : (q + 1) * width]]
        rows.append(wide[:, q * (width // 2) : (q + 1) * (width // 2)])
        for ref in (vec2_ref, vec1_ref):
            rows += [ref[at : at + 1, q * part : (q + 1) * part] for at in range(3)]
        rows = [jnp.pad(row, ((0, 0), (0, width - row.shape[1]))) for row in rows]
        rows.append(jnp.zeros((extra - len(rows), width), F32))
        block = jnp.concatenate(rows, axis=0).astype(BF)
        at = pl.ds(pl.multiple_of(jnp.where(rel < 2, size, 0) + base, 16), extra)

        @pl.when((rel & 1) == 1)
        def _():
            far_ref[at, :] = block

        @pl.when((rel & 1) == 0)
        def _():
            near_ref[at, :] = block


def share_grad_kernel(count, extra, ids_ref, *refs):
    pairs = [(refs[2 * at], refs[2 * at + 1]) for at in range(count)]
    *vec_refs, far_ref, near_ref = refs[2 * count :]
    part = pairs[0][0].shape[1] // 4
    size = count * part + extra
    for at, (left_ref, right_ref) in enumerate(pairs):
        grad = mm(left_ref[...], right_ref[...], TN).astype(BF)
        store_quarters(ids_ref, grad, far_ref, near_ref, at * part, size)
    if extra:
        store_vectors(ids_ref, vec_refs, far_ref, near_ref, count * part, size)


def spread_kernel(ids_ref, near_ref, mate_ref, keep_ref, send_ref):
    total = (near_ref[...].astype(F32) + mate_ref[...].astype(F32)).astype(BF)
    rows, half = total.shape[0] // 2, total.shape[1] // 2
    second = (ids_ref[1] & 1) == 1
    core = (ids_ref[0] & 1) == 1
    left, right = total[:, :half], total[:, half:]
    mine = jnp.where(second, right, left)
    other = jnp.where(second, left, right)
    keep_ref[:rows, :] = mine[rows:]
    keep_ref[rows:, :] = jnp.where(core, mine[:rows], other[rows:])
    send_ref[:rows, :] = jnp.where(core, other[rows:], mine[:rows])
    send_ref[rows:, :] = other[:rows]


def split_blocks_kernel(keep_ref, got_ref, mine_ref, other_ref):
    total = (keep_ref[...].astype(F32) + got_ref[...].astype(F32)).astype(BF)
    rows = mine_ref.shape[0]
    mine_ref[...] = total[:rows]
    other_ref[...] = total[rows:]


def split_rows_kernel(ids_ref, keep_ref, got_ref, mine_ref, other_ref):
    half = mine_ref.shape[0]
    bit = (ids_ref[1] >> 1) & 1

    def part(at):
        rows = pl.ds(pl.multiple_of(at * half, half), half)
        return (keep_ref[rows, :].astype(F32) + got_ref[rows, :].astype(F32)).astype(BF)

    mine_ref[...] = part(bit)
    other_ref[...] = part(1 - bit)


def add_kernel(left_ref, right_ref, out_ref):
    out_ref[...] = (left_ref[...].astype(F32) + right_ref[...].astype(F32)).astype(BF)


def join_kernel(ids_ref, own_ref, near_ref, far_own_ref, far_near_ref, out_ref):
    half_rows, half_cols = own_ref.shape
    second = (ids_ref[1] & 1) == 1
    bit = (ids_ref[1] >> 1) & 1
    for rel, (mine, other) in enumerate(((own_ref, far_own_ref), (near_ref, far_near_ref))):
        at = jnp.bitwise_xor(bit, rel)
        rows = pl.ds(pl.multiple_of(at * half_rows, half_rows), half_rows)
        a, b = mine[...].astype(F32), other[...].astype(F32)
        out_ref[rows, :half_cols] = jnp.where(second, b, a)
        out_ref[rows, half_cols:] = jnp.where(second, a, b)


def stack_kernel(ids_ref, own_ref, near_ref, out_ref):
    half = own_ref.shape[0]
    bit = (ids_ref[1] >> 1) & 1
    for rel, ref in enumerate((own_ref, near_ref)):
        at = jnp.bitwise_xor(bit, rel)
        out_ref[pl.ds(pl.multiple_of(at * half, half), half), :] = ref[...]


def join_into(ids_ref, mine_ref, other_ref, out_ref):
    half = mine_ref.shape[1]
    second = (ids_ref[1] & 1) == 1
    a, b = mine_ref[...].astype(F32), other_ref[...].astype(F32)
    out_ref[:, :half] = jnp.where(second, b, a)
    out_ref[:, half:] = jnp.where(second, a, b)


def join_kernel(ids_ref, mine_ref, other_ref, out_ref):
    join_into(ids_ref, mine_ref, other_ref, out_ref)


def attend_join_kernel(groups, ids_ref, *refs):
    a_refs, b_refs = refs[:2], refs[2:4]
    gwq_ref, gwo_ref, qv_ref, hid_ref = refs[4:8]
    vec_refs, (a_all, b_all) = refs[8:14], refs[14:]
    join_into(ids_ref, *a_refs, a_all)
    join_into(ids_ref, *b_refs, b_all)
    part, width = gwo_ref.shape
    cols = width // groups
    gwo_ref[...] = a_all[:part, :]
    places = [(a_all, part)] + [(b_all, part * at) for at in range(groups - 1)]
    for g, (ref, base) in enumerate(places):
        for at in range(3):
            gwq_ref[:, at * width + g * cols : at * width + (g + 1) * cols] = ref[
                base : base + part, at * cols : (at + 1) * cols
            ]
    base = part * (groups - 1)
    hid_ref[...] = b_all[base, :]
    qv_ref[...] = b_all[base + 1, : qv_ref.shape[0]]
    for at, ref in enumerate(vec_refs):
        ref[...] = b_all[base + 2 + at, : ref.shape[0]]


def exchange(values, axis, mask):
    count = lax.axis_size(axis)
    return lax.ppermute(values, axis, [(i, i ^ mask) for i in range(count)])


def exchange_mixed(values, core_along_x):
    seq, batch = lax.axis_size("seq"), lax.axis_size("batch")

    def partner(s, b):
        return (s ^ 2) * batch + b if s & 1 == core_along_x else s * batch + (b ^ 1)

    pairs = [(s * batch + b, partner(s, b)) for s in range(seq) for b in range(batch)]
    return lax.ppermute(values, ("seq", "batch"), pairs)


def simple(chain, body, name, args, out_shape, prefetch=0, vmem=12, scratch=(), cost=COST_SMALL, free=()):
    tensors = args[prefetch:]
    return call(
        chain,
        body,
        name,
        grid=(1,),
        in_specs=[whole_block(a.shape) for a in tensors],
        out_specs=[whole_block(o.shape) for o in out_shape],
        out_shape=out_shape,
        prefetch=prefetch,
        vmem=vmem,
        cost=cost,
        free=free,
        scratch=scratch,
    )(*args)


class Share:
    def __init__(self, chain, ids, name, near, mate, cost=COST_SMALL):
        self.chain, self.ids, self.name = chain, ids, name
        rows, cols = near.shape
        self.shape = (rows // 2, cols)
        self.keep, send = simple(
            chain, spread_kernel, name + "_c", (ids, near, mate), [vmem((rows, cols // 2), BF)] * 2,
            1, cost=cost,
        )
        self.got = exchange_mixed(send, 0)

    def step_xy(self, cost=COST_SMALL):
        rows, cols = self.shape
        self.keep, send = simple(
            self.chain, split_blocks_kernel, self.name + "_x", (self.keep, self.got),
            [vmem((rows, cols // 2), BF)] * 2, cost=cost,
        )
        self.got = exchange_mixed(send, 1)

    def halve(self, kernel, shape, label, mask, cost=COST_SMALL):
        self.keep, other = simple(
            self.chain, kernel, self.name + label, (self.ids, self.keep, self.got),
            [vmem(shape, BF)] * 2, 1, cost=cost,
        )
        self.got = exchange(other, "batch", mask)

    def step_z(self, cost=COST_SMALL):
        rows, cols = self.shape
        self.halve(split_rows_kernel, (rows // 2, cols // 2), "_z", 2, cost)

    def add(self, label, cost=COST_SMALL):
        (self.keep,) = simple(
            self.chain, add_kernel, self.name + label, (self.keep, self.got),
            [vmem(self.keep.shape, BF)], cost=cost,
        )

    def step_far(self, cost=COST_SMALL):
        mask = 4
        while mask <= lax.axis_size("batch") // 2:
            self.add("_a", cost)
            self.got = exchange(self.keep, "batch", mask)
            mask *= 2

    def step_back(self, cost=COST_SMALL):
        self.add("_f", cost)
        self.got = exchange(self.keep, "batch", 2)

    def step_wide(self):
        rows, cols = self.shape
        (self.keep,) = simple(
            self.chain, stack_kernel, self.name + "_g", (self.ids, self.keep, self.got),
            [vmem((rows, cols // 2), BF)], 1,
        )
        self.pieces = (self.keep, exchange(self.keep, "batch", 1))

    def join(self):
        (whole,) = simple(
            self.chain, join_kernel, self.name + "_j", (self.ids, *self.pieces),
            [hbm(self.shape, F32)], 1,
        )
        return whole


def body(
    hidden_in, seq_lengths, head_swap, place, w_qkv, qv_bias, w_out, out_bias, norm1_gain,
    norm1_bias, w_in, in_bias, w_down, down_bias, norm2_gain, norm2_bias, cotangent,
):
    rows, width = hidden_in.shape
    ff = w_in.shape[1]
    ffn_rows = cotangent.shape[0]
    devices = lax.axis_size(("seq", "batch"))
    capacity = (rows + devices - 1) // devices
    slots = devices * capacity
    head_count = head_swap.shape[0]
    head_size = width // head_count
    half = rows // 2
    cols = 256
    groups = width // cols
    heads = cols // head_size
    pair = 128 // head_size
    ids = jnp.stack([lax.axis_index("seq"), lax.axis_index("batch")]).astype(I32)
    chain = Chain()
    chain.keep(pltpu.HBM, hidden_in, w_qkv, w_out, w_in, w_down, cotangent)

    slot_row, out_target = simple(
        chain,
        functools.partial(route_kernel, ffn_rows, capacity),
        "route",
        (place.reshape(1, -1),),
        [sds((1, rows), I32), sds((devices, capacity), I32)],
    )
    in_target = lax.all_to_all(out_target, ("seq", "batch"), split_axis=0, concat_axis=0, tiled=True)

    bf_rows = (rows, width)
    vec_spec = whole_block((width,))
    steps = heads // pair
    some = lambda count, dtype: hbm((rows, count * cols), dtype)
    col = lambda base: pl.BlockSpec((width, cols), lambda g, p, *_: (0, base + g))
    out_col = pl.BlockSpec((rows, cols), lambda g, p, *_: (0, g))
    pair_out = pl.BlockSpec((rows, 128), lambda g, p, *_: (0, g * steps + p))
    soft_spec = pl.BlockSpec((pair, 2, half, half), lambda g, p, *_: (g * steps + p, 0, 0, 0))
    head_outs = [out_col] * 3 + [pair_out, soft_spec, pair_out]
    head_shapes = lambda count: [some(count, BF)] * 4 + [
        hbm((count * heads, 2, half, half), BF), some(count, F32)
    ]
    head_args = (seq_lengths, head_swap, hidden_in, w_qkv, w_qkv, w_qkv, qv_bias)
    head_specs = lambda first: [
        smem(), smem(), whole_block(bf_rows), col(first), col(groups + first),
        col(2 * groups + first), whole_block((2 * width,)),
    ]
    first_heads = call(
        chain,
        functools.partial(attend_kernel, 0, steps, pair),
        "attend_first",
        vmem=32,
        grid=(1, steps),
        in_specs=head_specs(0),
        out_specs=head_outs,
        out_shape=head_shapes(1),
    )(*head_args)
    context0, linv0 = first_heads[3], first_heads[5]
    cot_out, in_row = simple(
        chain,
        functools.partial(gather_kernel, capacity),
        "cot_gather",
        (in_target, cotangent),
        [sds((slots, width), BF), sds((1, slots), I32)],
        free=(1,),
    )
    cot_in = lax.all_to_all(cot_out, ("seq", "batch"), split_axis=0, concat_axis=0, tiled=True)
    *rest_heads, first_low, normed1, inv1, context = call(
        chain,
        functools.partial(attend_kernel, 1, steps, pair),
        "attend_rest",
        vmem=40,
        grid=(groups - 1, steps),
        in_specs=head_specs(1)
        + [
            whole_block((rows, cols)), pl.BlockSpec((cols, width), lambda g, p, *_: (0, 0)),
            pl.BlockSpec((cols, width), lambda g, p, *_: (1 + g, 0)), vec_spec, vec_spec, vec_spec,
        ],
        out_specs=head_outs[:3] + head_outs[4:]
        + [whole_block(bf_rows), whole_block(bf_rows), whole_block((rows, 1)), whole_block(bf_rows)],
        out_shape=head_shapes(groups - 1)[:3] + head_shapes(groups - 1)[4:]
        + [hbm(bf_rows, BF), hbm(bf_rows, BF), hbm((rows, 1), F32), hbm(bf_rows, BF)],
        scratch=[pltpu.VMEM(bf_rows, F32)],
    )(*head_args, context0, w_out, w_out, out_bias, norm1_gain, norm1_bias)
    linv_rest = rest_heads[4]

    blk = ff // 4
    act_shape = (rows, ff)
    act_col = pl.BlockSpec((rows, blk), lambda j, *_: (0, j))
    hid, slope, normed2, inv2, mixed_home = call(
        chain,
        ffn_kernel,
        "ffn",
        vmem=36,
        grid=(4,),
        in_specs=[
            whole_block(bf_rows),
            pl.BlockSpec((width, blk), lambda j, *_: (0, j)),
            whole_block((ff,)),
            pl.BlockSpec((blk, width), lambda j, *_: (j, 0)),
            vec_spec, vec_spec, vec_spec,
        ],
        out_specs=[
            act_col, act_col, whole_block(bf_rows), whole_block((rows, 1)), whole_block(bf_rows),
        ],
        out_shape=[
            hbm(act_shape, BF), hbm(act_shape, BF), hbm(bf_rows, BF), hbm((rows, 1), F32),
            vmem(bf_rows, BF),
        ],
        scratch=[pltpu.VMEM(bf_rows, F32)],
    )(first_low, w_in, in_bias, w_down, down_bias, norm2_gain, norm2_bias)

    (mixed_out,) = simple(
        chain, place_kernel, "mixed_slots", (slot_row, mixed_home), [sds((slots, width), BF)],
        cost=COST,
    )
    mixed_in = lax.all_to_all(mixed_out, ("seq", "batch"), split_axis=0, concat_axis=0, tiled=True)

    g_pre2, g_branch, vec2 = simple(
        chain,
        cot_back_kernel,
        "cot_back",
        (slot_row, cot_in, normed2, inv2, norm2_gain),
        [vmem(bf_rows, F32), vmem(bf_rows, BF), sds((8, width), F32)],
        vmem=24,
        cost=COST,
    )
    part = width // 4
    quarter_rows = pl.BlockSpec((blk, width), lambda j, i: (quarter_at(j, i), 0))
    quarter_cols = pl.BlockSpec((rows, blk), lambda j, i: (0, quarter_at(j, i)))
    down_shape = (2, blk, width)
    g_act, bias_row, gwd_far, gwd_near = call(
        chain,
        down_back_kernel,
        "down_back",
        vmem=24,
        grid=(4,),
        in_specs=[whole_block(bf_rows), quarter_rows, quarter_cols, quarter_cols],
        out_specs=[
            whole_block(act_shape), whole_block((1, ff)), whole_block(down_shape),
            whole_block(down_shape),
        ],
        out_shape=[
            vmem(act_shape, BF), sds((1, ff), F32), vmem(down_shape, BF), vmem(down_shape, BF),
        ],
        prefetch=1,
    )(ids, g_branch, w_down, slope, hid)
    gwd_far, gwd_near = (a.reshape(2 * blk, width) for a in (gwd_far, gwd_near))
    gwd_mate = exchange(gwd_far, "seq", 1)
    in_shape = (2 * part, ff)
    gwi_far, gwi_near = call(
        chain,
        in_back_kernel,
        "in_back",
        vmem=16,
        grid=(4,),
        in_specs=[whole_block(bf_rows), whole_block(act_shape)],
        out_specs=[whole_block(in_shape)] * 2,
        out_shape=[vmem(in_shape, BF)] * 2,
        prefetch=1,
        free=(1,),
    )(ids, first_low, g_act)
    gwi_mate = exchange(gwi_far, "seq", 1)
    down_share = Share(chain, ids, "w_down", gwd_near, gwd_mate, COST)
    in_share = Share(chain, ids, "w_in", gwi_near, gwi_mate)

    g_pre1, g_attn, g_ctx, vec1 = call(
        chain,
        first_back_kernel,
        "first_back",
        vmem=32,
        grid=(4,),
        in_specs=[
            whole_block(bf_rows), whole_block(act_shape),
            pl.BlockSpec((width, blk), lambda j: (0, j)),
            whole_block(bf_rows), whole_block((rows, 1)), vec_spec,
            whole_block((width, width)), whole_block(linv0.shape), whole_block(linv_rest.shape),
        ],
        out_specs=[
            whole_block(bf_rows), whole_block(bf_rows), whole_block(bf_rows),
            whole_block((8, width)),
        ],
        out_shape=[hbm(bf_rows, F32), vmem(bf_rows, BF), vmem(bf_rows, BF), sds((8, width), F32)],
        scratch=[pltpu.VMEM(bf_rows, F32)],
        free=(0, 3, 6, 7, 8),
    )(g_pre2, g_act, w_in, normed1, inv1, norm1_gain, w_out, linv0, linv_rest)

    projs, vecs = [], []
    low = hbm(bf_rows, BF)

    def group_back(g):
        own_col = pl.BlockSpec((rows, 128), lambda p: (0, g * steps + p))
        arrays, base = (first_heads[:3] + first_heads[4:], 0) if g == 0 else (rest_heads, g - 1)
        head_col = pl.BlockSpec((rows, 128), lambda p: (0, base * steps + p))
        proj, vec = call(
            chain,
            functools.partial(attend_back_kernel, g * heads, pair),
            "attend_back",
            vmem=20,
            grid=(steps,),
            in_specs=[
                smem(), smem(), head_col, head_col, head_col,
                pl.BlockSpec((pair, 2, half, half), lambda p: (base * steps + p, 0, 0, 0)),
                own_col, own_col,
            ],
            out_specs=[whole_block((rows, 3 * cols)), whole_block((1, 3 * cols))],
            out_shape=[vmem((rows, 3 * cols), BF), sds((1, 3 * cols), F32)],
            scratch=[pltpu.VMEM((rows, 128), F32)] * 3,
        )(seq_lengths, head_swap, *arrays[:4], g_ctx, context)
        projs.append(proj)
        vecs.append(vec)

    def attention_share(pairs, vec_ins, name, cost=COST):
        extra = 32 if vec_ins else 0
        size = len(pairs) * part + extra
        flat = [a for both in pairs for a in both]
        far_grad, near_grad = simple(
            chain,
            functools.partial(share_grad_kernel, len(pairs), extra),
            name + "_w",
            (ids, *flat, *vec_ins),
            [vmem((2 * size, width), BF)] * 2,
            1,
            vmem=20,
            cost=cost,
            free=(1, 3),
        )
        mate = exchange(far_grad, "seq", 1)
        return lambda: Share(chain, ids, name, near_grad, mate)

    down_share.step_xy()
    group_back(0)
    start_a = attention_share([(context, g_attn), (hidden_in, projs[0])], [], "attn_a")
    down_share.step_z()
    in_share.step_xy()
    group_back(1)
    down_share.step_far()
    in_share.step_z()
    share_a = start_a()
    group_back(2)
    share_a.step_xy(COST_TINY)
    vec_ins = [vec2, bias_row, vec1, *vecs]
    start_b = attention_share(
        [(hidden_in, projs[1]), (hidden_in, projs[2])], vec_ins, "attn_b", COST_TINY
    )
    in_share.step_far()
    down_share.step_back(COST_MID)
    share_b = start_b()
    input_grad = call(
        chain,
        functools.partial(input_grad_kernel, groups),
        "input_grad",
        vmem=24,
        grid=(groups,),
        in_specs=[whole_block((rows, 3 * cols))] * groups
        + [
            pl.BlockSpec((width, cols), lambda g: (0, g)),
            pl.BlockSpec((width, cols), lambda g: (0, groups + g)),
            pl.BlockSpec((width, cols), lambda g: (0, 2 * groups + g)),
            whole_block((rows, width)),
        ],
        out_specs=whole_block((rows, width)),
        out_shape=low,
        scratch=[pltpu.VMEM((rows, width), F32)],
    )(*projs, w_qkv, w_qkv, w_qkv, g_pre1)
    share_a.step_z()
    share_b.step_xy()
    (mixed,) = simple(
        chain, place_kernel, "mixed_place", (in_row, mixed_in), [hbm((ffn_rows, width), BF)]
    )
    share_b.step_z()
    down_share.step_wide()
    in_share.step_back()
    share_a.step_far()
    share_b.step_far()
    in_share.step_wide()
    share_a.step_back()
    g_w_down = down_share.join()
    share_b.step_back()
    share_a.step_wide()
    share_b.step_wide()
    g_w_in = in_share.join()
    one = lambda size: sds((size,), F32)
    g_w_qkv, g_w_out, g_qv, g_in_bias, g_n2g, g_n2b, g_down_bias, g_n1g, g_n1b, g_out_bias = simple(
        chain,
        functools.partial(attend_join_kernel, groups),
        "attn_join",
        (ids, *share_a.pieces, *share_b.pieces),
        [hbm((part, 3 * width), F32), hbm((part, width), F32), one(width // 2), one(width)]
        + [one(part)] * 6,
        1,
        scratch=[pltpu.VMEM(share_a.shape, F32), pltpu.VMEM(share_b.shape, F32)],
    )
    return (
        mixed, input_grad, g_w_qkv, g_qv, g_w_out, g_out_bias, g_n1g, g_n1b, g_w_in, g_in_bias,
        g_w_down, g_down_bias, g_n2g, g_n2b,
    )


def solution(mesh):
    rows_spec = P(("seq", "batch"), None)
    in_specs = (
        rows_spec, rows_spec, P(), P(("seq", "batch")), P(), P(), P(), P(), P(), P(), P(), P(),
        P(), P(), P(), P(), rows_spec,
    )
    out_specs = (
        rows_spec, rows_spec, P("seq", None), P("seq"), P("seq", None), P("seq"), P("seq"),
        P("seq"), P("seq", None), P("seq"), P("seq", None), P("seq"), P("seq"), P("seq"),
    )
    return jax.shard_map(body, mesh=mesh, in_specs=in_specs, out_specs=out_specs, check_vma=False)
```

```python
import functools

import jax
import jax.numpy as jnp
from jax import lax
from jax.experimental import pallas as pl
from jax.experimental.pallas import tpu as pltpu
from jax.sharding import PartitionSpec as P

EPS = 1e-05
BIG = 1e30
BF = jnp.bfloat16
F32 = jnp.float32
I32 = jnp.int32
MIB = 1 << 20
COST = 5e10
COST_MID = 2e10
COST_SMALL = 1e10
COST_TINY = 1e9
COST_TINY = 1e9

NN = (((1,), (0,)), ((), ()))
NT = (((1,), (1,)), ((), ()))
TN = (((0,), (0,)), ((), ()))


def mm(left_op, right_op, dims):
    return lax.dot_general(left_op, right_op, dims, preferred_element_type=F32)


def sds(shape, dtype):
    return jax.ShapeDtypeStruct(shape, dtype)


def hbm(shape, dtype):
    return pltpu.HBM(shape, dtype)


def vmem(shape, dtype):
    return pltpu.VMEM(shape, dtype)


def whole_block(shape):
    zeros = (0,) * len(shape)
    return pl.BlockSpec(shape, lambda *_: zeros)


def smem():
    return pl.BlockSpec(memory_space=pltpu.SMEM)


class Chain:
    def __init__(self):
        self.last = None
        self.spaces = {}

    def link(self, outs, shapes):
        flat = jax.tree.leaves(outs)
        self.last = min(flat, key=lambda a: a.size * a.dtype.itemsize)
        for out, shape in zip(flat, shapes if isinstance(shapes, (list, tuple)) else [shapes]):
            if getattr(shape, "memory_space", None) in (pltpu.HBM, pltpu.VMEM):
                self.keep(shape.memory_space, out)

    def keep(self, space, *arrays):
        for array in arrays:
            self.spaces[id(array)] = (space, array)

    def place(self, array):
        if id(array) in self.spaces:
            return pltpu.with_memory_space_constraint(array, self.spaces[id(array)][0])
        return array


def call(chain, body, name, *, grid, in_specs, out_specs, out_shape, scratch=(), prefetch=0,
         aliases=None, vmem=56, cost=COST, free=()):
    count = prefetch + len(in_specs)
    before = [] if chain.last is None else [chain.last]

    def ordered(*refs):
        body(*refs[:count], *refs[count + len(before) :])

    kernel = pl.pallas_call(
        ordered,
        name=name,
        grid_spec=pltpu.PrefetchScalarGridSpec(
            num_scalar_prefetch=prefetch,
            grid=grid,
            in_specs=list(in_specs) + [pl.BlockSpec(memory_space=pl.ANY)] * len(before),
            out_specs=out_specs,
            scratch_shapes=list(scratch),
        ),
        out_shape=out_shape,
        input_output_aliases=aliases or {},
        compiler_params=pltpu.CompilerParams(
            vmem_limit_bytes=vmem * MIB, dimension_semantics=("arbitrary",) * len(grid)
        ),
        cost_estimate=pl.CostEstimate(flops=int(cost), bytes_accessed=1, transcendentals=0),
    )

    def run(*args):
        placed = [a if at in free else chain.place(a) for at, a in enumerate(args)]
        outs = kernel(*placed, *[chain.place(a) for a in before])
        chain.link(outs, out_shape)
        return outs

    return run


def floor_div(values, divisor):
    return jnp.floor((values.astype(F32) + 0.5) * (1.0 / divisor)).astype(I32)


def route_kernel(ffn_rows, capacity, place_ref, slot_ref, target_ref):
    devices = target_ref.shape[0]
    rows = place_ref.shape[1]
    place = place_ref[...]
    live = place >= 0
    dev = jnp.where(live, floor_div(place, ffn_rows), -1)
    local = place - dev * ffn_rows
    hit = lax.broadcasted_iota(I32, (devices, rows), 0) == dev
    onehot = hit.astype(F32)
    upper = (
        lax.broadcasted_iota(I32, (rows, rows), 0) <= lax.broadcasted_iota(I32, (rows, rows), 1)
    ).astype(F32).astype(BF)
    running = mm(onehot.astype(BF), upper, NN)
    rank = (jnp.sum(running * onehot, axis=0, keepdims=True) - 1.0).astype(I32)
    slot_ref[...] = jnp.where(live, dev * capacity + rank, devices * capacity)
    ranked = (lax.broadcasted_iota(I32, (capacity, rows), 0) == rank).astype(F32).astype(BF)
    high = (local >> 5).astype(F32)
    low = (local & 31).astype(F32)
    filled = mm(onehot.astype(BF), ranked, NT)
    high_at = mm((onehot * high).astype(BF), ranked, NT)
    low_at = mm((onehot * low).astype(BF), ranked, NT)
    target = (high_at * 32.0 + low_at).astype(I32)
    target_ref[...] = jnp.where(filled > 0.5, target, ffn_rows)


def expand_targets(target, capacity):
    devices = target.shape[0]
    slots = devices * capacity
    lane = lax.broadcasted_iota(I32, (capacity, slots), 1)
    lane_dev = floor_div(lane, capacity)
    spread = ((lane - lane_dev * capacity) == lax.broadcasted_iota(I32, (capacity, slots), 0)).astype(
        F32
    ).astype(BF)
    high = mm((target >> 5).astype(F32).astype(BF), spread, NN)
    low = mm((target & 31).astype(F32).astype(BF), spread, NN)
    wide = high * 32.0 + low
    own_dev = floor_div(lax.broadcasted_iota(I32, (devices, slots), 1), capacity)
    own = own_dev == lax.broadcasted_iota(I32, (devices, slots), 0)
    return jnp.sum(jnp.where(own, wide, 0.0), axis=0, keepdims=True).astype(I32)


def onehot_rows(row_index, row_count):
    lanes = row_index.shape[1]
    return (lax.broadcasted_iota(I32, (row_count, lanes), 0) == row_index).astype(F32).astype(BF)


def onehot_cols(row_index, col_count):
    rows = row_index.shape[1]
    column = jnp.broadcast_to(row_index.astype(F32), (128, rows)).T[:, :1].astype(I32)
    return (lax.broadcasted_iota(I32, (rows, col_count), 1) == column).astype(F32).astype(BF)


def gather_kernel(capacity, target_ref, cot_ref, out_ref, row_ref):
    row = expand_targets(target_ref[...], capacity)
    row_ref[...] = row
    chosen = onehot_cols(row, cot_ref.shape[0])
    out_ref[...] = mm(chosen, cot_ref[...], NN).astype(BF)


def place_kernel(row_ref, in_ref, out_ref):
    chosen = onehot_rows(row_ref[...], out_ref.shape[0])
    out_ref[...] = mm(chosen, in_ref[...], NN).astype(BF)


def norm_rows(values):
    center = values - jnp.mean(values, axis=-1, keepdims=True)
    inverse = lax.rsqrt(jnp.mean(center * center, axis=-1, keepdims=True) + EPS)
    return center * inverse, inverse


def project(x_ref, w_refs, bq, bv, outs):
    x = x_ref[...]
    wq_ref, wk_ref, wv_ref = w_refs
    q_ref, k_ref, v_ref = outs
    q_ref[...] = (mm(x, wq_ref[...], NN) + bq).astype(BF)
    k_ref[...] = mm(x, wk_ref[...], NN).astype(BF)
    v_ref[...] = (mm(x, wv_ref[...], NN) + bv).astype(BF)


def attend_pair(
    head_base, heads, len_ref, swap_ref, q_ref, k_ref, v_ref, cut, ctx_ref, soft_ref, linv_ref
):
    rows = q_ref.shape[0]
    half = rows // 2
    quarter = rows // 4
    head_size = 128 // heads
    scale = head_size ** (-0.5)
    len0, len1 = len_ref[0, 0], len_ref[0, 1]
    is_long = len1 == 0
    lane = lax.broadcasted_iota(I32, (1, 128), 1)
    row = lax.broadcasted_iota(I32, (half, 1), 0)
    row_quarter = (row >= quarter).astype(I32)
    for b in range(2):
        q_rows = slice(b * half, (b + 1) * half)
        q_blk = q_ref[q_rows, cut].astype(F32) * scale
        out_blk = linv_blk = None
        for sub in range(heads):
            swapped = swap_ref[head_base + sub] == 1
            cross = jnp.logical_and(is_long, swapped)
            kb = jnp.where(cross, 1 - b, b)
            limit = jnp.where(is_long, len0 - kb * half, jnp.where(kb == 0, len0, len1))
            mine = jnp.logical_and(lane >= sub * head_size, lane < (sub + 1) * head_size)
            spare = ((sub + 1) % heads) * head_size
            key_rows = pl.ds(pl.multiple_of(kb * half, half), half)
            k_one = jnp.where(mine, k_ref[key_rows, cut].astype(F32), 0.0)
            q_one = jnp.where(mine, q_blk, 0.0)
            for part in range(2):
                other = jnp.where(swapped, 1 - part, part)
                band_ok = jnp.logical_or(is_long, row_quarter == other)
                bias = jnp.where(jnp.logical_and(band_ok, row < limit), 0.0, -BIG)
                at = lane == spare + part
                k_one = jnp.where(at, bias, k_one)
                q_one = jnp.where(at, jnp.where(row_quarter == part, 1.0, 0.0), q_one)
            scores = mm(q_one.astype(BF), k_one.astype(BF), NT)
            top = jnp.max(scores, axis=1, keepdims=True)
            weights = jnp.exp(scores - top)
            linv = 1.0 / jnp.sum(weights, axis=1, keepdims=True)
            soft = weights.astype(BF)
            soft_ref[sub, b] = soft
            mixed = mm(soft, v_ref[key_rows, cut], NN) * linv
            out_blk = mixed if out_blk is None else jnp.where(mine, mixed, out_blk)
            linv_blk = (
                jnp.broadcast_to(linv, mixed.shape)
                if linv_blk is None
                else jnp.where(mine, linv, linv_blk)
            )
        ctx_ref[q_rows, :] = out_blk.astype(BF)
        linv_ref[q_rows, :] = linv_blk


def attend_kernel(
    first, pairs, heads, len_ref, swap_ref, x_ref, wq_ref, wk_ref, wv_ref, b_ref, *refs
):
    if first == 0:
        q_ref, k_ref, v_ref, ctx_ref, soft_ref, linv_ref = refs
    else:
        (
            ctx0_ref, wo0_ref, wo_ref, ob_ref, gain_ref, shift_ref,
            q_ref, k_ref, v_ref, soft_ref, linv_ref, first_ref, normed_ref, inv_ref, ctx_all,
            acc_ref,
        ) = refs
    cols = q_ref.shape[1]
    width = x_ref.shape[1]
    group = first + pl.program_id(0)
    pair = pl.program_id(1)

    @pl.when(pair == 0)
    def _():
        bq = b_ref[pl.ds(pl.multiple_of(group * cols, cols), cols)].reshape(1, -1)
        bv = b_ref[pl.ds(pl.multiple_of(width + group * cols, cols), cols)].reshape(1, -1)
        project(x_ref, (wq_ref, wk_ref, wv_ref), bq, bv, (q_ref, k_ref, v_ref))

    cut = pl.ds(pl.multiple_of(pair * 128, 128), 128)
    if first > 0:
        ctx_ref = ctx_all.at[:, pl.ds(pl.multiple_of(group * cols + pair * 128, 128), 128)]
    attend_pair(
        group * (pairs * heads) + pair * heads, heads, len_ref, swap_ref, q_ref, k_ref, v_ref, cut,
        ctx_ref, soft_ref, linv_ref,
    )
    if first == 0:
        return

    @pl.when(pair == pairs - 1)
    def _():
        own = pl.ds(pl.multiple_of(group * cols, cols), cols)
        part_sum = mm(ctx_all[:, own], wo_ref[...], NN)

        @pl.when(group == first)
        def _():
            ctx_all[:, :cols] = ctx0_ref[...]
            acc_ref[...] = part_sum + mm(ctx0_ref[...], wo0_ref[...], NN)

        @pl.when(group > first)
        def _():
            acc_ref[...] += part_sum

        @pl.when(pl.program_id(0) == pl.num_programs(0) - 1)
        def _():
            attn = acc_ref[...] + ob_ref[...].reshape(1, -1)
            normed, inverse = norm_rows(x_ref[...].astype(F32) + attn)
            normed_ref[...] = normed.astype(BF)
            inv_ref[...] = inverse
            out = normed * gain_ref[...].reshape(1, -1) + shift_ref[...].reshape(1, -1)
            first_ref[...] = out.astype(BF)


def block_cols(index, size):
    return pl.ds(pl.multiple_of(index * size, size), size)


def ffn_kernel(
    x_ref, wi_ref, bi_ref, wd_ref, bd_ref, gain_ref, shift_ref,
    hid_ref, slope_ref, normed_ref, inv_ref, out_ref, acc_ref,
):
    step = pl.program_id(0)
    steps = pl.num_programs(0)
    x = x_ref[...]
    own = block_cols(step, wi_ref.shape[1])
    pre = mm(x, wi_ref[...], NN) + bi_ref[own].reshape(1, -1)
    phi = 0.5 * (1.0 + lax.erf(pre * 0.7071067811865476))
    hid = (pre * phi).astype(BF)
    hid_ref[...] = hid
    slope_ref[...] = (phi + pre * jnp.exp(-0.5 * pre * pre) * 0.3989422804014327).astype(BF)
    part_sum = mm(hid, wd_ref[...], NN)

    @pl.when(step == 0)
    def _():
        acc_ref[...] = part_sum

    @pl.when(step > 0)
    def _():
        acc_ref[...] += part_sum

    @pl.when(step == steps - 1)
    def _():
        branch = acc_ref[...] + bd_ref[...].reshape(1, -1)
        normed, inverse = norm_rows(x_ref[...].astype(F32) + branch)
        normed_ref[...] = normed.astype(BF)
        inv_ref[...] = inverse
        out = normed * gain_ref[...].reshape(1, -1) + shift_ref[...].reshape(1, -1)
        out_ref[...] = out.astype(BF)


def norm_back(upstream, normed, inverse, gain):
    scaled = upstream * gain
    inner = (
        scaled
        - jnp.mean(scaled, axis=-1, keepdims=True)
        - normed * jnp.mean(scaled * normed, axis=-1, keepdims=True)
    )
    return inner * inverse


def put_rows(ref, *rows):
    for at, row in enumerate(rows):
        ref[at : at + 1, :] = row


def quarter_at(step, ids_ref):
    rel = jnp.where(step == 0, 3, jnp.where(step == 3, 0, step))
    return jnp.bitwise_xor(ids_ref[0], rel)


def store_quarters(ids_ref, grad, far_ref, near_ref, base, size, cols=slice(None)):
    part = grad.shape[0] // 4
    for q in range(4):
        rel = jnp.bitwise_xor(ids_ref[0], q)
        value = grad[q * part : (q + 1) * part]
        rows = pl.ds(pl.multiple_of(jnp.where(rel < 2, size, 0) + base, 16), part)

        @pl.when((rel & 1) == 1)
        def _():
            far_ref[rows, cols] = value

        @pl.when((rel & 1) == 0)
        def _():
            near_ref[rows, cols] = value


def cot_back_kernel(
    slot_ref, in_ref, normed_ref, inv_ref, gain_ref, pre_ref, branch_ref, vec_ref
):
    chosen = onehot_cols(slot_ref[...], in_ref.shape[0])
    cot = mm(chosen, in_ref[...], NN)
    normed = normed_ref[...].astype(F32)
    g_pre = norm_back(cot, normed, inv_ref[...], gain_ref[...].reshape(1, -1))
    pre_ref[...] = g_pre
    branch = g_pre.astype(BF)
    branch_ref[...] = branch
    put_rows(
        vec_ref,
        jnp.sum(cot * normed, axis=0, keepdims=True),
        jnp.sum(cot, axis=0, keepdims=True),
        jnp.sum(branch.astype(F32), axis=0, keepdims=True),
    )


def down_back_kernel(
    ids_ref, branch_ref, wd_ref, slope_ref, hid_ref, act_ref, bias_ref, far_ref, near_ref
):
    step = pl.program_id(0)
    branch = branch_ref[...]
    own = block_cols(quarter_at(step, ids_ref), wd_ref.shape[0])
    g_act = (mm(branch, wd_ref[...], NT) * slope_ref[...].astype(F32)).astype(BF)
    act_ref[:, own] = g_act
    bias_ref[:, own] = jnp.sum(g_act.astype(F32), axis=0, keepdims=True)
    grad = mm(hid_ref[...], branch, TN).astype(BF)

    @pl.when(step < 2)
    def _():
        far_ref[step] = grad

    @pl.when(step >= 2)
    def _():
        near_ref[step - 2] = grad


def in_back_kernel(ids_ref, x_ref, act_ref, far_ref, near_ref):
    blk = x_ref.shape[1]
    own = block_cols(pl.program_id(0), blk)
    grad = mm(x_ref[...], act_ref[:, own], TN).astype(BF)
    store_quarters(ids_ref, grad, far_ref, near_ref, 0, blk // 4, own)


def first_back_kernel(
    pre2_ref, act_ref, wi_ref, normed_ref, inv_ref, gain_ref, wo_ref, linv0_ref, linv_ref,
    pre1_ref, gattn_ref, gctx_ref, vec_ref,
):
    g_first = pre2_ref[...] + mm(act_ref[...], wi_ref[...], NT)
    g_first = g_first.astype(BF).astype(F32)
    normed = normed_ref[...].astype(F32)
    g_pre = norm_back(g_first, normed, inv_ref[...], gain_ref[...].reshape(1, -1))
    pre1_ref[...] = g_pre
    g_attn = g_pre.astype(BF)
    put_rows(
        vec_ref,
        jnp.sum(g_first * normed, axis=0, keepdims=True),
        jnp.sum(g_first, axis=0, keepdims=True),
        jnp.sum(g_attn.astype(F32), axis=0, keepdims=True),
    )
    g_ctx = mm(g_attn, wo_ref[...], NT)
    cols = linv0_ref.shape[1]
    gctx_ref[:, :cols] = (g_ctx[:, :cols] * linv0_ref[...]).astype(BF)
    gctx_ref[:, cols:] = (g_ctx[:, cols:] * linv_ref[...]).astype(BF)
    gattn_ref[...] = g_attn


def attend_back_kernel(
    head_base, heads, len_ref, swap_ref, q_ref, k_ref, v_ref, soft_ref, gctx_ref, ctx_ref,
    proj_ref, vec_ref, gq_s, gk_s, gv_s,
):
    step = pl.program_id(0)
    rows = q_ref.shape[0]
    half = rows // 2
    head_size = 128 // heads
    scale = head_size ** (-0.5)
    is_long = len_ref[0, 1] == 0
    lane = lax.broadcasted_iota(I32, (1, 128), 1)
    for sub in range(heads):
        swapped = swap_ref[head_base + step * heads + sub] == 1
        cross = jnp.logical_and(is_long, swapped)
        mine = jnp.logical_and(lane >= sub * head_size, lane < (sub + 1) * head_size)
        for b in range(2):
            q_rows = slice(b * half, (b + 1) * half)
            kb = jnp.where(cross, 1 - b, b)
            key_rows = pl.ds(pl.multiple_of(kb * half, half), half)
            soft = soft_ref[sub, b]
            up = gctx_ref[q_rows, :]
            up_one = jnp.where(mine, up, jnp.zeros_like(up))
            inner = jnp.sum(
                up_one.astype(F32) * ctx_ref[q_rows, :].astype(F32), axis=1, keepdims=True
            )
            g_soft = mm(up_one, v_ref[key_rows, :], NT)
            g_scores = (soft.astype(F32) * (g_soft - inner)).astype(BF)
            g_q = mm(g_scores, k_ref[key_rows, :], NN) * scale
            g_k = mm(g_scores, q_ref[q_rows, :], TN) * scale
            g_v = mm(soft, up, TN)
            if sub == 0:
                gq_s[q_rows, :] = g_q
                gk_s[key_rows, :] = g_k
                gv_s[key_rows, :] = g_v
            else:
                gq_s[q_rows, :] = jnp.where(mine, g_q, gq_s[q_rows, :])
                gk_s[key_rows, :] = jnp.where(mine, g_k, gk_s[key_rows, :])
                gv_s[key_rows, :] = jnp.where(mine, g_v, gv_s[key_rows, :])
    cols = proj_ref.shape[1] // 3
    for at, ref in enumerate((gq_s, gk_s, gv_s)):
        low = ref[...].astype(BF)
        out_cols = pl.ds(pl.multiple_of(at * cols + step * 128, 128), 128)
        proj_ref[:, out_cols] = low
        vec_ref[:, out_cols] = jnp.sum(low.astype(F32), axis=0, keepdims=True)


def input_grad_kernel(groups, *refs):
    proj_refs, (wq_ref, wk_ref, wv_ref, pre_ref, out_ref, acc_ref) = refs[:groups], refs[groups:]
    step = pl.program_id(0)
    cols = wq_ref.shape[1]

    @pl.when(step == 0)
    def _():
        acc_ref[...] = pre_ref[...]

    for at, proj_ref in enumerate(proj_refs):

        @pl.when(step == at)
        def _():
            acc_ref[...] += (
                mm(proj_ref[:, :cols], wq_ref[...], NT)
                + mm(proj_ref[:, cols : 2 * cols], wk_ref[...], NT)
                + mm(proj_ref[:, 2 * cols :], wv_ref[...], NT)
            )

    @pl.when(step == groups - 1)
    def _():
        out_ref[...] = acc_ref[...].astype(BF)


def store_vectors(ids_ref, vec_refs, far_ref, near_ref, base, size):
    vec2_ref, bias_ref, vec1_ref, *qkv_refs = vec_refs
    width = vec1_ref.shape[1]
    cols = width // len(qkv_refs)
    part = width // 4
    wide = jnp.concatenate(
        [ref[:, :cols] for ref in qkv_refs] + [ref[:, 2 * cols :] for ref in qkv_refs], axis=1
    )
    extra = size - base
    for q in range(4):
        rel = jnp.bitwise_xor(ids_ref[0], q)
        rows = [bias_ref[:, q * width : (q + 1) * width]]
        rows.append(wide[:, q * (width // 2) : (q + 1) * (width // 2)])
        for ref in (vec2_ref, vec1_ref):
            rows += [ref[at : at + 1, q * part : (q + 1) * part] for at in range(3)]
        rows = [jnp.pad(row, ((0, 0), (0, width - row.shape[1]))) for row in rows]
        rows.append(jnp.zeros((extra - len(rows), width), F32))
        block = jnp.concatenate(rows, axis=0).astype(BF)
        at = pl.ds(pl.multiple_of(jnp.where(rel < 2, size, 0) + base, 16), extra)

        @pl.when((rel & 1) == 1)
        def _():
            far_ref[at, :] = block

        @pl.when((rel & 1) == 0)
        def _():
            near_ref[at, :] = block


def share_grad_kernel(count, extra, ids_ref, *refs):
    pairs = [(refs[2 * at], refs[2 * at + 1]) for at in range(count)]
    *vec_refs, far_ref, near_ref = refs[2 * count :]
    part = pairs[0][0].shape[1] // 4
    size = count * part + extra
    for at, (left_ref, right_ref) in enumerate(pairs):
        grad = mm(left_ref[...], right_ref[...], TN).astype(BF)
        store_quarters(ids_ref, grad, far_ref, near_ref, at * part, size)
    if extra:
        store_vectors(ids_ref, vec_refs, far_ref, near_ref, count * part, size)


def spread_kernel(ids_ref, near_ref, mate_ref, keep_ref, send_ref):
    total = (near_ref[...].astype(F32) + mate_ref[...].astype(F32)).astype(BF)
    rows, half = total.shape[0] // 2, total.shape[1] // 2
    second = (ids_ref[1] & 1) == 1
    core = (ids_ref[0] & 1) == 1
    left, right = total[:, :half], total[:, half:]
    mine = jnp.where(second, right, left)
    other = jnp.where(second, left, right)
    keep_ref[:rows, :] = mine[rows:]
    keep_ref[rows:, :] = jnp.where(core, mine[:rows], other[rows:])
    send_ref[:rows, :] = jnp.where(core, other[rows:], mine[:rows])
    send_ref[rows:, :] = other[:rows]


def split_blocks_kernel(keep_ref, got_ref, mine_ref, other_ref):
    total = (keep_ref[...].astype(F32) + got_ref[...].astype(F32)).astype(BF)
    rows = mine_ref.shape[0]
    mine_ref[...] = total[:rows]
    other_ref[...] = total[rows:]


def split_rows_kernel(ids_ref, keep_ref, got_ref, mine_ref, other_ref):
    half = mine_ref.shape[0]
    bit = (ids_ref[1] >> 1) & 1

    def part(at):
        rows = pl.ds(pl.multiple_of(at * half, half), half)
        return (keep_ref[rows, :].astype(F32) + got_ref[rows, :].astype(F32)).astype(BF)

    mine_ref[...] = part(bit)
    other_ref[...] = part(1 - bit)


def add_kernel(left_ref, right_ref, out_ref):
    out_ref[...] = (left_ref[...].astype(F32) + right_ref[...].astype(F32)).astype(BF)


def join_kernel(ids_ref, own_ref, near_ref, far_own_ref, far_near_ref, out_ref):
    half_rows, half_cols = own_ref.shape
    second = (ids_ref[1] & 1) == 1
    bit = (ids_ref[1] >> 1) & 1
    for rel, (mine, other) in enumerate(((own_ref, far_own_ref), (near_ref, far_near_ref))):
        at = jnp.bitwise_xor(bit, rel)
        rows = pl.ds(pl.multiple_of(at * half_rows, half_rows), half_rows)
        a, b = mine[...].astype(F32), other[...].astype(F32)
        out_ref[rows, :half_cols] = jnp.where(second, b, a)
        out_ref[rows, half_cols:] = jnp.where(second, a, b)


def stack_kernel(ids_ref, own_ref, near_ref, out_ref):
    half = own_ref.shape[0]
    bit = (ids_ref[1] >> 1) & 1
    for rel, ref in enumerate((own_ref, near_ref)):
        at = jnp.bitwise_xor(bit, rel)
        out_ref[pl.ds(pl.multiple_of(at * half, half), half), :] = ref[...]


def join_into(ids_ref, mine_ref, other_ref, out_ref):
    half = mine_ref.shape[1]
    second = (ids_ref[1] & 1) == 1
    a, b = mine_ref[...].astype(F32), other_ref[...].astype(F32)
    out_ref[:, :half] = jnp.where(second, b, a)
    out_ref[:, half:] = jnp.where(second, a, b)


def join_kernel(ids_ref, mine_ref, other_ref, out_ref):
    join_into(ids_ref, mine_ref, other_ref, out_ref)


def attend_join_kernel(groups, ids_ref, *refs):
    a_refs, b_refs = refs[:2], refs[2:4]
    gwq_ref, gwo_ref, qv_ref, hid_ref = refs[4:8]
    vec_refs, (a_all, b_all) = refs[8:14], refs[14:]
    join_into(ids_ref, *a_refs, a_all)
    join_into(ids_ref, *b_refs, b_all)
    part, width = gwo_ref.shape
    cols = width // groups
    gwo_ref[...] = a_all[:part, :]
    places = [(a_all, part)] + [(b_all, part * at) for at in range(groups - 1)]
    for g, (ref, base) in enumerate(places):
        for at in range(3):
            gwq_ref[:, at * width + g * cols : at * width + (g + 1) * cols] = ref[
                base : base + part, at * cols : (at + 1) * cols
            ]
    base = part * (groups - 1)
    hid_ref[...] = b_all[base, :]
    qv_ref[...] = b_all[base + 1, : qv_ref.shape[0]]
    for at, ref in enumerate(vec_refs):
        ref[...] = b_all[base + 2 + at, : ref.shape[0]]


def exchange(values, axis, mask):
    count = lax.axis_size(axis)
    return lax.ppermute(values, axis, [(i, i ^ mask) for i in range(count)])


def exchange_mixed(values, core_along_x):
    seq, batch = lax.axis_size("seq"), lax.axis_size("batch")

    def partner(s, b):
        return (s ^ 2) * batch + b if s & 1 == core_along_x else s * batch + (b ^ 1)

    pairs = [(s * batch + b, partner(s, b)) for s in range(seq) for b in range(batch)]
    return lax.ppermute(values, ("seq", "batch"), pairs)


def simple(chain, body, name, args, out_shape, prefetch=0, vmem=12, scratch=(), cost=COST_SMALL, free=()):
    tensors = args[prefetch:]
    return call(
        chain,
        body,
        name,
        grid=(1,),
        in_specs=[whole_block(a.shape) for a in tensors],
        out_specs=[whole_block(o.shape) for o in out_shape],
        out_shape=out_shape,
        prefetch=prefetch,
        vmem=vmem,
        cost=cost,
        free=free,
        scratch=scratch,
    )(*args)


class Share:
    def __init__(self, chain, ids, name, near, mate, cost=COST_SMALL):
        self.chain, self.ids, self.name = chain, ids, name
        rows, cols = near.shape
        self.shape = (rows // 2, cols)
        self.keep, send = simple(
            chain, spread_kernel, name + "_c", (ids, near, mate), [vmem((rows, cols // 2), BF)] * 2,
            1, cost=cost,
        )
        self.got = exchange_mixed(send, 0)

    def step_xy(self, cost=COST_SMALL):
        rows, cols = self.shape
        self.keep, send = simple(
            self.chain, split_blocks_kernel, self.name + "_x", (self.keep, self.got),
            [vmem((rows, cols // 2), BF)] * 2, cost=cost,
        )
        self.got = exchange_mixed(send, 1)

    def halve(self, kernel, shape, label, mask, cost=COST_SMALL):
        self.keep, other = simple(
            self.chain, kernel, self.name + label, (self.ids, self.keep, self.got),
            [vmem(shape, BF)] * 2, 1, cost=cost,
        )
        self.got = exchange(other, "batch", mask)

    def step_z(self, cost=COST_SMALL):
        rows, cols = self.shape
        self.halve(split_rows_kernel, (rows // 2, cols // 2), "_z", 2, cost)

    def add(self, label, cost=COST_SMALL):
        (self.keep,) = simple(
            self.chain, add_kernel, self.name + label, (self.keep, self.got),
            [vmem(self.keep.shape, BF)], cost=cost,
        )

    def step_far(self, cost=COST_SMALL):
        mask = 4
        while mask <= lax.axis_size("batch") // 2:
            self.add("_a", cost)
            self.got = exchange(self.keep, "batch", mask)
            mask *= 2

    def step_back(self, cost=COST_SMALL):
        self.add("_f", cost)
        self.got = exchange(self.keep, "batch", 2)

    def step_wide(self):
        rows, cols = self.shape
        (self.keep,) = simple(
            self.chain, stack_kernel, self.name + "_g", (self.ids, self.keep, self.got),
            [vmem((rows, cols // 2), BF)], 1,
        )
        self.pieces = (self.keep, exchange(self.keep, "batch", 1))

    def join(self):
        (whole,) = simple(
            self.chain, join_kernel, self.name + "_j", (self.ids, *self.pieces),
            [hbm(self.shape, F32)], 1,
        )
        return whole


def body(
    hidden_in, seq_lengths, head_swap, place, w_qkv, qv_bias, w_out, out_bias, norm1_gain,
    norm1_bias, w_in, in_bias, w_down, down_bias, norm2_gain, norm2_bias, cotangent,
):
    rows, width = hidden_in.shape
    ff = w_in.shape[1]
    ffn_rows = cotangent.shape[0]
    devices = lax.axis_size(("seq", "batch"))
    capacity = (rows + devices - 1) // devices
    slots = devices * capacity
    head_count = head_swap.shape[0]
    head_size = width // head_count
    half = rows // 2
    cols = 256
    groups = width // cols
    heads = cols // head_size
    pair = 128 // head_size
    ids = jnp.stack([lax.axis_index("seq"), lax.axis_index("batch")]).astype(I32)
    chain = Chain()
    chain.keep(pltpu.HBM, hidden_in, w_qkv, w_out, w_in, w_down, cotangent)

    slot_row, out_target = simple(
        chain,
        functools.partial(route_kernel, ffn_rows, capacity),
        "route",
        (place.reshape(1, -1),),
        [sds((1, rows), I32), sds((devices, capacity), I32)],
    )
    in_target = lax.all_to_all(out_target, ("seq", "batch"), split_axis=0, concat_axis=0, tiled=True)

    bf_rows = (rows, width)
    vec_spec = whole_block((width,))
    steps = heads // pair
    some = lambda count, dtype: hbm((rows, count * cols), dtype)
    col = lambda base: pl.BlockSpec((width, cols), lambda g, p, *_: (0, base + g))
    out_col = pl.BlockSpec((rows, cols), lambda g, p, *_: (0, g))
    pair_out = pl.BlockSpec((rows, 128), lambda g, p, *_: (0, g * steps + p))
    soft_spec = pl.BlockSpec((pair, 2, half, half), lambda g, p, *_: (g * steps + p, 0, 0, 0))
    head_outs = [out_col] * 3 + [pair_out, soft_spec, pair_out]
    head_shapes = lambda count: [some(count, BF)] * 4 + [
        hbm((count * heads, 2, half, half), BF), some(count, F32)
    ]
    head_args = (seq_lengths, head_swap, hidden_in, w_qkv, w_qkv, w_qkv, qv_bias)
    head_specs = lambda first: [
        smem(), smem(), whole_block(bf_rows), col(first), col(groups + first),
        col(2 * groups + first), whole_block((2 * width,)),
    ]
    first_heads = call(
        chain,
        functools.partial(attend_kernel, 0, steps, pair),
        "attend_first",
        vmem=32,
        grid=(1, steps),
        in_specs=head_specs(0),
        out_specs=head_outs,
        out_shape=head_shapes(1),
    )(*head_args)
    context0, linv0 = first_heads[3], first_heads[5]
    cot_out, in_row = simple(
        chain,
        functools.partial(gather_kernel, capacity),
        "cot_gather",
        (in_target, cotangent),
        [sds((slots, width), BF), sds((1, slots), I32)],
        free=(1,),
    )
    cot_in = lax.all_to_all(cot_out, ("seq", "batch"), split_axis=0, concat_axis=0, tiled=True)
    *rest_heads, first_low, normed1, inv1, context = call(
        chain,
        functools.partial(attend_kernel, 1, steps, pair),
        "attend_rest",
        vmem=40,
        grid=(groups - 1, steps),
        in_specs=head_specs(1)
        + [
            whole_block((rows, cols)), pl.BlockSpec((cols, width), lambda g, p, *_: (0, 0)),
            pl.BlockSpec((cols, width), lambda g, p, *_: (1 + g, 0)), vec_spec, vec_spec, vec_spec,
        ],
        out_specs=head_outs[:3] + head_outs[4:]
        + [whole_block(bf_rows), whole_block(bf_rows), whole_block((rows, 1)), whole_block(bf_rows)],
        out_shape=head_shapes(groups - 1)[:3] + head_shapes(groups - 1)[4:]
        + [hbm(bf_rows, BF), hbm(bf_rows, BF), hbm((rows, 1), F32), hbm(bf_rows, BF)],
        scratch=[pltpu.VMEM(bf_rows, F32)],
    )(*head_args, context0, w_out, w_out, out_bias, norm1_gain, norm1_bias)
    linv_rest = rest_heads[4]

    blk = ff // 4
    act_shape = (rows, ff)
    act_col = pl.BlockSpec((rows, blk), lambda j, *_: (0, j))
    hid, slope, normed2, inv2, mixed_home = call(
        chain,
        ffn_kernel,
        "ffn",
        vmem=36,
        grid=(4,),
        in_specs=[
            whole_block(bf_rows),
            pl.BlockSpec((width, blk), lambda j, *_: (0, j)),
            whole_block((ff,)),
            pl.BlockSpec((blk, width), lambda j, *_: (j, 0)),
            vec_spec, vec_spec, vec_spec,
        ],
        out_specs=[
            act_col, act_col, whole_block(bf_rows), whole_block((rows, 1)), whole_block(bf_rows),
        ],
        out_shape=[
            hbm(act_shape, BF), hbm(act_shape, BF), hbm(bf_rows, BF), hbm((rows, 1), F32),
            vmem(bf_rows, BF),
        ],
        scratch=[pltpu.VMEM(bf_rows, F32)],
    )(first_low, w_in, in_bias, w_down, down_bias, norm2_gain, norm2_bias)

    (mixed_out,) = simple(
        chain, place_kernel, "mixed_slots", (slot_row, mixed_home), [sds((slots, width), BF)],
        cost=COST,
    )
    mixed_in = lax.all_to_all(mixed_out, ("seq", "batch"), split_axis=0, concat_axis=0, tiled=True)

    g_pre2, g_branch, vec2 = simple(
        chain,
        cot_back_kernel,
        "cot_back",
        (slot_row, cot_in, normed2, inv2, norm2_gain),
        [vmem(bf_rows, F32), vmem(bf_rows, BF), sds((8, width), F32)],
        vmem=24,
        cost=COST,
    )
    part = width // 4
    quarter_rows = pl.BlockSpec((blk, width), lambda j, i: (quarter_at(j, i), 0))
    quarter_cols = pl.BlockSpec((rows, blk), lambda j, i: (0, quarter_at(j, i)))
    down_shape = (2, blk, width)
    g_act, bias_row, gwd_far, gwd_near = call(
        chain,
        down_back_kernel,
        "down_back",
        vmem=24,
        grid=(4,),
        in_specs=[whole_block(bf_rows), quarter_rows, quarter_cols, quarter_cols],
        out_specs=[
            whole_block(act_shape), whole_block((1, ff)), whole_block(down_shape),
            whole_block(down_shape),
        ],
        out_shape=[
            vmem(act_shape, BF), sds((1, ff), F32), vmem(down_shape, BF), vmem(down_shape, BF),
        ],
        prefetch=1,
    )(ids, g_branch, w_down, slope, hid)
    gwd_far, gwd_near = (a.reshape(2 * blk, width) for a in (gwd_far, gwd_near))
    gwd_mate = exchange(gwd_far, "seq", 1)
    in_shape = (2 * part, ff)
    gwi_far, gwi_near = call(
        chain,
        in_back_kernel,
        "in_back",
        vmem=16,
        grid=(4,),
        in_specs=[whole_block(bf_rows), whole_block(act_shape)],
        out_specs=[whole_block(in_shape)] * 2,
        out_shape=[vmem(in_shape, BF)] * 2,
        prefetch=1,
        free=(1,),
    )(ids, first_low, g_act)
    gwi_mate = exchange(gwi_far, "seq", 1)
    down_share = Share(chain, ids, "w_down", gwd_near, gwd_mate, COST)
    in_share = Share(chain, ids, "w_in", gwi_near, gwi_mate)

    g_pre1, g_attn, g_ctx, vec1 = call(
        chain,
        first_back_kernel,
        "first_back",
        vmem=32,
        grid=(1,),
        in_specs=[
            whole_block(bf_rows), whole_block(act_shape),
            whole_block((width, ff)),
            whole_block(bf_rows), whole_block((rows, 1)), vec_spec,
            whole_block((width, width)), whole_block(linv0.shape), whole_block(linv_rest.shape),
        ],
        out_specs=[
            whole_block(bf_rows), whole_block(bf_rows), whole_block(bf_rows),
            whole_block((8, width)),
        ],
        out_shape=[hbm(bf_rows, F32), vmem(bf_rows, BF), vmem(bf_rows, BF), sds((8, width), F32)],
        free=(0, 2, 3, 6, 7, 8),
    )(g_pre2, g_act, w_in, normed1, inv1, norm1_gain, w_out, linv0, linv_rest)

    projs, vecs = [], []
    low = hbm(bf_rows, BF)

    def group_back(g):
        own_col = pl.BlockSpec((rows, 128), lambda p: (0, g * steps + p))
        arrays, base = (first_heads[:3] + first_heads[4:], 0) if g == 0 else (rest_heads, g - 1)
        head_col = pl.BlockSpec((rows, 128), lambda p: (0, base * steps + p))
        proj, vec = call(
            chain,
            functools.partial(attend_back_kernel, g * heads, pair),
            "attend_back",
            vmem=20,
            grid=(steps,),
            in_specs=[
                smem(), smem(), head_col, head_col, head_col,
                pl.BlockSpec((pair, 2, half, half), lambda p: (base * steps + p, 0, 0, 0)),
                own_col, own_col,
            ],
            out_specs=[whole_block((rows, 3 * cols)), whole_block((1, 3 * cols))],
            out_shape=[vmem((rows, 3 * cols), BF), sds((1, 3 * cols), F32)],
            scratch=[pltpu.VMEM((rows, 128), F32)] * 3,
        )(seq_lengths, head_swap, *arrays[:4], g_ctx, context)
        projs.append(proj)
        vecs.append(vec)

    def attention_share(pairs, vec_ins, name, cost=COST):
        extra = 32 if vec_ins else 0
        size = len(pairs) * part + extra
        flat = [a for both in pairs for a in both]
        far_grad, near_grad = simple(
            chain,
            functools.partial(share_grad_kernel, len(pairs), extra),
            name + "_w",
            (ids, *flat, *vec_ins),
            [vmem((2 * size, width), BF)] * 2,
            1,
            vmem=20,
            cost=cost,
            free=(1, 3),
        )
        mate = exchange(far_grad, "seq", 1)
        return lambda: Share(chain, ids, name, near_grad, mate)

    down_share.step_xy()
    group_back(0)
    start_a = attention_share([(context, g_attn), (hidden_in, projs[0])], [], "attn_a")
    down_share.step_z()
    in_share.step_xy()
    group_back(1)
    down_share.step_far()
    in_share.step_z()
    share_a = start_a()
    group_back(2)
    share_a.step_xy(COST_TINY)
    vec_ins = [vec2, bias_row, vec1, *vecs]
    start_b = attention_share(
        [(hidden_in, projs[1]), (hidden_in, projs[2])], vec_ins, "attn_b", COST_TINY
    )
    in_share.step_far()
    down_share.step_back(COST_MID)
    share_b = start_b()
    input_grad = call(
        chain,
        functools.partial(input_grad_kernel, groups),
        "input_grad",
        vmem=24,
        grid=(groups,),
        in_specs=[whole_block((rows, 3 * cols))] * groups
        + [
            pl.BlockSpec((width, cols), lambda g: (0, g)),
            pl.BlockSpec((width, cols), lambda g: (0, groups + g)),
            pl.BlockSpec((width, cols), lambda g: (0, 2 * groups + g)),
            whole_block((rows, width)),
        ],
        out_specs=whole_block((rows, width)),
        out_shape=low,
        scratch=[pltpu.VMEM((rows, width), F32)],
    )(*projs, w_qkv, w_qkv, w_qkv, g_pre1)
    share_a.step_z()
    share_b.step_xy()
    (mixed,) = simple(
        chain, place_kernel, "mixed_place", (in_row, mixed_in), [hbm((ffn_rows, width), BF)]
    )
    down_share.step_wide()
    in_share.step_back()
    share_b.step_z()
    share_a.step_far()
    in_share.step_wide()
    share_b.step_far()
    share_a.step_back()
    g_w_down = down_share.join()
    share_b.step_back()
    share_a.step_wide()
    share_b.step_wide()
    g_w_in = in_share.join()
    one = lambda size: sds((size,), F32)
    g_w_qkv, g_w_out, g_qv, g_in_bias, g_n2g, g_n2b, g_down_bias, g_n1g, g_n1b, g_out_bias = simple(
        chain,
        functools.partial(attend_join_kernel, groups),
        "attn_join",
        (ids, *share_a.pieces, *share_b.pieces),
        [hbm((part, 3 * width), F32), hbm((part, width), F32), one(width // 2), one(width)]
        + [one(part)] * 6,
        1,
        scratch=[pltpu.VMEM(share_a.shape, F32), pltpu.VMEM(share_b.shape, F32)],
    )
    return (
        mixed, input_grad, g_w_qkv, g_qv, g_w_out, g_out_bias, g_n1g, g_n1b, g_w_in, g_in_bias,
        g_w_down, g_down_bias, g_n2g, g_n2b,
    )


def solution(mesh):
    rows_spec = P(("seq", "batch"), None)
    in_specs = (
        rows_spec, rows_spec, P(), P(("seq", "batch")), P(), P(), P(), P(), P(), P(), P(), P(),
        P(), P(), P(), P(), rows_spec,
    )
    out_specs = (
        rows_spec, rows_spec, P("seq", None), P("seq"), P("seq", None), P("seq"), P("seq"),
        P("seq"), P("seq", None), P("seq"), P("seq", None), P("seq"), P("seq"), P("seq"),
    )
    return jax.shard_map(body, mesh=mesh, in_specs=in_specs, out_specs=out_specs, check_vma=False)
```

```python
import functools

import jax
import jax.numpy as jnp
from jax import lax
from jax.experimental import pallas as pl
from jax.experimental.pallas import tpu as pltpu
from jax.sharding import PartitionSpec as P

EPS = 1e-05
BIG = 1e30
BF = jnp.bfloat16
F32 = jnp.float32
I32 = jnp.int32
MIB = 1 << 20
COST = 5e10
COST_MID = 2e10
COST_SMALL = 1e10
COST_TINY = 1e9
COST_TINY = 1e9

NN = (((1,), (0,)), ((), ()))
NT = (((1,), (1,)), ((), ()))
TN = (((0,), (0,)), ((), ()))


def mm(left_op, right_op, dims):
    return lax.dot_general(left_op, right_op, dims, preferred_element_type=F32)


def sds(shape, dtype):
    return jax.ShapeDtypeStruct(shape, dtype)


def hbm(shape, dtype):
    return pltpu.HBM(shape, dtype)


def vmem(shape, dtype):
    return pltpu.VMEM(shape, dtype)


def whole_block(shape):
    zeros = (0,) * len(shape)
    return pl.BlockSpec(shape, lambda *_: zeros)


def smem():
    return pl.BlockSpec(memory_space=pltpu.SMEM)


class Chain:
    def __init__(self):
        self.last = None
        self.spaces = {}

    def link(self, outs, shapes):
        flat = jax.tree.leaves(outs)
        self.last = min(flat, key=lambda a: a.size * a.dtype.itemsize)
        for out, shape in zip(flat, shapes if isinstance(shapes, (list, tuple)) else [shapes]):
            if getattr(shape, "memory_space", None) in (pltpu.HBM, pltpu.VMEM):
                self.keep(shape.memory_space, out)

    def keep(self, space, *arrays):
        for array in arrays:
            self.spaces[id(array)] = (space, array)

    def place(self, array):
        if id(array) in self.spaces:
            return pltpu.with_memory_space_constraint(array, self.spaces[id(array)][0])
        return array


def call(chain, body, name, *, grid, in_specs, out_specs, out_shape, scratch=(), prefetch=0,
         aliases=None, vmem=56, cost=COST, free=()):
    count = prefetch + len(in_specs)
    before = [] if chain.last is None else [chain.last]

    def ordered(*refs):
        body(*refs[:count], *refs[count + len(before) :])

    kernel = pl.pallas_call(
        ordered,
        name=name,
        grid_spec=pltpu.PrefetchScalarGridSpec(
            num_scalar_prefetch=prefetch,
            grid=grid,
            in_specs=list(in_specs) + [pl.BlockSpec(memory_space=pl.ANY)] * len(before),
            out_specs=out_specs,
            scratch_shapes=list(scratch),
        ),
        out_shape=out_shape,
        input_output_aliases=aliases or {},
        compiler_params=pltpu.CompilerParams(
            vmem_limit_bytes=vmem * MIB, dimension_semantics=("arbitrary",) * len(grid)
        ),
        cost_estimate=pl.CostEstimate(flops=int(cost), bytes_accessed=1, transcendentals=0),
    )

    def run(*args):
        placed = [a if at in free else chain.place(a) for at, a in enumerate(args)]
        outs = kernel(*placed, *[chain.place(a) for a in before])
        chain.link(outs, out_shape)
        return outs

    return run


def floor_div(values, divisor):
    return jnp.floor((values.astype(F32) + 0.5) * (1.0 / divisor)).astype(I32)


def route_kernel(ffn_rows, capacity, place_ref, slot_ref, target_ref):
    devices = target_ref.shape[0]
    rows = place_ref.shape[1]
    place = place_ref[...]
    live = place >= 0
    dev = jnp.where(live, floor_div(place, ffn_rows), -1)
    local = place - dev * ffn_rows
    hit = lax.broadcasted_iota(I32, (devices, rows), 0) == dev
    onehot = hit.astype(F32)
    upper = (
        lax.broadcasted_iota(I32, (rows, rows), 0) <= lax.broadcasted_iota(I32, (rows, rows), 1)
    ).astype(F32).astype(BF)
    running = mm(onehot.astype(BF), upper, NN)
    rank = (jnp.sum(running * onehot, axis=0, keepdims=True) - 1.0).astype(I32)
    slot_ref[...] = jnp.where(live, dev * capacity + rank, devices * capacity)
    ranked = (lax.broadcasted_iota(I32, (capacity, rows), 0) == rank).astype(F32).astype(BF)
    high = (local >> 5).astype(F32)
    low = (local & 31).astype(F32)
    filled = mm(onehot.astype(BF), ranked, NT)
    high_at = mm((onehot * high).astype(BF), ranked, NT)
    low_at = mm((onehot * low).astype(BF), ranked, NT)
    target = (high_at * 32.0 + low_at).astype(I32)
    target_ref[...] = jnp.where(filled > 0.5, target, ffn_rows)


def expand_targets(target, capacity):
    devices = target.shape[0]
    slots = devices * capacity
    lane = lax.broadcasted_iota(I32, (capacity, slots), 1)
    lane_dev = floor_div(lane, capacity)
    spread = ((lane - lane_dev * capacity) == lax.broadcasted_iota(I32, (capacity, slots), 0)).astype(
        F32
    ).astype(BF)
    high = mm((target >> 5).astype(F32).astype(BF), spread, NN)
    low = mm((target & 31).astype(F32).astype(BF), spread, NN)
    wide = high * 32.0 + low
    own_dev = floor_div(lax.broadcasted_iota(I32, (devices, slots), 1), capacity)
    own = own_dev == lax.broadcasted_iota(I32, (devices, slots), 0)
    return jnp.sum(jnp.where(own, wide, 0.0), axis=0, keepdims=True).astype(I32)


def onehot_rows(row_index, row_count):
    lanes = row_index.shape[1]
    return (lax.broadcasted_iota(I32, (row_count, lanes), 0) == row_index).astype(F32).astype(BF)


def onehot_cols(row_index, col_count):
    rows = row_index.shape[1]
    column = jnp.broadcast_to(row_index.astype(F32), (128, rows)).T[:, :1].astype(I32)
    return (lax.broadcasted_iota(I32, (rows, col_count), 1) == column).astype(F32).astype(BF)


def gather_kernel(capacity, target_ref, cot_ref, out_ref, row_ref):
    row = expand_targets(target_ref[...], capacity)
    row_ref[...] = row
    chosen = onehot_cols(row, cot_ref.shape[0])
    out_ref[...] = mm(chosen, cot_ref[...], NN).astype(BF)


def place_kernel(row_ref, in_ref, out_ref):
    chosen = onehot_rows(row_ref[...], out_ref.shape[0])
    out_ref[...] = mm(chosen, in_ref[...], NN).astype(BF)


def norm_rows(values):
    center = values - jnp.mean(values, axis=-1, keepdims=True)
    inverse = lax.rsqrt(jnp.mean(center * center, axis=-1, keepdims=True) + EPS)
    return center * inverse, inverse


def project(x_ref, w_refs, bq, bv, outs):
    x = x_ref[...]
    wq_ref, wk_ref, wv_ref = w_refs
    q_ref, k_ref, v_ref = outs
    q_ref[...] = (mm(x, wq_ref[...], NN) + bq).astype(BF)
    k_ref[...] = mm(x, wk_ref[...], NN).astype(BF)
    v_ref[...] = (mm(x, wv_ref[...], NN) + bv).astype(BF)


def attend_pair(
    head_base, heads, len_ref, swap_ref, q_ref, k_ref, v_ref, cut, ctx_ref, soft_ref, linv_ref
):
    rows = q_ref.shape[0]
    half = rows // 2
    quarter = rows // 4
    head_size = 128 // heads
    scale = head_size ** (-0.5)
    len0, len1 = len_ref[0, 0], len_ref[0, 1]
    is_long = len1 == 0
    lane = lax.broadcasted_iota(I32, (1, 128), 1)
    row = lax.broadcasted_iota(I32, (half, 1), 0)
    row_quarter = (row >= quarter).astype(I32)
    for b in range(2):
        q_rows = slice(b * half, (b + 1) * half)
        q_blk = q_ref[q_rows, cut].astype(F32) * scale
        out_blk = linv_blk = None
        for sub in range(heads):
            swapped = swap_ref[head_base + sub] == 1
            cross = jnp.logical_and(is_long, swapped)
            kb = jnp.where(cross, 1 - b, b)
            limit = jnp.where(is_long, len0 - kb * half, jnp.where(kb == 0, len0, len1))
            mine = jnp.logical_and(lane >= sub * head_size, lane < (sub + 1) * head_size)
            spare = ((sub + 1) % heads) * head_size
            key_rows = pl.ds(pl.multiple_of(kb * half, half), half)
            k_one = jnp.where(mine, k_ref[key_rows, cut].astype(F32), 0.0)
            q_one = jnp.where(mine, q_blk, 0.0)
            for part in range(2):
                other = jnp.where(swapped, 1 - part, part)
                band_ok = jnp.logical_or(is_long, row_quarter == other)
                bias = jnp.where(jnp.logical_and(band_ok, row < limit), 0.0, -BIG)
                at = lane == spare + part
                k_one = jnp.where(at, bias, k_one)
                q_one = jnp.where(at, jnp.where(row_quarter == part, 1.0, 0.0), q_one)
            scores = mm(q_one.astype(BF), k_one.astype(BF), NT)
            top = jnp.max(scores, axis=1, keepdims=True)
            weights = jnp.exp(scores - top)
            linv = 1.0 / jnp.sum(weights, axis=1, keepdims=True)
            soft = weights.astype(BF)
            soft_ref[sub, b] = soft
            mixed = mm(soft, v_ref[key_rows, cut], NN) * linv
            out_blk = mixed if out_blk is None else jnp.where(mine, mixed, out_blk)
            linv_blk = (
                jnp.broadcast_to(linv, mixed.shape)
                if linv_blk is None
                else jnp.where(mine, linv, linv_blk)
            )
        ctx_ref[q_rows, :] = out_blk.astype(BF)
        linv_ref[q_rows, :] = linv_blk


def attend_kernel(
    first, pairs, heads, len_ref, swap_ref, x_ref, wq_ref, wk_ref, wv_ref, b_ref, *refs
):
    if first == 0:
        q_ref, k_ref, v_ref, ctx_ref, soft_ref, linv_ref = refs
    else:
        (
            ctx0_ref, wo0_ref, wo_ref, ob_ref, gain_ref, shift_ref,
            q_ref, k_ref, v_ref, soft_ref, linv_ref, first_ref, normed_ref, inv_ref, ctx_all,
            acc_ref,
        ) = refs
    cols = q_ref.shape[1]
    width = x_ref.shape[1]
    group = first + pl.program_id(0)
    pair = pl.program_id(1)

    @pl.when(pair == 0)
    def _():
        bq = b_ref[pl.ds(pl.multiple_of(group * cols, cols), cols)].reshape(1, -1)
        bv = b_ref[pl.ds(pl.multiple_of(width + group * cols, cols), cols)].reshape(1, -1)
        project(x_ref, (wq_ref, wk_ref, wv_ref), bq, bv, (q_ref, k_ref, v_ref))

    cut = pl.ds(pl.multiple_of(pair * 128, 128), 128)
    if first > 0:
        ctx_ref = ctx_all.at[:, pl.ds(pl.multiple_of(group * cols + pair * 128, 128), 128)]
    attend_pair(
        group * (pairs * heads) + pair * heads, heads, len_ref, swap_ref, q_ref, k_ref, v_ref, cut,
        ctx_ref, soft_ref, linv_ref,
    )
    if first == 0:
        return

    @pl.when(pair == pairs - 1)
    def _():
        own = pl.ds(pl.multiple_of(group * cols, cols), cols)
        part_sum = mm(ctx_all[:, own], wo_ref[...], NN)

        @pl.when(group == first)
        def _():
            ctx_all[:, :cols] = ctx0_ref[...]
            acc_ref[...] = part_sum + mm(ctx0_ref[...], wo0_ref[...], NN)

        @pl.when(group > first)
        def _():
            acc_ref[...] += part_sum

        @pl.when(pl.program_id(0) == pl.num_programs(0) - 1)
        def _():
            attn = acc_ref[...] + ob_ref[...].reshape(1, -1)
            normed, inverse = norm_rows(x_ref[...].astype(F32) + attn)
            normed_ref[...] = normed.astype(BF)
            inv_ref[...] = inverse
            out = normed * gain_ref[...].reshape(1, -1) + shift_ref[...].reshape(1, -1)
            first_ref[...] = out.astype(BF)


def block_cols(index, size):
    return pl.ds(pl.multiple_of(index * size, size), size)


def ffn_kernel(
    x_ref, wi_ref, bi_ref, wd_ref, bd_ref, gain_ref, shift_ref,
    hid_ref, slope_ref, normed_ref, inv_ref, out_ref, acc_ref,
):
    step = pl.program_id(0)
    steps = pl.num_programs(0)
    x = x_ref[...]
    own = block_cols(step, wi_ref.shape[1])
    pre = mm(x, wi_ref[...], NN) + bi_ref[own].reshape(1, -1)
    phi = 0.5 * (1.0 + lax.erf(pre * 0.7071067811865476))
    hid = (pre * phi).astype(BF)
    hid_ref[...] = hid
    slope_ref[...] = (phi + pre * jnp.exp(-0.5 * pre * pre) * 0.3989422804014327).astype(BF)
    part_sum = mm(hid, wd_ref[...], NN)

    @pl.when(step == 0)
    def _():
        acc_ref[...] = part_sum

    @pl.when(step > 0)
    def _():
        acc_ref[...] += part_sum

    @pl.when(step == steps - 1)
    def _():
        branch = acc_ref[...] + bd_ref[...].reshape(1, -1)
        normed, inverse = norm_rows(x_ref[...].astype(F32) + branch)
        normed_ref[...] = normed.astype(BF)
        inv_ref[...] = inverse
        out = normed * gain_ref[...].reshape(1, -1) + shift_ref[...].reshape(1, -1)
        out_ref[...] = out.astype(BF)


def norm_back(upstream, normed, inverse, gain):
    scaled = upstream * gain
    inner = (
        scaled
        - jnp.mean(scaled, axis=-1, keepdims=True)
        - normed * jnp.mean(scaled * normed, axis=-1, keepdims=True)
    )
    return inner * inverse


def put_rows(ref, *rows):
    for at, row in enumerate(rows):
        ref[at : at + 1, :] = row


def quarter_at(step, ids_ref):
    rel = jnp.where(step == 0, 3, jnp.where(step == 3, 0, step))
    return jnp.bitwise_xor(ids_ref[0], rel)


def store_quarters(ids_ref, grad, far_ref, near_ref, base, size, cols=slice(None)):
    part = grad.shape[0] // 4
    for q in range(4):
        rel = jnp.bitwise_xor(ids_ref[0], q)
        value = grad[q * part : (q + 1) * part]
        rows = pl.ds(pl.multiple_of(jnp.where(rel < 2, size, 0) + base, 16), part)

        @pl.when((rel & 1) == 1)
        def _():
            far_ref[rows, cols] = value

        @pl.when((rel & 1) == 0)
        def _():
            near_ref[rows, cols] = value


def cot_back_kernel(
    slot_ref, in_ref, normed_ref, inv_ref, gain_ref, pre_ref, branch_ref, vec_ref
):
    chosen = onehot_cols(slot_ref[...], in_ref.shape[0])
    cot = mm(chosen, in_ref[...], NN)
    normed = normed_ref[...].astype(F32)
    g_pre = norm_back(cot, normed, inv_ref[...], gain_ref[...].reshape(1, -1))
    pre_ref[...] = g_pre
    branch = g_pre.astype(BF)
    branch_ref[...] = branch
    put_rows(
        vec_ref,
        jnp.sum(cot * normed, axis=0, keepdims=True),
        jnp.sum(cot, axis=0, keepdims=True),
        jnp.sum(branch.astype(F32), axis=0, keepdims=True),
    )


def down_back_kernel(
    ids_ref, branch_ref, wd_ref, slope_ref, hid_ref, act_ref, bias_ref, far_ref, near_ref
):
    step = pl.program_id(0)
    branch = branch_ref[...]
    own = block_cols(quarter_at(step, ids_ref), wd_ref.shape[0])
    g_act = (mm(branch, wd_ref[...], NT) * slope_ref[...].astype(F32)).astype(BF)
    act_ref[:, own] = g_act
    bias_ref[:, own] = jnp.sum(g_act.astype(F32), axis=0, keepdims=True)
    grad = mm(hid_ref[...], branch, TN).astype(BF)

    @pl.when(step < 2)
    def _():
        far_ref[step] = grad

    @pl.when(step >= 2)
    def _():
        near_ref[step - 2] = grad


def in_back_kernel(ids_ref, x_ref, act_ref, far_ref, near_ref):
    blk = x_ref.shape[1]
    own = block_cols(pl.program_id(0), blk)
    grad = mm(x_ref[...], act_ref[:, own], TN).astype(BF)
    store_quarters(ids_ref, grad, far_ref, near_ref, 0, blk // 4, own)


def first_back_kernel(
    pre2_ref, act_ref, wi_ref, normed_ref, inv_ref, gain_ref, wo_ref, linv0_ref, linv_ref,
    pre1_ref, gattn_ref, gctx_ref, vec_ref,
):
    g_first = pre2_ref[...] + mm(act_ref[...], wi_ref[...], NT)
    g_first = g_first.astype(BF).astype(F32)
    normed = normed_ref[...].astype(F32)
    g_pre = norm_back(g_first, normed, inv_ref[...], gain_ref[...].reshape(1, -1))
    pre1_ref[...] = g_pre
    g_attn = g_pre.astype(BF)
    put_rows(
        vec_ref,
        jnp.sum(g_first * normed, axis=0, keepdims=True),
        jnp.sum(g_first, axis=0, keepdims=True),
        jnp.sum(g_attn.astype(F32), axis=0, keepdims=True),
    )
    g_ctx = mm(g_attn, wo_ref[...], NT)
    cols = linv0_ref.shape[1]
    gctx_ref[:, :cols] = (g_ctx[:, :cols] * linv0_ref[...]).astype(BF)
    gctx_ref[:, cols:] = (g_ctx[:, cols:] * linv_ref[...]).astype(BF)
    gattn_ref[...] = g_attn


def attend_back_kernel(
    head_base, heads, len_ref, swap_ref, q_ref, k_ref, v_ref, soft_ref, gctx_ref, ctx_ref,
    proj_ref, vec_ref, gq_s, gk_s, gv_s,
):
    step = pl.program_id(0)
    rows = q_ref.shape[0]
    half = rows // 2
    head_size = 128 // heads
    scale = head_size ** (-0.5)
    is_long = len_ref[0, 1] == 0
    lane = lax.broadcasted_iota(I32, (1, 128), 1)
    for sub in range(heads):
        swapped = swap_ref[head_base + step * heads + sub] == 1
        cross = jnp.logical_and(is_long, swapped)
        mine = jnp.logical_and(lane >= sub * head_size, lane < (sub + 1) * head_size)
        for b in range(2):
            q_rows = slice(b * half, (b + 1) * half)
            kb = jnp.where(cross, 1 - b, b)
            key_rows = pl.ds(pl.multiple_of(kb * half, half), half)
            soft = soft_ref[sub, b]
            up = gctx_ref[q_rows, :]
            up_one = jnp.where(mine, up, jnp.zeros_like(up))
            inner = jnp.sum(
                up_one.astype(F32) * ctx_ref[q_rows, :].astype(F32), axis=1, keepdims=True
            )
            g_soft = mm(up_one, v_ref[key_rows, :], NT)
            g_scores = (soft.astype(F32) * (g_soft - inner)).astype(BF)
            g_q = mm(g_scores, k_ref[key_rows, :], NN) * scale
            g_k = mm(g_scores, q_ref[q_rows, :], TN) * scale
            g_v = mm(soft, up, TN)
            if sub == 0:
                gq_s[q_rows, :] = g_q
                gk_s[key_rows, :] = g_k
                gv_s[key_rows, :] = g_v
            else:
                gq_s[q_rows, :] = jnp.where(mine, g_q, gq_s[q_rows, :])
                gk_s[key_rows, :] = jnp.where(mine, g_k, gk_s[key_rows, :])
                gv_s[key_rows, :] = jnp.where(mine, g_v, gv_s[key_rows, :])
    cols = proj_ref.shape[1] // 3
    for at, ref in enumerate((gq_s, gk_s, gv_s)):
        low = ref[...].astype(BF)
        out_cols = pl.ds(pl.multiple_of(at * cols + step * 128, 128), 128)
        proj_ref[:, out_cols] = low
        vec_ref[:, out_cols] = jnp.sum(low.astype(F32), axis=0, keepdims=True)


def input_grad_kernel(groups, *refs):
    proj_refs, (wq_ref, wk_ref, wv_ref, pre_ref, out_ref, acc_ref) = refs[:groups], refs[groups:]
    step = pl.program_id(0)
    cols = wq_ref.shape[1]

    @pl.when(step == 0)
    def _():
        acc_ref[...] = pre_ref[...]

    for at, proj_ref in enumerate(proj_refs):

        @pl.when(step == at)
        def _():
            acc_ref[...] += (
                mm(proj_ref[:, :cols], wq_ref[...], NT)
                + mm(proj_ref[:, cols : 2 * cols], wk_ref[...], NT)
                + mm(proj_ref[:, 2 * cols :], wv_ref[...], NT)
            )

    @pl.when(step == groups - 1)
    def _():
        out_ref[...] = acc_ref[...].astype(BF)


def store_vectors(ids_ref, vec_refs, far_ref, near_ref, base, size):
    vec2_ref, bias_ref, vec1_ref, *qkv_refs = vec_refs
    width = vec1_ref.shape[1]
    cols = width // len(qkv_refs)
    part = width // 4
    wide = jnp.concatenate(
        [ref[:, :cols] for ref in qkv_refs] + [ref[:, 2 * cols :] for ref in qkv_refs], axis=1
    )
    extra = size - base
    for q in range(4):
        rel = jnp.bitwise_xor(ids_ref[0], q)
        rows = [bias_ref[:, q * width : (q + 1) * width]]
        rows.append(wide[:, q * (width // 2) : (q + 1) * (width // 2)])
        for ref in (vec2_ref, vec1_ref):
            rows += [ref[at : at + 1, q * part : (q + 1) * part] for at in range(3)]
        rows = [jnp.pad(row, ((0, 0), (0, width - row.shape[1]))) for row in rows]
        rows.append(jnp.zeros((extra - len(rows), width), F32))
        block = jnp.concatenate(rows, axis=0).astype(BF)
        at = pl.ds(pl.multiple_of(jnp.where(rel < 2, size, 0) + base, 16), extra)

        @pl.when((rel & 1) == 1)
        def _():
            far_ref[at, :] = block

        @pl.when((rel & 1) == 0)
        def _():
            near_ref[at, :] = block


def share_grad_kernel(count, extra, ids_ref, *refs):
    pairs = [(refs[2 * at], refs[2 * at + 1]) for at in range(count)]
    *vec_refs, far_ref, near_ref = refs[2 * count :]
    part = pairs[0][0].shape[1] // 4
    size = count * part + extra
    for at, (left_ref, right_ref) in enumerate(pairs):
        grad = mm(left_ref[...], right_ref[...], TN).astype(BF)
        store_quarters(ids_ref, grad, far_ref, near_ref, at * part, size)
    if extra:
        store_vectors(ids_ref, vec_refs, far_ref, near_ref, count * part, size)


def spread_kernel(ids_ref, near_ref, mate_ref, keep_ref, send_ref):
    total = (near_ref[...].astype(F32) + mate_ref[...].astype(F32)).astype(BF)
    rows, half = total.shape[0] // 2, total.shape[1] // 2
    second = (ids_ref[1] & 1) == 1
    core = (ids_ref[0] & 1) == 1
    left, right = total[:, :half], total[:, half:]
    mine = jnp.where(second, right, left)
    other = jnp.where(second, left, right)
    keep_ref[:rows, :] = mine[rows:]
    keep_ref[rows:, :] = jnp.where(core, mine[:rows], other[rows:])
    send_ref[:rows, :] = jnp.where(core, other[rows:], mine[:rows])
    send_ref[rows:, :] = other[:rows]


def split_blocks_kernel(keep_ref, got_ref, mine_ref, other_ref):
    total = (keep_ref[...].astype(F32) + got_ref[...].astype(F32)).astype(BF)
    rows = mine_ref.shape[0]
    mine_ref[...] = total[:rows]
    other_ref[...] = total[rows:]


def split_rows_kernel(ids_ref, keep_ref, got_ref, mine_ref, other_ref):
    half = mine_ref.shape[0]
    bit = (ids_ref[1] >> 1) & 1

    def part(at):
        rows = pl.ds(pl.multiple_of(at * half, half), half)
        return (keep_ref[rows, :].astype(F32) + got_ref[rows, :].astype(F32)).astype(BF)

    mine_ref[...] = part(bit)
    other_ref[...] = part(1 - bit)


def add_kernel(left_ref, right_ref, out_ref):
    out_ref[...] = (left_ref[...].astype(F32) + right_ref[...].astype(F32)).astype(BF)


def join_kernel(ids_ref, own_ref, near_ref, far_own_ref, far_near_ref, out_ref):
    half_rows, half_cols = own_ref.shape
    second = (ids_ref[1] & 1) == 1
    bit = (ids_ref[1] >> 1) & 1
    for rel, (mine, other) in enumerate(((own_ref, far_own_ref), (near_ref, far_near_ref))):
        at = jnp.bitwise_xor(bit, rel)
        rows = pl.ds(pl.multiple_of(at * half_rows, half_rows), half_rows)
        a, b = mine[...].astype(F32), other[...].astype(F32)
        out_ref[rows, :half_cols] = jnp.where(second, b, a)
        out_ref[rows, half_cols:] = jnp.where(second, a, b)


def stack_kernel(ids_ref, own_ref, near_ref, out_ref):
    half = own_ref.shape[0]
    bit = (ids_ref[1] >> 1) & 1
    for rel, ref in enumerate((own_ref, near_ref)):
        at = jnp.bitwise_xor(bit, rel)
        out_ref[pl.ds(pl.multiple_of(at * half, half), half), :] = ref[...]


def join_into(ids_ref, mine_ref, other_ref, out_ref):
    half = mine_ref.shape[1]
    second = (ids_ref[1] & 1) == 1
    a, b = mine_ref[...].astype(F32), other_ref[...].astype(F32)
    out_ref[:, :half] = jnp.where(second, b, a)
    out_ref[:, half:] = jnp.where(second, a, b)


def join_kernel(ids_ref, mine_ref, other_ref, out_ref):
    join_into(ids_ref, mine_ref, other_ref, out_ref)


def attend_join_kernel(groups, ids_ref, *refs):
    a_refs, b_refs = refs[:2], refs[2:4]
    gwq_ref, gwo_ref, qv_ref, hid_ref = refs[4:8]
    vec_refs, (a_all, b_all) = refs[8:14], refs[14:]
    join_into(ids_ref, *a_refs, a_all)
    join_into(ids_ref, *b_refs, b_all)
    part, width = gwo_ref.shape
    cols = width // groups
    gwo_ref[...] = a_all[:part, :]
    places = [(a_all, part)] + [(b_all, part * at) for at in range(groups - 1)]
    for g, (ref, base) in enumerate(places):
        for at in range(3):
            gwq_ref[:, at * width + g * cols : at * width + (g + 1) * cols] = ref[
                base : base + part, at * cols : (at + 1) * cols
            ]
    base = part * (groups - 1)
    hid_ref[...] = b_all[base, :]
    qv_ref[...] = b_all[base + 1, : qv_ref.shape[0]]
    for at, ref in enumerate(vec_refs):
        ref[...] = b_all[base + 2 + at, : ref.shape[0]]


def exchange(values, axis, mask):
    count = lax.axis_size(axis)
    return lax.ppermute(values, axis, [(i, i ^ mask) for i in range(count)])


def exchange_mixed(values, core_along_x):
    seq, batch = lax.axis_size("seq"), lax.axis_size("batch")

    def partner(s, b):
        return (s ^ 2) * batch + b if s & 1 == core_along_x else s * batch + (b ^ 1)

    pairs = [(s * batch + b, partner(s, b)) for s in range(seq) for b in range(batch)]
    return lax.ppermute(values, ("seq", "batch"), pairs)


def simple(chain, body, name, args, out_shape, prefetch=0, vmem=12, scratch=(), cost=COST_SMALL, free=()):
    tensors = args[prefetch:]
    return call(
        chain,
        body,
        name,
        grid=(1,),
        in_specs=[whole_block(a.shape) for a in tensors],
        out_specs=[whole_block(o.shape) for o in out_shape],
        out_shape=out_shape,
        prefetch=prefetch,
        vmem=vmem,
        cost=cost,
        free=free,
        scratch=scratch,
    )(*args)


class Share:
    def __init__(self, chain, ids, name, near, mate, cost=COST_SMALL):
        self.chain, self.ids, self.name = chain, ids, name
        rows, cols = near.shape
        self.shape = (rows // 2, cols)
        self.keep, send = simple(
            chain, spread_kernel, name + "_c", (ids, near, mate), [vmem((rows, cols // 2), BF)] * 2,
            1, cost=cost,
        )
        self.got = exchange_mixed(send, 0)

    def step_xy(self, cost=COST_SMALL):
        rows, cols = self.shape
        self.keep, send = simple(
            self.chain, split_blocks_kernel, self.name + "_x", (self.keep, self.got),
            [vmem((rows, cols // 2), BF)] * 2, cost=cost,
        )
        self.got = exchange_mixed(send, 1)

    def halve(self, kernel, shape, label, mask, cost=COST_SMALL):
        self.keep, other = simple(
            self.chain, kernel, self.name + label, (self.ids, self.keep, self.got),
            [vmem(shape, BF)] * 2, 1, cost=cost,
        )
        self.got = exchange(other, "batch", mask)

    def step_z(self, cost=COST_SMALL):
        rows, cols = self.shape
        self.halve(split_rows_kernel, (rows // 2, cols // 2), "_z", 2, cost)

    def add(self, label, cost=COST_SMALL):
        (self.keep,) = simple(
            self.chain, add_kernel, self.name + label, (self.keep, self.got),
            [vmem(self.keep.shape, BF)], cost=cost,
        )

    def step_far(self, cost=COST_SMALL):
        mask = 4
        while mask <= lax.axis_size("batch") // 2:
            self.add("_a", cost)
            self.got = exchange(self.keep, "batch", mask)
            mask *= 2

    def step_back(self, cost=COST_SMALL):
        self.add("_f", cost)
        self.got = exchange(self.keep, "batch", 2)

    def step_wide(self):
        rows, cols = self.shape
        (self.keep,) = simple(
            self.chain, stack_kernel, self.name + "_g", (self.ids, self.keep, self.got),
            [vmem((rows, cols // 2), BF)], 1,
        )
        self.pieces = (self.keep, exchange(self.keep, "batch", 1))

    def join(self):
        (whole,) = simple(
            self.chain, join_kernel, self.name + "_j", (self.ids, *self.pieces),
            [hbm(self.shape, F32)], 1,
        )
        return whole


def body(
    hidden_in, seq_lengths, head_swap, place, w_qkv, qv_bias, w_out, out_bias, norm1_gain,
    norm1_bias, w_in, in_bias, w_down, down_bias, norm2_gain, norm2_bias, cotangent,
):
    rows, width = hidden_in.shape
    ff = w_in.shape[1]
    ffn_rows = cotangent.shape[0]
    devices = lax.axis_size(("seq", "batch"))
    capacity = (rows + devices - 1) // devices
    slots = devices * capacity
    head_count = head_swap.shape[0]
    head_size = width // head_count
    half = rows // 2
    cols = 256
    groups = width // cols
    heads = cols // head_size
    pair = 128 // head_size
    ids = jnp.stack([lax.axis_index("seq"), lax.axis_index("batch")]).astype(I32)
    chain = Chain()
    chain.keep(pltpu.HBM, hidden_in, w_qkv, w_out, w_in, w_down, cotangent)

    slot_row, out_target = simple(
        chain,
        functools.partial(route_kernel, ffn_rows, capacity),
        "route",
        (place.reshape(1, -1),),
        [sds((1, rows), I32), sds((devices, capacity), I32)],
    )
    in_target = lax.all_to_all(out_target, ("seq", "batch"), split_axis=0, concat_axis=0, tiled=True)

    bf_rows = (rows, width)
    vec_spec = whole_block((width,))
    steps = heads // pair
    some = lambda count, dtype: hbm((rows, count * cols), dtype)
    col = lambda base: pl.BlockSpec((width, cols), lambda g, p, *_: (0, base + g))
    out_col = pl.BlockSpec((rows, cols), lambda g, p, *_: (0, g))
    pair_out = pl.BlockSpec((rows, 128), lambda g, p, *_: (0, g * steps + p))
    soft_spec = pl.BlockSpec((pair, 2, half, half), lambda g, p, *_: (g * steps + p, 0, 0, 0))
    head_outs = [out_col] * 3 + [pair_out, soft_spec, pair_out]
    head_shapes = lambda count: [some(count, BF)] * 4 + [
        hbm((count * heads, 2, half, half), BF), some(count, F32)
    ]
    head_args = (seq_lengths, head_swap, hidden_in, w_qkv, w_qkv, w_qkv, qv_bias)
    head_specs = lambda first: [
        smem(), smem(), whole_block(bf_rows), col(first), col(groups + first),
        col(2 * groups + first), whole_block((2 * width,)),
    ]
    first_heads = call(
        chain,
        functools.partial(attend_kernel, 0, steps, pair),
        "attend_first",
        vmem=32,
        grid=(1, steps),
        in_specs=head_specs(0),
        out_specs=head_outs,
        out_shape=head_shapes(1),
    )(*head_args)
    context0, linv0 = first_heads[3], first_heads[5]
    cot_out, in_row = simple(
        chain,
        functools.partial(gather_kernel, capacity),
        "cot_gather",
        (in_target, cotangent),
        [sds((slots, width), BF), sds((1, slots), I32)],
        free=(1,),
    )
    cot_in = lax.all_to_all(cot_out, ("seq", "batch"), split_axis=0, concat_axis=0, tiled=True)
    *rest_heads, first_low, normed1, inv1, context = call(
        chain,
        functools.partial(attend_kernel, 1, steps, pair),
        "attend_rest",
        vmem=40,
        grid=(groups - 1, steps),
        in_specs=head_specs(1)
        + [
            whole_block((rows, cols)), pl.BlockSpec((cols, width), lambda g, p, *_: (0, 0)),
            pl.BlockSpec((cols, width), lambda g, p, *_: (1 + g, 0)), vec_spec, vec_spec, vec_spec,
        ],
        out_specs=head_outs[:3] + head_outs[4:]
        + [whole_block(bf_rows), whole_block(bf_rows), whole_block((rows, 1)), whole_block(bf_rows)],
        out_shape=head_shapes(groups - 1)[:3] + head_shapes(groups - 1)[4:]
        + [hbm(bf_rows, BF), hbm(bf_rows, BF), hbm((rows, 1), F32), hbm(bf_rows, BF)],
        scratch=[pltpu.VMEM(bf_rows, F32)],
    )(*head_args, context0, w_out, w_out, out_bias, norm1_gain, norm1_bias)
    linv_rest = rest_heads[4]

    blk = ff // 4
    act_shape = (rows, ff)
    act_col = pl.BlockSpec((rows, blk), lambda j, *_: (0, j))
    hid, slope, normed2, inv2, mixed_home = call(
        chain,
        ffn_kernel,
        "ffn",
        vmem=36,
        grid=(4,),
        in_specs=[
            whole_block(bf_rows),
            pl.BlockSpec((width, blk), lambda j, *_: (0, j)),
            whole_block((ff,)),
            pl.BlockSpec((blk, width), lambda j, *_: (j, 0)),
            vec_spec, vec_spec, vec_spec,
        ],
        out_specs=[
            act_col, act_col, whole_block(bf_rows), whole_block((rows, 1)), whole_block(bf_rows),
        ],
        out_shape=[
            hbm(act_shape, BF), hbm(act_shape, BF), hbm(bf_rows, BF), hbm((rows, 1), F32),
            vmem(bf_rows, BF),
        ],
        scratch=[pltpu.VMEM(bf_rows, F32)],
    )(first_low, w_in, in_bias, w_down, down_bias, norm2_gain, norm2_bias)

    (mixed_out,) = simple(
        chain, place_kernel, "mixed_slots", (slot_row, mixed_home), [sds((slots, width), BF)],
        cost=COST,
    )
    mixed_in = lax.all_to_all(mixed_out, ("seq", "batch"), split_axis=0, concat_axis=0, tiled=True)

    g_pre2, g_branch, vec2 = simple(
        chain,
        cot_back_kernel,
        "cot_back",
        (slot_row, cot_in, normed2, inv2, norm2_gain),
        [vmem(bf_rows, F32), vmem(bf_rows, BF), sds((8, width), F32)],
        vmem=24,
        cost=COST,
    )
    part = width // 4
    quarter_rows = pl.BlockSpec((blk, width), lambda j, i: (quarter_at(j, i), 0))
    quarter_cols = pl.BlockSpec((rows, blk), lambda j, i: (0, quarter_at(j, i)))
    down_shape = (2, blk, width)
    g_act, bias_row, gwd_far, gwd_near = call(
        chain,
        down_back_kernel,
        "down_back",
        vmem=18,
        grid=(4,),
        in_specs=[whole_block(bf_rows), quarter_rows, quarter_cols, quarter_cols],
        out_specs=[
            whole_block(act_shape), whole_block((1, ff)), whole_block(down_shape),
            whole_block(down_shape),
        ],
        out_shape=[
            vmem(act_shape, BF), sds((1, ff), F32), vmem(down_shape, BF), vmem(down_shape, BF),
        ],
        prefetch=1,
    )(ids, g_branch, w_down, slope, hid)
    gwd_far, gwd_near = (a.reshape(2 * blk, width) for a in (gwd_far, gwd_near))
    gwd_mate = exchange(gwd_far, "seq", 1)
    in_shape = (2 * part, ff)
    gwi_far, gwi_near = call(
        chain,
        in_back_kernel,
        "in_back",
        vmem=16,
        grid=(4,),
        in_specs=[whole_block(bf_rows), whole_block(act_shape)],
        out_specs=[whole_block(in_shape)] * 2,
        out_shape=[vmem(in_shape, BF)] * 2,
        prefetch=1,
        free=(1,),
    )(ids, first_low, g_act)
    gwi_mate = exchange(gwi_far, "seq", 1)
    down_share = Share(chain, ids, "w_down", gwd_near, gwd_mate, COST)
    in_share = Share(chain, ids, "w_in", gwi_near, gwi_mate)

    g_pre1, g_attn, g_ctx, vec1 = call(
        chain,
        first_back_kernel,
        "first_back",
        vmem=20,
        grid=(1,),
        in_specs=[
            whole_block(bf_rows), whole_block(act_shape),
            whole_block((width, ff)),
            whole_block(bf_rows), whole_block((rows, 1)), vec_spec,
            whole_block((width, width)), whole_block(linv0.shape), whole_block(linv_rest.shape),
        ],
        out_specs=[
            whole_block(bf_rows), whole_block(bf_rows), whole_block(bf_rows),
            whole_block((8, width)),
        ],
        out_shape=[vmem(bf_rows, F32), vmem(bf_rows, BF), vmem(bf_rows, BF), sds((8, width), F32)],
        free=(0, 2, 3, 6, 7, 8),
    )(g_pre2, g_act, w_in, normed1, inv1, norm1_gain, w_out, linv0, linv_rest)

    projs, vecs = [], []
    low = hbm(bf_rows, BF)

    def group_back(g):
        own_col = pl.BlockSpec((rows, 128), lambda p: (0, g * steps + p))
        arrays, base = (first_heads[:3] + first_heads[4:], 0) if g == 0 else (rest_heads, g - 1)
        head_col = pl.BlockSpec((rows, 128), lambda p: (0, base * steps + p))
        proj, vec = call(
            chain,
            functools.partial(attend_back_kernel, g * heads, pair),
            "attend_back",
            vmem=14,
            grid=(steps,),
            in_specs=[
                smem(), smem(), head_col, head_col, head_col,
                pl.BlockSpec((pair, 2, half, half), lambda p: (base * steps + p, 0, 0, 0)),
                own_col, own_col,
            ],
            out_specs=[whole_block((rows, 3 * cols)), whole_block((1, 3 * cols))],
            out_shape=[vmem((rows, 3 * cols), BF), sds((1, 3 * cols), F32)],
            scratch=[pltpu.VMEM((rows, 128), F32)] * 3,
        )(seq_lengths, head_swap, *arrays[:4], g_ctx, context)
        projs.append(proj)
        vecs.append(vec)

    def attention_share(pairs, vec_ins, name, cost=COST):
        extra = 32 if vec_ins else 0
        size = len(pairs) * part + extra
        flat = [a for both in pairs for a in both]
        far_grad, near_grad = simple(
            chain,
            functools.partial(share_grad_kernel, len(pairs), extra),
            name + "_w",
            (ids, *flat, *vec_ins),
            [vmem((2 * size, width), BF)] * 2,
            1,
            vmem=20,
            cost=cost,
            free=(1, 3),
        )
        mate = exchange(far_grad, "seq", 1)
        return lambda: Share(chain, ids, name, near_grad, mate)

    down_share.step_xy()
    group_back(0)
    start_a = attention_share([(context, g_attn), (hidden_in, projs[0])], [], "attn_a")
    down_share.step_z()
    in_share.step_xy()
    group_back(1)
    down_share.step_far()
    in_share.step_z()
    share_a = start_a()
    group_back(2)
    share_a.step_xy(COST_TINY)
    vec_ins = [vec2, bias_row, vec1, *vecs]
    start_b = attention_share(
        [(hidden_in, projs[1]), (hidden_in, projs[2])], vec_ins, "attn_b", COST_TINY
    )
    in_share.step_far()
    down_share.step_back(COST_MID)
    share_b = start_b()
    input_grad = call(
        chain,
        functools.partial(input_grad_kernel, groups),
        "input_grad",
        vmem=18,
        grid=(groups,),
        in_specs=[whole_block((rows, 3 * cols))] * groups
        + [
            pl.BlockSpec((width, cols), lambda g: (0, g)),
            pl.BlockSpec((width, cols), lambda g: (0, groups + g)),
            pl.BlockSpec((width, cols), lambda g: (0, 2 * groups + g)),
            whole_block((rows, width)),
        ],
        out_specs=whole_block((rows, width)),
        out_shape=low,
        scratch=[pltpu.VMEM((rows, width), F32)],
    )(*projs, w_qkv, w_qkv, w_qkv, g_pre1)
    share_a.step_z()
    share_b.step_xy()
    (mixed,) = simple(
        chain, place_kernel, "mixed_place", (in_row, mixed_in), [hbm((ffn_rows, width), BF)]
    )
    down_share.step_wide()
    in_share.step_back()
    share_b.step_z()
    share_a.step_far()
    in_share.step_wide()
    share_b.step_far()
    share_a.step_back()
    g_w_down = down_share.join()
    share_b.step_back()
    share_a.step_wide()
    share_b.step_wide()
    g_w_in = in_share.join()
    one = lambda size: sds((size,), F32)
    g_w_qkv, g_w_out, g_qv, g_in_bias, g_n2g, g_n2b, g_down_bias, g_n1g, g_n1b, g_out_bias = simple(
        chain,
        functools.partial(attend_join_kernel, groups),
        "attn_join",
        (ids, *share_a.pieces, *share_b.pieces),
        [hbm((part, 3 * width), F32), hbm((part, width), F32), one(width // 2), one(width)]
        + [one(part)] * 6,
        1,
        scratch=[pltpu.VMEM(share_a.shape, F32), pltpu.VMEM(share_b.shape, F32)],
    )
    return (
        mixed, input_grad, g_w_qkv, g_qv, g_w_out, g_out_bias, g_n1g, g_n1b, g_w_in, g_in_bias,
        g_w_down, g_down_bias, g_n2g, g_n2b,
    )


def solution(mesh):
    rows_spec = P(("seq", "batch"), None)
    in_specs = (
        rows_spec, rows_spec, P(), P(("seq", "batch")), P(), P(), P(), P(), P(), P(), P(), P(),
        P(), P(), P(), P(), rows_spec,
    )
    out_specs = (
        rows_spec, rows_spec, P("seq", None), P("seq"), P("seq", None), P("seq"), P("seq"),
        P("seq"), P("seq", None), P("seq"), P("seq", None), P("seq"), P("seq"), P("seq"),
    )
    return jax.shard_map(body, mesh=mesh, in_specs=in_specs, out_specs=out_specs, check_vma=False)
```
